32 devices in a mesh: groups: 2 (over y), fsdp: 16 (over z, x, core).
Axes of the slice: x: 2, y: 2, z: 4, core: 2. Of those that a mesh axis runs over, the one named last changes fastest.
Arguments:
- inputs: bfloat16 [2048, 5120], P(('groups', 'fsdp')), parts along dimension 0, may hold values from -6 to 6
- out_grad: bfloat16 [2048, 5120], P(('groups', 'fsdp')), parts along dimension 0, may hold values from -6 to 6
- example_ids: int32 [2048], P(('groups', 'fsdp')), parts along dimension 0, may hold values from 0 to 1, never falling along the last dimension, each value on 1 to 768 neighbouring positions
- gate_weight: bfloat16 [5120, 13824], P(None, 'fsdp'), may hold values from -0.078125 to 0.078125
- up_weight: bfloat16 [5120, 13824], P(None, 'fsdp'), may hold values from -0.078125 to 0.078125
- down_weight: bfloat16 [13824, 5120], P('fsdp'), may hold values from -0.0546875 to 0.0546875
- unit_buckets: int32 [3, 13824], P(None, 'fsdp'), may hold values from 0 to 255
- unit_signs: int32 [3, 13824], P(None, 'fsdp'), may hold values from 0 to 1
- feature_buckets: int32 [5120], replicated, may hold values from 0 to 255
- feature_signs: int32 [5120], replicated, may hold values from 0 to 1
Outputs:
- sketch: float32 [4, 256, 256], P('groups', 'fsdp'), parts along dimension 0
The draws below stay inside these ranges and needn't reach their ends.
There are 2 independent parts, one for each index of `groups`. The reference program is written for one: setup_inputs(seed, part) draws one part's arguments, and reference() takes and returns one part's arrays. A program takes and returns all parts, laid end to end along the dimension named above; an argument that names none is the same for every part. Nothing has to cross between parts.
Inputs may be any that keep to these rules, and one draw needn't show every extreme that they name: `example_ids`: ids never fall along the tokens; every example has 1 to min(1024, 768) tokens in one run.
All inputs are finite; a program needn't handle non-finite values.
Results may differ from the reference program's by a relative error of at most 0.0046.
Values may be sent and summed in bfloat16 or wider, within the bound.
No kernel may reach another device: no remote copies, remote signals or barrier semaphores. Data moves between devices by JAX's collectives and lax.ppermute only.
A program may use at most 128 MiB of HBM per device.

```python
import math
import jax
import jax.numpy as jnp
import numpy as np
from jax import lax

D = 5120
FF = 13824
EX = 2
SEQ = 512
K1 = 256
K2 = 256
TOKENS = 1024
N_FSDP = 16


def touch_ends(drawn, stream_key, smallest, high):
    longest = drawn.shape.index(max(drawn.shape))
    spots = []
    for shift in (0, 1):
        where = [jax.random.randint(jax.random.fold_in(stream_key, axis), (), 0, length) for axis, length in enumerate(drawn.shape)]
        where[longest] = (where[longest] + shift) % drawn.shape[longest]
        spots.append(tuple(where))
    return drawn.at[spots[0]].set(smallest).at[spots[1]].set(high)


def steps_of(own_key, shape, pieces, least, high):
    level, own = 1.0, jax.random.fold_in(own_key, 6)
    for position, blocks in pieces:
        draws = jnp.exp(jax.random.uniform(jax.random.fold_in(own, position), (blocks,), jnp.float32, least / len(pieces), high / len(pieces)))
        level = level * jnp.repeat(draws, shape[position] // blocks).reshape([-1 if axis == position else 1 for axis in range(len(shape))])
    return level


def length_profile(count, total, bound, lean):
    loads = [(1 << 20) // math.isqrt(rank ** lean) + 1 for rank in range(2, count + 1)]
    surplus, holding = total - bound - (count - 1), [1] * (count - 1)
    while surplus > 0:
        free = [i for i in range(count - 1) if holding[i] < bound]
        mass, budget = sum([loads[i] for i in free]), surplus
        for i in free:
            more = min(bound - holding[i], max(1, budget * loads[i] // mass), surplus)
            holding[i] = holding[i] + more
            surplus = surplus - more
    return np.array([bound] + holding)


def uneven_parts(own_key, count, total, limit, skew):
    if count == 2:
        one = jax.random.randint(own_key, (), max(1, total - limit), min(limit, total - 1) + 1)
        return jnp.stack([one, total - one])
    sizes = jnp.asarray(length_profile(count, total, limit, skew), jnp.int32)
    pairs = (count - 1) // 2
    donor, taker = sizes[1:1 + 2 * pairs:2], sizes[2:2 + 2 * pairs:2]
    margin = jnp.minimum(donor - 1, limit - taker)
    shifted = jax.random.randint(jax.random.fold_in(own_key, 1), (pairs,), 0, 1 << 20) % (margin + 1)
    sizes = sizes.at[1:1 + 2 * pairs:2].set(donor - shifted).at[2:2 + 2 * pairs:2].set(taker + shifted)
    return sizes[jax.random.permutation(jax.random.fold_in(own_key, 2), count)]


def bell_draw(key, dims, width, limit, pieces=(), kind=jnp.bfloat16):
    loudness = steps_of(key, dims, pieces, -0.22, 0.18) if pieces else 1.0
    values = jax.random.normal(key, dims, jnp.float32) * width * loudness
    return jnp.minimum(jnp.maximum(values, -limit), limit).astype(kind)


def setup_inputs(seed: int = 0, part: int = 0) -> dict:
    key_list = jax.random.split(jax.random.key(seed), 11)
    own_keys = jax.random.split(jax.random.fold_in(key_list[10], part), 11)
    return {
        "inputs": bell_draw(own_keys[0], (TOKENS, D), 1.0, 6.0, ((0, 16),)),
        "out_grad": bell_draw(own_keys[1], (TOKENS, D), 1.0, 6.0, ((0, 16),)),
        "example_ids": jnp.searchsorted(jnp.cumsum(uneven_parts(own_keys[2], EX, TOKENS, min(TOKENS, SEQ + SEQ // 2), 1)), jnp.arange(TOKENS), side="right").astype(jnp.int32),
        "gate_weight": bell_draw(key_list[3], (D, FF), D ** -0.5, 0.078125, ((1, 16),)),
        "up_weight": bell_draw(key_list[4], (D, FF), D ** -0.5, 0.078125, ((1, 16),)),
        "down_weight": bell_draw(key_list[5], (FF, D), FF ** -0.5, 0.0546875, ((0, 16),)),
        "unit_buckets": touch_ends(jax.random.randint(key_list[6], (3, FF), 0, K1), jax.random.fold_in(key_list[6], 1), 0, K1 - 1).astype(jnp.int32),
        "unit_signs": touch_ends(jax.random.randint(key_list[7], (3, FF), 0, 2), jax.random.fold_in(key_list[7], 1), 0, 1).astype(jnp.int32),
        "feature_buckets": touch_ends(jax.random.randint(key_list[8], (D,), 0, K2), jax.random.fold_in(key_list[8], 1), 0, K2 - 1).astype(jnp.int32),
        "feature_signs": touch_ends(jax.random.randint(key_list[9], (D,), 0, 2), jax.random.fold_in(key_list[9], 1), 0, 1).astype(jnp.int32),
    }


def sign_tables(buckets, sign_bits, buckets_count):
    matches = buckets[..., None] == jnp.arange(buckets_count, dtype=jnp.int32)
    signed = (2 * sign_bits - 1).astype(jnp.float32)[..., None]
    return jnp.where(matches, signed, jnp.zeros_like(signed))


def reference(inputs, out_grad, example_ids, gate_weight, up_weight, down_weight, unit_buckets, unit_signs, feature_buckets, feature_signs):
    block_width = FF // N_FSDP
    feature_table = sign_tables(feature_buckets, feature_signs, K2).astype(jnp.bfloat16)
    feature_in = jnp.dot(inputs, feature_table, preferred_element_type=jnp.float32).astype(jnp.bfloat16)
    feature_out = jnp.dot(out_grad, feature_table, preferred_element_type=jnp.float32).astype(jnp.bfloat16)

    def block_step(running, block_index):
        first_unit = (block_index * block_width).astype(jnp.int32)
        gate_block = lax.dynamic_slice_in_dim(gate_weight, first_unit, block_width, 1)
        up_block = lax.dynamic_slice_in_dim(up_weight, first_unit, block_width, 1)
        down_block = lax.dynamic_slice_in_dim(down_weight, first_unit, block_width, 0)
        bucket_block = lax.dynamic_slice_in_dim(unit_buckets, first_unit, block_width, 1)
        sign_block = lax.dynamic_slice_in_dim(unit_signs, first_unit, block_width, 1)
        unit_tables = sign_tables(bucket_block, sign_block, K1)
        gate_value = jnp.dot(inputs, gate_block, preferred_element_type=jnp.float32)
        up_value = jnp.dot(inputs, up_block, preferred_element_type=jnp.float32)
        sigmoid_gate = jax.nn.sigmoid(gate_value)
        activated = gate_value * sigmoid_gate
        hidden = (activated * up_value).astype(jnp.bfloat16)
        hidden_grad = lax.dot_general(out_grad, down_block, (((1,), (1,)), ((), ())), preferred_element_type=jnp.float32)
        gate_grad = hidden_grad * up_value * sigmoid_gate * (1.0 + gate_value * (1.0 - sigmoid_gate))
        up_grad = hidden_grad * activated
        down_part = jnp.dot(hidden, unit_tables[2].astype(jnp.bfloat16), preferred_element_type=jnp.float32).astype(jnp.bfloat16)
        input_part = (jnp.dot(gate_grad, unit_tables[0], precision=lax.Precision.HIGHEST)
                      + jnp.dot(up_grad, unit_tables[1], precision=lax.Precision.HIGHEST)).astype(jnp.bfloat16)
        return (running[0] + down_part.astype(jnp.float32), running[1] + input_part.astype(jnp.float32)), None

    zeros = jnp.zeros((inputs.shape[0], K1), jnp.float32)
    (down_sum, input_sum), _ = lax.scan(block_step, (zeros, zeros), jnp.arange(N_FSDP, dtype=jnp.int32))
    onehot = (example_ids[:, None] == jnp.arange(EX, dtype=jnp.int32)).astype(jnp.float32)
    factor = (3.0 * SEQ * FF * D / (K1 * K2)) ** -0.5
    sketch = jnp.einsum("te,tk,tl->ekl", onehot, down_sum, feature_out.astype(jnp.float32), precision=lax.Precision.HIGHEST)
    sketch = sketch + jnp.einsum("te,tk,tl->ekl", onehot, input_sum, feature_in.astype(jnp.float32), precision=lax.Precision.HIGHEST)
    return factor * sketch
```

```python
import jax
import jax.numpy as jnp
from jax import lax
from jax.sharding import PartitionSpec as P

D = 5120
FF = 13824
EX = 2
SEQ = 512
K1 = 256
K2 = 256
CORES = 2
OUTER = 4


def sign_tables(buckets, sign_bits, buckets_count):
    matches = buckets[..., None] == jnp.arange(buckets_count, dtype=jnp.int32)
    signed = (2 * sign_bits - 1).astype(jnp.bfloat16)[..., None]
    return jnp.where(matches, signed, jnp.zeros_like(signed))


class Layout:
    def __init__(self, count):
        self.outer = OUTER if count % (OUTER * CORES) == 0 else 1
        self.inner = count // (self.outer * CORES)
        self.count = count

    def index(self, outer, inner, core):
        return ((outer % self.outer) * self.inner + inner % self.inner) * CORES + core

    def pairs(self, step):
        places = [
            (o, i, c)
            for o in range(self.outer)
            for i in range(self.inner)
            for c in range(CORES)
        ]
        return [(self.index(o, i, c), self.index(*step(o, i, c))) for o, i, c in places]

    def outer_ring(self):
        return self.pairs(lambda o, i, c: (o + 1 - 2 * c, i, c))

    def inner_ring(self):
        return self.pairs(lambda o, i, c: (o, i + 1 - 2 * c, c))

    def outer_shift(self, by):
        return self.pairs(lambda o, i, c: (o + by, i, c))

    def inner_shift(self, by):
        return self.pairs(lambda o, i, c: (o, i + by, c))

    def core_swap(self):
        return self.pairs(lambda o, i, c: (o, i, 1 - c))


def on_device(
    layout,
    inputs,
    out_grad,
    example_ids,
    gate_weight,
    up_weight,
    down_weight,
    unit_buckets,
    unit_signs,
    feature_buckets,
    feature_signs,
):
    def move(value, pairs):
        return lax.ppermute(value, "fsdp", pairs)

    me = lax.axis_index("fsdp")
    core = me % CORES
    inner = (me // CORES) % layout.inner
    outer = me // (CORES * layout.inner)
    rows = inputs.shape[0]

    unit_tables = sign_tables(unit_buckets, unit_signs, K1)
    feature_table = sign_tables(feature_buckets, feature_signs, K2)

    held = {(0, 0): (inputs, out_grad)}
    for o in range(layout.outer):
        if o:
            held[o, 0] = tuple(move(v, layout.outer_ring()) for v in held[o - 1, 0])
        for i in range(1, layout.inner):
            held[o, i] = tuple(move(v, layout.inner_ring()) for v in held[o, i - 1])
    swapped = {
        at: tuple(move(v, layout.core_swap()) for v in pair) for at, pair in held.items()
    }

    all_ids = lax.all_gather(example_ids, "fsdp", axis=0, tiled=True).reshape(-1, rows)

    def owner(at, its_core):
        sign = 1 - 2 * its_core
        return layout.index(outer - at[0] * sign, inner - at[1] * sign, its_core)

    def chunk(places):
        rows_in = jnp.concatenate([t[at][0] for at in places for t in (held, swapped)], axis=0)
        rows_out = jnp.concatenate([t[at][1] for at in places for t in (held, swapped)], axis=0)
        owners = jnp.stack([owner(at, c) for at in places for c in (core, 1 - core)])
        ids = jnp.take(all_ids, owners, axis=0).reshape(-1)
        gate = jnp.dot(rows_in, gate_weight, preferred_element_type=jnp.float32)
        up = jnp.dot(rows_in, up_weight, preferred_element_type=jnp.float32)
        sigmoid = jax.nn.sigmoid(gate)
        activated = gate * sigmoid
        hidden = (activated * up).astype(jnp.bfloat16)
        hidden_grad = lax.dot_general(
            rows_out, down_weight, (((1,), (1,)), ((), ())), preferred_element_type=jnp.float32
        )
        gate_grad = hidden_grad * up * sigmoid * (1.0 + gate * (1.0 - sigmoid))
        up_grad = hidden_grad * activated

        def project(value, table):
            return jnp.dot(
                value.astype(jnp.bfloat16), table, preferred_element_type=jnp.float32
            )

        down_part = project(hidden, unit_tables[2]).astype(jnp.bfloat16)
        input_part = (
            project(gate_grad, unit_tables[0]) + project(up_grad, unit_tables[1])
        ).astype(jnp.bfloat16)
        feature_in = project(rows_in, feature_table).astype(jnp.bfloat16)
        feature_out = project(rows_out, feature_table).astype(jnp.bfloat16)
        onehot = ids[:, None] == jnp.arange(EX, dtype=jnp.int32)
        left = jnp.concatenate([down_part, input_part], axis=0)
        onehot = jnp.concatenate([onehot, onehot], axis=0)
        left = jnp.where(onehot[:, :, None], left[:, None, :], jnp.zeros_like(left)[:, None, :])
        right = jnp.concatenate([feature_out, feature_in], axis=0)
        return lax.dot_general(
            left.reshape(-1, EX * K1),
            right,
            (((0,), (0,)), ((), ())),
            preferred_element_type=jnp.float32,
        )

    order = sorted(held, key=lambda at: (at[0] + at[1], at[1]))
    groups = {}
    for at in order:
        groups.setdefault(at[0] + at[1], []).append(at)
    total = sum(chunk(groups[when]) for when in sorted(groups))

    part = total.reshape(EX, layout.outer, layout.inner, CORES, -1, K2)
    take = lambda v, at, axis: lax.dynamic_index_in_dim(v, at, axis, keepdims=False)
    part = take(part, core, 3) + move(take(part, 1 - core, 3), layout.core_swap())
    part = take(part, inner, 2) + sum(
        move(take(part, (inner + by) % layout.inner, 2), layout.inner_shift(by))
        for by in range(1, layout.inner)
    )
    part = take(part, outer, 1) + sum(
        move(take(part, (outer + by) % layout.outer, 1), layout.outer_shift(by))
        for by in range(1, layout.outer)
    )
    factor = (3.0 * SEQ * FF * D / (K1 * K2)) ** (-0.5)
    return factor * part


def solution(mesh):
    layout = Layout(mesh.shape["fsdp"])
    in_specs = (
        P(("groups", "fsdp"), None),
        P(("groups", "fsdp"), None),
        P(("groups", "fsdp")),
        P(None, "fsdp"),
        P(None, "fsdp"),
        P("fsdp", None),
        P(None, "fsdp"),
        P(None, "fsdp"),
        P(),
        P(),
    )
    out_specs = P("groups", "fsdp", None)
    return jax.shard_map(
        lambda *args: on_device(layout, *args),
        mesh=mesh,
        in_specs=in_specs,
        out_specs=out_specs,
        check_vma=False,
    )
```

```python
import functools

import jax
import jax.numpy as jnp
from jax import lax
from jax.experimental import pallas as pl
from jax.experimental.pallas import tpu as pltpu
from jax.sharding import PartitionSpec as P

D = 5120
FF = 13824
EX = 2
SEQ = 512
K1 = 256
K2 = 256
CORES = 2
OUTER = 4
DEPTH = 1024
VMEM_LIMIT = 32 << 20


def sign_tables(buckets, sign_bits, buckets_count):
    matches = buckets[..., None] == jnp.arange(buckets_count, dtype=jnp.int32)
    signed = (2 * sign_bits - 1).astype(jnp.bfloat16)[..., None]
    return jnp.where(matches, signed, jnp.zeros_like(signed))


class Layout:
    def __init__(self, count):
        self.outer = OUTER if count % (OUTER * CORES) == 0 else 1
        self.inner = count // (self.outer * CORES)
        self.count = count

    def index(self, outer, inner, core):
        return ((outer % self.outer) * self.inner + inner % self.inner) * CORES + core

    def pairs(self, step):
        places = [
            (o, i, c)
            for o in range(self.outer)
            for i in range(self.inner)
            for c in range(CORES)
        ]
        return [(self.index(o, i, c), self.index(*step(o, i, c))) for o, i, c in places]

    def outer_ring(self):
        return self.pairs(lambda o, i, c: (o + 1 - 2 * c, i, c))

    def inner_ring(self):
        return self.pairs(lambda o, i, c: (o, i + 1 - 2 * c, c))

    def outer_shift(self, by):
        return self.pairs(lambda o, i, c: (o + by, i, c))

    def inner_shift(self, by):
        return self.pairs(lambda o, i, c: (o, i + by, c))

    def core_swap(self):
        return self.pairs(lambda o, i, c: (o, i, 1 - c))


def rows_of(refs):
    return jnp.concatenate([ref[...] for ref in refs], axis=0) if len(refs) > 1 else refs[0][...]


def dot(left, right):
    return jnp.dot(left, right, preferred_element_type=jnp.float32)


def forward_kernel(pieces, *refs):
    rows = rows_of(refs[:pieces])
    gate_w, up_w, feature_w, down_table = refs[pieces : pieces + 4]
    to_gate, to_up, down_part, feature_in = refs[pieces + 4 : pieces + 8]
    gate_acc, up_acc, feature_acc = refs[pieces + 8 :]
    step = pl.program_id(0)
    sums = (
        (gate_acc, dot(rows, gate_w[...])),
        (up_acc, dot(rows, up_w[...])),
        (feature_acc, dot(rows, feature_w[...])),
    )

    @pl.when(step == 0)
    def _():
        for acc, value in sums:
            acc[...] = value

    @pl.when(step > 0)
    def _():
        for acc, value in sums:
            acc[...] += value

    @pl.when(step == pl.num_programs(0) - 1)
    def _():
        gate, up = gate_acc[...], up_acc[...]
        sigmoid = jax.nn.sigmoid(gate)
        activated = gate * sigmoid
        to_gate[...] = up * sigmoid * (1.0 + gate * (1.0 - sigmoid))
        to_up[...] = activated
        hidden = (activated * up).astype(jnp.bfloat16)
        down_part[...] = dot(hidden, down_table[...]).astype(jnp.bfloat16)
        feature_in[...] = feature_acc[...].astype(jnp.bfloat16)


def backward_kernel(pieces, bounds, owners, *refs):
    piece_refs = refs[:pieces]
    down_w, feature_w, to_gate, to_up, gate_table, up_table = refs[pieces : pieces + 6]
    down_part, feature_in, before = refs[pieces + 6 : pieces + 9]
    total = refs[pieces + 9]
    hidden_acc, feature_acc = refs[pieces + 10 :]
    rows = rows_of(piece_refs)
    step = pl.program_id(0)
    sums = (
        (
            hidden_acc,
            lax.dot_general(
                rows, down_w[...], (((1,), (1,)), ((), ())), preferred_element_type=jnp.float32
            ),
        ),
        (feature_acc, dot(rows, feature_w[...])),
    )

    @pl.when(step == 0)
    def _():
        for acc, value in sums:
            acc[...] = value

    @pl.when(step > 0)
    def _():
        for acc, value in sums:
            acc[...] += value

    @pl.when(step == pl.num_programs(0) - 1)
    def _():
        hidden_grad = hidden_acc[...]
        gate_grad = (hidden_grad * to_gate[...]).astype(jnp.bfloat16)
        up_grad = (hidden_grad * to_up[...]).astype(jnp.bfloat16)
        input_part = (dot(gate_grad, gate_table[...]) + dot(up_grad, up_table[...])).astype(
            jnp.bfloat16
        )
        right = jnp.concatenate([feature_acc[...].astype(jnp.bfloat16), feature_in[...]], axis=0)
        left = jnp.concatenate([down_part[...], input_part], axis=0)
        count = owners.shape[0]
        own = left.shape[0] // 2 // count
        places = jnp.concatenate(
            [owners[i] * own + lax.broadcasted_iota(jnp.int32, (own, K1), 0) for i in range(count)],
            axis=0,
        )
        places = jnp.concatenate([places, places], axis=0)
        for e in range(EX):
            inside = (places >= bounds[e]) & (places < bounds[e + 1])
            own_left = jnp.where(inside, left.astype(jnp.float32), 0.0).astype(jnp.bfloat16)
            part = lax.dot_general(
                own_left, right, (((0,), (0,)), ((), ())), preferred_element_type=jnp.float32
            )
            here = slice(e * K1, (e + 1) * K1)
            total[here, :] = before[here, :] + part


def whole(shape):
    return pl.BlockSpec(shape, lambda k: (0,) * len(shape))


def forward(pieces, gate_weight, up_weight, feature_table, down_table):
    own, model = pieces[0].shape
    rows = own * len(pieces)
    units = gate_weight.shape[1]
    depth = min(DEPTH, model)
    piece = pl.BlockSpec((own, depth), lambda k: (0, k))
    deep = lambda width: pl.BlockSpec((depth, width), lambda k: (k, 0))
    f32, bf16 = jnp.float32, jnp.bfloat16
    return pl.pallas_call(
        functools.partial(forward_kernel, len(pieces)),
        grid=(model // depth,),
        in_specs=[piece] * len(pieces)
        + [deep(units), deep(units), deep(K2), whole((units, K1))],
        out_specs=[whole((rows, units)), whole((rows, units)), whole((rows, K1)), whole((rows, K2))],
        out_shape=[
            jax.ShapeDtypeStruct((rows, units), f32),
            jax.ShapeDtypeStruct((rows, units), f32),
            jax.ShapeDtypeStruct((rows, K1), bf16),
            jax.ShapeDtypeStruct((rows, K2), bf16),
        ],
        scratch_shapes=[
            pltpu.VMEM((rows, units), f32),
            pltpu.VMEM((rows, units), f32),
            pltpu.VMEM((rows, K2), f32),
        ],
        compiler_params=pltpu.CompilerParams(vmem_limit_bytes=VMEM_LIMIT),
        cost_estimate=pl.CostEstimate(
            flops=2 * rows * model * (2 * units + K2),
            bytes_accessed=2 * model * (2 * units + K2 + rows),
            transcendentals=rows * units,
        ),
        name="forward",
    )(*pieces, gate_weight, up_weight, feature_table, down_table)


def backward(
    bounds, owners, pieces, down_weight, feature_table, saved, gate_table, up_table, before
):
    to_gate, to_up, down_part, feature_in = saved
    own, model = pieces[0].shape
    rows = own * len(pieces)
    units = down_weight.shape[0]
    depth = min(DEPTH, model)
    piece = pl.BlockSpec((own, depth), lambda k: (0, k))
    f32 = jnp.float32
    smem = pl.BlockSpec(memory_space=pltpu.SMEM)
    return pl.pallas_call(
        functools.partial(backward_kernel, len(pieces)),
        grid=(model // depth,),
        in_specs=[smem, smem]
        + [piece] * len(pieces)
        + [
            pl.BlockSpec((units, depth), lambda k: (0, k)),
            pl.BlockSpec((depth, K2), lambda k: (k, 0)),
            whole((rows, units)),
            whole((rows, units)),
            whole((units, K1)),
            whole((units, K1)),
            whole((rows, K1)),
            whole((rows, K2)),
            whole((EX * K1, K2)),
        ],
        out_specs=whole((EX * K1, K2)),
        out_shape=jax.ShapeDtypeStruct((EX * K1, K2), f32),
        scratch_shapes=[pltpu.VMEM((rows, units), f32), pltpu.VMEM((rows, K2), f32)],
        compiler_params=pltpu.CompilerParams(vmem_limit_bytes=VMEM_LIMIT),
        cost_estimate=pl.CostEstimate(
            flops=2 * rows * model * (units + K2),
            bytes_accessed=2 * model * (units + K2 + rows),
            transcendentals=0,
        ),
        name="backward",
    )(
        bounds,
        owners,
        *pieces,
        down_weight,
        feature_table,
        to_gate,
        to_up,
        gate_table,
        up_table,
        down_part,
        feature_in,
        before,
    )


def on_device(
    layout,
    inputs,
    out_grad,
    example_ids,
    gate_weight,
    up_weight,
    down_weight,
    unit_buckets,
    unit_signs,
    feature_buckets,
    feature_signs,
):
    def move(value, pairs):
        return lax.ppermute(value, "fsdp", pairs)

    me = lax.axis_index("fsdp")
    core = me % CORES
    inner = (me // CORES) % layout.inner
    outer = me // (CORES * layout.inner)
    rows = inputs.shape[0]

    unit_tables = sign_tables(unit_buckets, unit_signs, K1)
    feature_table = sign_tables(feature_buckets, feature_signs, K2)

    bounds = jnp.sum(
        (example_ids[None, :] < jnp.arange(EX + 1, dtype=jnp.int32)[:, None]).astype(jnp.int32),
        axis=1,
    )
    if layout.inner == 2:
        bounds = bounds + move(bounds, layout.core_swap())
        bounds = bounds + move(bounds, layout.inner_shift(1))
        bounds = bounds + sum(move(bounds, layout.outer_shift(by)) for by in range(1, layout.outer))
    else:
        bounds = lax.psum(bounds, "fsdp")

    def owner(at, its_core):
        sign = 1 - 2 * its_core
        return layout.index(outer - at[0] * sign, inner - at[1] * sign, its_core)

    if layout.inner == 2:
        held = {(0, 0): (inputs, out_grad)}
        for o in range(layout.outer):
            if o:
                held[o, 0] = tuple(move(v, layout.outer_ring()) for v in held[o - 1, 0])
            held[o, 1] = tuple(move(v, layout.inner_ring()) for v in held[o, 0])
        swapped = {
            at: tuple(move(v, layout.core_swap()) for v in pair) for at, pair in held.items()
        }
        groups = {}
        for at in sorted(held, key=lambda at: (sum(at), at[1])):
            groups.setdefault(sum(at), []).append(at)
        chunks = []
        for when in sorted(groups):
            pairs = [table[at] for at in groups[when] for table in (held, swapped)]
            owners = [owner(at, c) for at in groups[when] for c in (core, 1 - core)]
            chunks.append(([p[0] for p in pairs], [p[1] for p in pairs], jnp.stack(owners)))
    else:
        gathered = [lax.all_gather(v, "fsdp", axis=0, tiled=True) for v in (inputs, out_grad)]
        chunks = [([gathered[0]], [gathered[1]], jnp.zeros((1,), jnp.int32))]

    total = jnp.zeros((EX * K1, K2), jnp.float32)
    for pieces_in, pieces_out, owners in chunks:
        saved = forward(pieces_in, gate_weight, up_weight, feature_table, unit_tables[2])
        total = backward(
            bounds,
            owners.astype(jnp.int32),
            pieces_out,
            down_weight,
            feature_table,
            saved,
            unit_tables[0],
            unit_tables[1],
            total,
        )

    part = total.reshape(EX, layout.outer, layout.inner, CORES, -1, K2)
    take = lambda v, at, axis: lax.dynamic_index_in_dim(v, at, axis, keepdims=False)
    part = take(part, core, 3) + move(take(part, 1 - core, 3), layout.core_swap())
    part = take(part, inner, 2) + sum(
        move(take(part, (inner + by) % layout.inner, 2), layout.inner_shift(by))
        for by in range(1, layout.inner)
    )
    part = take(part, outer, 1) + sum(
        move(take(part, (outer + by) % layout.outer, 1), layout.outer_shift(by))
        for by in range(1, layout.outer)
    )
    factor = (3.0 * SEQ * FF * D / (K1 * K2)) ** (-0.5)
    return factor * part


def solution(mesh):
    layout = Layout(mesh.shape["fsdp"])
    in_specs = (
        P(("groups", "fsdp"), None),
        P(("groups", "fsdp"), None),
        P(("groups", "fsdp")),
        P(None, "fsdp"),
        P(None, "fsdp"),
        P("fsdp", None),
        P(None, "fsdp"),
        P(None, "fsdp"),
        P(),
        P(),
    )
    out_specs = P("groups", "fsdp", None)
    return jax.shard_map(
        lambda *args: on_device(layout, *args),
        mesh=mesh,
        in_specs=in_specs,
        out_specs=out_specs,
        check_vma=False,
    )
```

```python
import functools

import jax
import jax.numpy as jnp
from jax import lax
from jax.experimental import pallas as pl
from jax.experimental.pallas import tpu as pltpu
from jax.sharding import PartitionSpec as P

D = 5120
FF = 13824
EX = 2
SEQ = 512
K1 = 256
K2 = 256
CORES = 2
OUTER = 4
DEPTH = 1024
LANES = 128
VMEM_LIMIT = 56 << 20


def sign_tables(buckets, sign_bits, buckets_count):
    matches = buckets[..., None, :] == jnp.arange(buckets_count, dtype=jnp.int32)[:, None]
    signed = (2 * sign_bits - 1).astype(jnp.bfloat16)[..., None, :]
    return jnp.where(matches, signed, jnp.zeros_like(signed))


class Layout:
    def __init__(self, count):
        self.outer = OUTER if count % (OUTER * CORES) == 0 else 1
        self.inner = count // (self.outer * CORES)
        self.count = count

    def index(self, outer, inner, core):
        return ((outer % self.outer) * self.inner + inner % self.inner) * CORES + core

    def pairs(self, step):
        places = [
            (o, i, c)
            for o in range(self.outer)
            for i in range(self.inner)
            for c in range(CORES)
        ]
        return [(self.index(o, i, c), self.index(*step(o, i, c))) for o, i, c in places]

    def outer_ring(self):
        return self.pairs(lambda o, i, c: (o + 1 - 2 * c, i, c))

    def inner_ring(self):
        return self.pairs(lambda o, i, c: (o, i + 1 - 2 * c, c))

    def outer_shift(self, by):
        return self.pairs(lambda o, i, c: (o + by, i, c))

    def inner_shift(self, by):
        return self.pairs(lambda o, i, c: (o, i + by, c))

    def core_swap(self):
        return self.pairs(lambda o, i, c: (o, i, 1 - c))


def rows_of(refs):
    return jnp.concatenate([ref[...] for ref in refs], axis=0) if len(refs) > 1 else refs[0][...]


def dot(left, right):
    return jnp.dot(left, right, preferred_element_type=jnp.float32)


def dot_rows(left, right):
    return lax.dot_general(
        left, right, (((1,), (1,)), ((), ())), preferred_element_type=jnp.float32
    )


def chunk_kernel(pieces, *refs):
    ins, outs, ids = (refs[i * pieces : (i + 1) * pieces] for i in range(3))
    gate_w, up_w, down_w, feature_w, tables, before, total = refs[3 * pieces : 3 * pieces + 7]
    gate_acc, up_acc, hidden_acc, in_acc, out_acc = accs = refs[3 * pieces + 7 :]
    step = pl.program_id(0)

    @pl.when(step == 0)
    def _():
        for acc in accs:
            acc[...] = jnp.zeros_like(acc)

    rows_in, rows_out = rows_of(ins), rows_of(outs)
    gate_acc[...] += dot_rows(gate_w[...], rows_in)
    up_acc[...] += dot_rows(up_w[...], rows_in)
    in_acc[...] += dot_rows(rows_in, feature_w[...])
    hidden_acc[...] += dot_rows(down_w[...], rows_out)
    out_acc[...] += dot_rows(rows_out, feature_w[...])

    @pl.when(step == pl.num_programs(0) - 1)
    def _():
        gate, up, hidden_grad = gate_acc[...], up_acc[...], hidden_acc[...]
        sigmoid = jax.nn.sigmoid(gate)
        activated = gate * sigmoid
        hidden = activated * up
        gate_grad = hidden_grad * up * sigmoid * (1.0 + gate * (1.0 - sigmoid))
        up_grad = hidden_grad * activated
        bf16 = jnp.bfloat16
        down_part = dot(tables[2], hidden.astype(bf16)).astype(bf16)
        input_part = (
            dot(tables[0], gate_grad.astype(bf16)) + dot(tables[1], up_grad.astype(bf16))
        ).astype(bf16)
        example = rows_of(ids).astype(jnp.float32)
        example = jnp.concatenate([example] * (K2 // LANES), axis=1)

        def by_example(features):
            rounded = features.astype(bf16).astype(jnp.float32)
            return jnp.concatenate(
                [jnp.where(example == e, rounded, 0.0) for e in range(EX)], axis=1
            ).astype(bf16)

        total[...] = (
            before[...]
            + dot(down_part, by_example(out_acc[...]))
            + dot(input_part, by_example(in_acc[...]))
        )


def chunk(pieces, gate_rows, up_rows, down_rows, feature_table, tables, before):
    own = pieces[0].shape[0]
    units, model = gate_rows.shape
    rows = own * len(pieces)
    depth = min(DEPTH, model)
    steps = model // depth
    whole = lambda shape: pl.BlockSpec(shape, lambda k: (0,) * len(shape))
    weight = pl.BlockSpec((units, depth), lambda k: (0, k))
    f32 = jnp.float32
    return pl.pallas_call(
        functools.partial(chunk_kernel, len(pieces)),
        grid=(steps,),
        in_specs=[pl.BlockSpec((own, depth), lambda k: (0, k))] * len(pieces)
        + [pl.BlockSpec((own, depth), lambda k: (0, steps + k))] * len(pieces)
        + [pl.BlockSpec((own, LANES), lambda k: (0, 2 * model // LANES))] * len(pieces)
        + [weight, weight, weight, pl.BlockSpec((K2, depth), lambda k: (0, k))]
        + [whole(tables.shape), whole(before.shape)],
        out_specs=whole(before.shape),
        out_shape=jax.ShapeDtypeStruct(before.shape, f32),
        scratch_shapes=[pltpu.VMEM((units, rows), f32)] * 3 + [pltpu.VMEM((rows, K2), f32)] * 2,
        compiler_params=pltpu.CompilerParams(vmem_limit_bytes=VMEM_LIMIT),
        cost_estimate=pl.CostEstimate(
            flops=2 * rows * model * (3 * units + 2 * K2),
            bytes_accessed=2 * model * (3 * units + K2 + 2 * rows),
            transcendentals=rows * units,
        ),
        name="chunk",
    )(*pieces, *pieces, *pieces, gate_rows, up_rows, down_rows, feature_table, tables, before)


def on_device(
    layout,
    inputs,
    out_grad,
    example_ids,
    gate_weight,
    up_weight,
    down_weight,
    unit_buckets,
    unit_signs,
    feature_buckets,
    feature_signs,
):
    def move(value, pairs):
        return lax.ppermute(value, "fsdp", pairs)

    me = lax.axis_index("fsdp")
    core = me % CORES
    inner = (me // CORES) % layout.inner
    outer = me // (CORES * layout.inner)
    rows = inputs.shape[0]

    unit_tables = sign_tables(unit_buckets, unit_signs, K1)
    feature_table = sign_tables(feature_buckets, feature_signs, K2)

    example = jnp.broadcast_to(example_ids[:, None], (rows, LANES)).astype(jnp.bfloat16)
    own = jnp.concatenate([inputs, out_grad, example], axis=1)

    if layout.inner == 2:
        held = {(0, 0): own}
        for o in range(layout.outer):
            if o:
                held[o, 0] = move(held[o - 1, 0], layout.outer_ring())
            held[o, 1] = move(held[o, 0], layout.inner_ring())
        swapped = {at: move(piece, layout.core_swap()) for at, piece in held.items()}
        chunks = {}
        for at in sorted(held, key=lambda at: (sum(at), at[1])):
            chunks.setdefault(sum(at), []).extend([held[at], swapped[at]])
        chunks = [chunks[when] for when in sorted(chunks)]
    else:
        chunks = [[lax.all_gather(own, "fsdp", axis=0, tiled=True)]]

    total = jnp.zeros((K1, EX * K2), jnp.float32)
    for pieces in chunks:
        total = chunk(
            pieces,
            gate_weight.T,
            up_weight.T,
            down_weight,
            feature_table,
            unit_tables,
            total,
        )

    part = total.reshape(layout.outer, layout.inner, CORES, -1, EX * K2)
    take = lambda v, at, axis: lax.dynamic_index_in_dim(v, at, axis, keepdims=False)
    part = take(part, core, 2) + move(take(part, 1 - core, 2), layout.core_swap())
    part = take(part, inner, 1) + sum(
        move(take(part, (inner + by) % layout.inner, 1), layout.inner_shift(by))
        for by in range(1, layout.inner)
    )
    part = take(part, outer, 0) + sum(
        move(take(part, (outer + by) % layout.outer, 0), layout.outer_shift(by))
        for by in range(1, layout.outer)
    )
    factor = (3.0 * SEQ * FF * D / (K1 * K2)) ** (-0.5)
    return (factor * part).reshape(-1, EX, K2).transpose(1, 0, 2)


def solution(mesh):
    layout = Layout(mesh.shape["fsdp"])
    in_specs = (
        P(("groups", "fsdp"), None),
        P(("groups", "fsdp"), None),
        P(("groups", "fsdp")),
        P(None, "fsdp"),
        P(None, "fsdp"),
        P("fsdp", None),
        P(None, "fsdp"),
        P(None, "fsdp"),
        P(),
        P(),
    )
    out_specs = P("groups", "fsdp", None)
    return jax.shard_map(
        lambda *args: on_device(layout, *args),
        mesh=mesh,
        in_specs=in_specs,
        out_specs=out_specs,
        check_vma=False,
    )
```

```python
import functools

import jax
import jax.numpy as jnp
from jax import lax
from jax.experimental import pallas as pl
from jax.experimental.pallas import tpu as pltpu
from jax.sharding import PartitionSpec as P

D = 5120
FF = 13824
EX = 2
SEQ = 512
K1 = 256
K2 = 256
CORES = 2
OUTER = 4
DEPTH = 1024
LANES = 128
VMEM_LIMIT = 56 << 20


def sign_tables(buckets, sign_bits, buckets_count):
    matches = buckets[..., None, :] == jnp.arange(buckets_count, dtype=jnp.int32)[:, None]
    signed = (2 * sign_bits - 1).astype(jnp.bfloat16)[..., None, :]
    return jnp.where(matches, signed, jnp.zeros_like(signed))


class Layout:
    def __init__(self, count):
        self.outer = OUTER if count % (OUTER * CORES) == 0 else 1
        self.inner = count // (self.outer * CORES)
        self.count = count

    def index(self, outer, inner, core):
        return ((outer % self.outer) * self.inner + inner % self.inner) * CORES + core

    def pairs(self, step):
        places = [
            (o, i, c)
            for o in range(self.outer)
            for i in range(self.inner)
            for c in range(CORES)
        ]
        return [(self.index(o, i, c), self.index(*step(o, i, c))) for o, i, c in places]

    def outer_ring(self):
        return self.pairs(lambda o, i, c: (o + 1 - 2 * c, i, c))

    def inner_ring(self):
        return self.pairs(lambda o, i, c: (o, i + 1 - 2 * c, c))

    def outer_shift(self, by):
        return self.pairs(lambda o, i, c: (o + by, i, c))

    def inner_shift(self, by):
        return self.pairs(lambda o, i, c: (o, i + by, c))

    def core_swap(self):
        return self.pairs(lambda o, i, c: (o, i, 1 - c))


def rows_of(refs):
    return jnp.concatenate([ref[...] for ref in refs], axis=0) if len(refs) > 1 else refs[0][...]


def dot(left, right):
    return jnp.dot(left, right, preferred_element_type=jnp.float32)


def dot_rows(left, right):
    return lax.dot_general(
        left, right, (((1,), (1,)), ((), ())), preferred_element_type=jnp.float32
    )


def chunk_kernel(pieces, *refs):
    ins, outs, ids = (refs[i * pieces : (i + 1) * pieces] for i in range(3))
    gate_w, up_w, down_w, feature_w, tables, before, total = refs[3 * pieces : 3 * pieces + 7]
    gate_acc, up_acc, hidden_acc, in_acc, out_acc = accs = refs[3 * pieces + 7 :]
    step = pl.program_id(0)

    @pl.when(step == 0)
    def _():
        for acc in accs:
            acc[...] = jnp.zeros_like(acc)

    rows_in, rows_out = rows_of(ins), rows_of(outs)
    gate_acc[...] += dot_rows(gate_w[...], rows_in)
    up_acc[...] += dot_rows(up_w[...], rows_in)
    in_acc[...] += dot_rows(rows_in, feature_w[...])
    hidden_acc[...] += dot_rows(down_w[...], rows_out)
    out_acc[...] += dot_rows(rows_out, feature_w[...])

    @pl.when(step == pl.num_programs(0) - 1)
    def _():
        gate, up, hidden_grad = gate_acc[...], up_acc[...], hidden_acc[...]
        sigmoid = jax.nn.sigmoid(gate)
        activated = gate * sigmoid
        hidden = activated * up
        gate_grad = hidden_grad * up * sigmoid * (1.0 + gate * (1.0 - sigmoid))
        up_grad = hidden_grad * activated
        bf16 = jnp.bfloat16
        down_part = dot(tables[2], hidden.astype(bf16)).astype(bf16)
        input_part = (
            dot(tables[0], gate_grad.astype(bf16)) + dot(tables[1], up_grad.astype(bf16))
        ).astype(bf16)
        example = rows_of(ids).astype(jnp.float32)
        example = jnp.concatenate([example] * (K2 // LANES), axis=1)

        def by_example(features):
            rounded = features.astype(bf16).astype(jnp.float32)
            return jnp.concatenate(
                [jnp.where(example == e, rounded, 0.0) for e in range(EX)], axis=1
            ).astype(bf16)

        total[...] = (
            before[...]
            + dot(down_part, by_example(out_acc[...]))
            + dot(input_part, by_example(in_acc[...]))
        )


def chunk(pieces, gate_rows, up_rows, down_rows, feature_table, tables, before):
    own = pieces[0].shape[0]
    units, model = gate_rows.shape
    rows = own * len(pieces)
    depth = min(DEPTH, model)
    steps = model // depth
    whole = lambda shape: pl.BlockSpec(shape, lambda k: (0,) * len(shape))
    weight = pl.BlockSpec((units, depth), lambda k: (0, k))
    f32 = jnp.float32
    return pl.pallas_call(
        functools.partial(chunk_kernel, len(pieces)),
        grid=(steps,),
        in_specs=[pl.BlockSpec((own, depth), lambda k: (0, k))] * len(pieces)
        + [pl.BlockSpec((own, depth), lambda k: (0, steps + k))] * len(pieces)
        + [pl.BlockSpec((own, LANES), lambda k: (0, 2 * model // LANES))] * len(pieces)
        + [weight, weight, weight, pl.BlockSpec((K2, depth), lambda k: (0, k))]
        + [whole(tables.shape), whole(before.shape)],
        out_specs=whole(before.shape),
        out_shape=jax.ShapeDtypeStruct(before.shape, f32),
        scratch_shapes=[pltpu.VMEM((units, rows), f32)] * 3 + [pltpu.VMEM((rows, K2), f32)] * 2,
        compiler_params=pltpu.CompilerParams(vmem_limit_bytes=VMEM_LIMIT),
        cost_estimate=pl.CostEstimate(
            flops=2 * rows * model * (3 * units + 2 * K2),
            bytes_accessed=2 * model * (3 * units + K2 + 2 * rows),
            transcendentals=rows * units,
        ),
        name="chunk",
    )(*pieces, *pieces, *pieces, gate_rows, up_rows, down_rows, feature_table, tables, before)


def on_device(
    layout,
    inputs,
    out_grad,
    example_ids,
    gate_weight,
    up_weight,
    down_weight,
    unit_buckets,
    unit_signs,
    feature_buckets,
    feature_signs,
):
    def move(value, pairs):
        return lax.ppermute(value, "fsdp", pairs)

    me = lax.axis_index("fsdp")
    core = me % CORES
    inner = (me // CORES) % layout.inner
    outer = me // (CORES * layout.inner)
    rows = inputs.shape[0]

    unit_tables = sign_tables(unit_buckets, unit_signs, K1)
    feature_table = sign_tables(feature_buckets, feature_signs, K2)

    example = jnp.broadcast_to(example_ids[:, None], (rows, LANES)).astype(jnp.bfloat16)
    own = jnp.concatenate([inputs, out_grad, example], axis=1)

    total = jnp.zeros((K1, EX * K2), jnp.float32)
    add = lambda pieces, total: chunk(
        pieces, gate_weight.T, up_weight.T, down_weight, feature_table, unit_tables, total
    )
    if layout.inner == 2:
        swap = lambda piece: move(piece, layout.core_swap())
        here, across = own, None
        for step in range(layout.outer):
            ahead = move(here, layout.outer_ring()) if step < layout.outer - 1 else None
            next_across = move(here, layout.inner_ring())
            pieces = [here, swap(here)]
            if across is not None:
                pieces += [across, swap(across)]
            total = add(pieces, total)
            if ahead is not None:
                here, across, total = lax.optimization_barrier((ahead, next_across, total))
            else:
                across, total = lax.optimization_barrier((next_across, total))
        total = add([across, swap(across)], total)
    else:
        total = add([lax.all_gather(own, "fsdp", axis=0, tiled=True)], total)

    part = total.reshape(layout.outer, layout.inner, CORES, -1, EX * K2)
    take = lambda v, at, axis: lax.dynamic_index_in_dim(v, at, axis, keepdims=False)
    part = take(part, core, 2) + move(take(part, 1 - core, 2), layout.core_swap())
    part = take(part, inner, 1) + sum(
        move(take(part, (inner + by) % layout.inner, 1), layout.inner_shift(by))
        for by in range(1, layout.inner)
    )
    part = take(part, outer, 0) + sum(
        move(take(part, (outer + by) % layout.outer, 0), layout.outer_shift(by))
        for by in range(1, layout.outer)
    )
    factor = (3.0 * SEQ * FF * D / (K1 * K2)) ** (-0.5)
    return (factor * part).reshape(-1, EX, K2).transpose(1, 0, 2)


def solution(mesh):
    layout = Layout(mesh.shape["fsdp"])
    in_specs = (
        P(("groups", "fsdp"), None),
        P(("groups", "fsdp"), None),
        P(("groups", "fsdp")),
        P(None, "fsdp"),
        P(None, "fsdp"),
        P("fsdp", None),
        P(None, "fsdp"),
        P(None, "fsdp"),
        P(),
        P(),
    )
    out_specs = P("groups", "fsdp", None)
    return jax.shard_map(
        lambda *args: on_device(layout, *args),
        mesh=mesh,
        in_specs=in_specs,
        out_specs=out_specs,
        check_vma=False,
    )
```

```python
import jax
import jax.numpy as jnp
from jax import lax
from jax.experimental import pallas as pl
from jax.experimental.pallas import tpu as pltpu
from jax.sharding import PartitionSpec as P

D = 5120
FF = 13824
EX = 2
SEQ = 512
K1 = 256
K2 = 256
CORES = 2
OUTER = 4
DEPTH = 1024
LANES = 128
VMEM_LIMIT = 56 << 20


def sign_tables(buckets, sign_bits, buckets_count):
    matches = buckets[..., None, :] == jnp.arange(buckets_count, dtype=jnp.int32)[:, None]
    signed = (2 * sign_bits - 1).astype(jnp.bfloat16)[..., None, :]
    return jnp.where(matches, signed, jnp.zeros_like(signed))


class Layout:
    def __init__(self, count):
        self.outer = OUTER if count % (OUTER * CORES) == 0 else 1
        self.inner = count // (self.outer * CORES)
        self.count = count

    def index(self, outer, inner, core):
        return ((outer % self.outer) * self.inner + inner % self.inner) * CORES + core

    def pairs(self, step):
        places = [
            (o, i, c)
            for o in range(self.outer)
            for i in range(self.inner)
            for c in range(CORES)
        ]
        return [(self.index(o, i, c), self.index(*step(o, i, c))) for o, i, c in places]

    def outer_ring(self):
        return self.pairs(lambda o, i, c: (o + 1 - 2 * c, i, c))

    def inner_ring(self):
        return self.pairs(lambda o, i, c: (o, i + 1 - 2 * c, c))

    def outer_shift(self, by):
        return self.pairs(lambda o, i, c: (o + by, i, c))

    def inner_shift(self, by):
        return self.pairs(lambda o, i, c: (o, i + by, c))

    def core_swap(self):
        return self.pairs(lambda o, i, c: (o, i, 1 - c))


def dot(left, right):
    return jnp.dot(left, right, preferred_element_type=jnp.float32)


def dot_rows(left, right):
    return lax.dot_general(
        left, right, (((1,), (1,)), ((), ())), preferred_element_type=jnp.float32
    )


def chunk_kernel(own, offsets, refs, scratch):
    ins, outs, gate_w, up_w, down_w, feature_w, tables_in, before_in, total = refs
    in_w, out_w, in_x, out_x, in_acc, out_acc, tables, before, ids, sems, late_sems = scratch
    units, model = gate_w.shape
    pieces = len(ins)
    depth = in_w.shape[-1]
    steps = model // depth
    places = [pl.ds(p * own, own) for p in range(pieces)]

    def copies(step, slot, side):
        here = pl.ds(pl.multiple_of(step * depth, depth), depth)
        if side == 0:
            weights, buffer, xs, x_buffer = (gate_w, up_w, feature_w), in_w, ins, in_x
        else:
            weights, buffer, xs, x_buffer = (down_w, feature_w), out_w, outs, out_x
        at = 0
        found = []
        for weight in weights:
            height = weight.shape[0]
            found.append((weight.at[:, here], buffer.at[slot, pl.ds(at, height)]))
            at += height
        for x, offset, place in zip(xs, offsets[side], places):
            there = pl.ds(pl.multiple_of(offset + step * depth, LANES), depth)
            found.append((x.at[:, there], x_buffer.at[slot, place]))
        return [
            pltpu.make_async_copy(source, target, sems.at[slot, side, i])
            for i, (source, target) in enumerate(found)
        ]

    def start(step, slot):
        for side in range(2):
            for copy in copies(step, slot, side):
                copy.start()

    start(0, 0)
    late = [(tables_in, tables), (before_in, before)] + [
        (x.at[:, pl.ds(offset + model, LANES)], ids.at[place])
        for x, offset, place in zip(outs, offsets[1], places)
    ]
    late = [
        pltpu.make_async_copy(source, target, late_sems.at[i])
        for i, (source, target) in enumerate(late)
    ]
    for copy in late:
        copy.start()
    in_acc[...] = jnp.zeros_like(in_acc)
    out_acc[...] = jnp.zeros_like(out_acc)

    def body(step, _):
        slot = step % 2

        @pl.when(step < steps - 1)
        def _():
            start(step + 1, 1 - slot)

        for side, (weight, x, acc) in enumerate(((in_w, in_x, in_acc), (out_w, out_x, out_acc))):
            for copy in copies(step, slot, side):
                copy.wait()
            acc[...] += dot_rows(weight[slot], x[slot])
        return 0

    lax.fori_loop(0, steps, body, 0)
    for copy in late:
        copy.wait()

    bf16 = jnp.bfloat16
    gate, up, hidden_grad = in_acc[:units], in_acc[units : 2 * units], out_acc[:units]
    sigmoid = jax.nn.sigmoid(gate)
    activated = gate * sigmoid
    hidden = activated * up
    gate_grad = hidden_grad * up * sigmoid * (1.0 + gate * (1.0 - sigmoid))
    up_grad = hidden_grad * activated
    down_part = dot(tables[2], hidden.astype(bf16)).astype(bf16)
    input_part = (
        dot(tables[0], gate_grad.astype(bf16)) + dot(tables[1], up_grad.astype(bf16))
    ).astype(bf16)
    example = ids[...].astype(jnp.float32).T[:1, :]

    def by_example(features):
        return jnp.concatenate(
            [jnp.where(example == e, features, 0.0) for e in range(EX)], axis=0
        ).astype(bf16)

    total[...] = (
        before[...]
        + dot_rows(down_part, by_example(out_acc[units:]))
        + dot_rows(input_part, by_example(in_acc[2 * units :]))
    )


def chunk(pieces, gate_rows, up_rows, down_rows, feature_table, tables, before):
    own = pieces[0][0].shape[0]
    units, model = gate_rows.shape
    short = -units % 16
    if short:
        gate_rows, up_rows, down_rows = (
            jnp.pad(weight, ((0, short), (0, 0))) for weight in (gate_rows, up_rows, down_rows)
        )
        tables = jnp.pad(tables, ((0, 0), (0, 0), (0, short)))
        units += short
    rows = own * len(pieces)
    depth = min(DEPTH, model)
    ins, in_at, outs, out_at = zip(*pieces)
    f32, bf16 = jnp.float32, jnp.bfloat16
    in_height, out_height = 2 * units + K2, units + K2

    def kernel(*refs):
        count = len(pieces)
        named = (refs[:count], refs[count : 2 * count], *refs[2 * count : 2 * count + 7])
        chunk_kernel(own, (in_at, out_at), named, refs[2 * count + 7 :])

    return pl.pallas_call(
        kernel,
        in_specs=[pl.BlockSpec(memory_space=pl.ANY)] * (2 * len(pieces) + 6),
        out_specs=pl.BlockSpec(memory_space=pltpu.VMEM),
        out_shape=jax.ShapeDtypeStruct(before.shape, f32),
        scratch_shapes=[
            pltpu.VMEM((2, in_height, depth), bf16),
            pltpu.VMEM((2, out_height, depth), bf16),
            pltpu.VMEM((2, rows, depth), bf16),
            pltpu.VMEM((2, rows, depth), bf16),
            pltpu.VMEM((in_height, rows), f32),
            pltpu.VMEM((out_height, rows), f32),
            pltpu.VMEM(tables.shape, bf16),
            pltpu.VMEM(before.shape, f32),
            pltpu.VMEM((rows, LANES), bf16),
            pltpu.SemaphoreType.DMA((2, 2, 3 + len(pieces))),
            pltpu.SemaphoreType.DMA((2 + len(pieces),)),
        ],
        compiler_params=pltpu.CompilerParams(vmem_limit_bytes=VMEM_LIMIT),
        cost_estimate=pl.CostEstimate(
            flops=2 * rows * model * (3 * units + 2 * K2),
            bytes_accessed=2 * model * (3 * units + K2 + 2 * rows),
            transcendentals=rows * units,
        ),
        name="chunk",
    )(*ins, *outs, gate_rows, up_rows, down_rows, feature_table, tables, before)


def on_device(
    layout,
    inputs,
    out_grad,
    example_ids,
    gate_weight,
    up_weight,
    down_weight,
    unit_buckets,
    unit_signs,
    feature_buckets,
    feature_signs,
):
    def move(value, pairs):
        return lax.ppermute(value, "fsdp", pairs)

    me = lax.axis_index("fsdp")
    core = me % CORES
    inner = (me // CORES) % layout.inner
    outer = me // (CORES * layout.inner)
    rows = inputs.shape[0]

    unit_tables = sign_tables(unit_buckets, unit_signs, K1)
    feature_table = sign_tables(feature_buckets, feature_signs, K2)

    example = jnp.broadcast_to(example_ids[:, None], (rows, LANES)).astype(jnp.bfloat16)
    own = jnp.concatenate([inputs, out_grad, example], axis=1)

    total = jnp.zeros((K1, EX * K2), jnp.float32)
    add = lambda pieces, total: chunk(
        pieces, gate_weight.T, up_weight.T, down_weight, feature_table, unit_tables, total
    )
    width = inputs.shape[1]
    both = lambda piece: (piece, 0, piece, width)
    swap = lambda piece: move(piece, layout.core_swap())
    if layout.inner == 2:
        here, across = own, None
        for step in range(layout.outer):
            if step < layout.outer - 1:
                coming = [
                    move(here, layout.outer_ring()),
                    move(here, layout.inner_ring()),
                ]
            else:
                coming = [
                    move(here[:, :width], layout.inner_ring()),
                    move(across[:, width:], layout.outer_ring()),
                ]
            pieces = [both(here), both(swap(here))]
            if across is not None:
                pieces += [both(across), both(swap(across))]
            total = add(pieces, total)
            here, across, total = lax.optimization_barrier((*coming, total))
        pieces = [(here, 0, across, 0), (swap(here), 0, swap(across), 0)]
        total = add(pieces, total)
    else:
        total = add([both(lax.all_gather(own, "fsdp", axis=0, tiled=True))], total)

    part = total.reshape(layout.outer, layout.inner, CORES, -1, EX * K2)
    take = lambda v, at, axis: lax.dynamic_index_in_dim(v, at, axis, keepdims=False)
    part = take(part, core, 2) + move(take(part, 1 - core, 2), layout.core_swap())
    part = take(part, inner, 1) + sum(
        move(take(part, (inner + by) % layout.inner, 1), layout.inner_shift(by))
        for by in range(1, layout.inner)
    )
    part = take(part, outer, 0) + sum(
        move(take(part, (outer + by) % layout.outer, 0), layout.outer_shift(by))
        for by in range(1, layout.outer)
    )
    factor = (3.0 * SEQ * FF * D / (K1 * K2)) ** (-0.5)
    return (factor * part).reshape(-1, EX, K2).transpose(1, 0, 2)


def solution(mesh):
    layout = Layout(mesh.shape["fsdp"])
    in_specs = (
        P(("groups", "fsdp"), None),
        P(("groups", "fsdp"), None),
        P(("groups", "fsdp")),
        P(None, "fsdp"),
        P(None, "fsdp"),
        P("fsdp", None),
        P(None, "fsdp"),
        P(None, "fsdp"),
        P(),
        P(),
    )
    out_specs = P("groups", "fsdp", None)
    return jax.shard_map(
        lambda *args: on_device(layout, *args),
        mesh=mesh,
        in_specs=in_specs,
        out_specs=out_specs,
        check_vma=False,
    )
```

```python
import jax
import jax.numpy as jnp
from jax import lax
from jax.experimental import pallas as pl
from jax.experimental.pallas import tpu as pltpu
from jax.sharding import PartitionSpec as P

D = 5120
FF = 13824
EX = 2
SEQ = 512
K1 = 256
K2 = 256
CORES = 2
OUTER = 4
DEPTH = 1024
LANES = 128
VMEM_LIMIT = 16 << 20


def sign_tables(buckets, sign_bits, buckets_count):
    matches = buckets[..., None, :] == jnp.arange(buckets_count, dtype=jnp.int32)[:, None]
    signed = (2 * sign_bits - 1).astype(jnp.bfloat16)[..., None, :]
    return jnp.where(matches, signed, jnp.zeros_like(signed))


class Layout:
    def __init__(self, count):
        self.outer = OUTER if count % (OUTER * CORES) == 0 else 1
        self.inner = count // (self.outer * CORES)
        self.count = count

    def index(self, outer, inner, core):
        return ((outer % self.outer) * self.inner + inner % self.inner) * CORES + core

    def pairs(self, step):
        places = [
            (o, i, c)
            for o in range(self.outer)
            for i in range(self.inner)
            for c in range(CORES)
        ]
        return [(self.index(o, i, c), self.index(*step(o, i, c))) for o, i, c in places]

    def outer_ring(self):
        return self.pairs(lambda o, i, c: (o + 1 - 2 * c, i, c))

    def inner_ring(self):
        return self.pairs(lambda o, i, c: (o, i + 1 - 2 * c, c))

    def outer_shift(self, by):
        return self.pairs(lambda o, i, c: (o + by, i, c))

    def inner_shift(self, by):
        return self.pairs(lambda o, i, c: (o, i + by, c))

    def core_swap(self):
        return self.pairs(lambda o, i, c: (o, i, 1 - c))


def dot(left, right):
    return jnp.dot(left, right, preferred_element_type=jnp.float32)


def dot_rows(left, right):
    return lax.dot_general(
        left, right, (((1,), (1,)), ((), ())), preferred_element_type=jnp.float32
    )


def chunk_kernel(offsets, refs, scratch):
    ins, outs, gate_w, up_w, down_w, feature_w, tables, before, total = refs
    gate_acc, up_acc, hidden_acc, in_acc, out_acc = scratch
    model = gate_w.shape[1]
    depth = min(DEPTH, model)
    for acc in scratch:
        acc[...] = jnp.zeros_like(acc)

    def rows_of(xs, side, first, count):
        parts = [
            x[:, pl.ds(pl.multiple_of(offset + first, LANES), count)]
            for x, offset in zip(xs, offsets[side])
        ]
        return jnp.concatenate(parts, axis=0) if len(parts) > 1 else parts[0]

    def body(step, _):
        first = pl.multiple_of(step * depth, depth)
        here = pl.ds(first, depth)
        rows_in, rows_out = (rows_of(xs, side, first, depth) for side, xs in enumerate((ins, outs)))
        gate_acc[...] += dot_rows(rows_in, gate_w[:, here])
        up_acc[...] += dot_rows(rows_in, up_w[:, here])
        in_acc[...] += dot_rows(rows_in, feature_w[:, here])
        hidden_acc[...] += dot_rows(rows_out, down_w[:, here])
        out_acc[...] += dot_rows(rows_out, feature_w[:, here])
        return 0

    lax.fori_loop(0, model // depth, body, 0)

    bf16 = jnp.bfloat16
    gate, up, hidden_grad = gate_acc[...], up_acc[...], hidden_acc[...]
    sigmoid = jax.nn.sigmoid(gate)
    activated = gate * sigmoid
    hidden = activated * up
    gate_grad = hidden_grad * up * sigmoid * (1.0 + gate * (1.0 - sigmoid))
    up_grad = hidden_grad * activated
    down_part = dot_rows(hidden.astype(bf16), tables[2]).astype(bf16)
    input_part = (
        dot_rows(gate_grad.astype(bf16), tables[0]) + dot_rows(up_grad.astype(bf16), tables[1])
    ).astype(bf16)
    example = rows_of(outs, 1, model, LANES).astype(jnp.float32)
    example = jnp.concatenate([example] * (K2 // LANES), axis=1)

    def by_example(features):
        rounded = features.astype(bf16).astype(jnp.float32)
        return jnp.concatenate(
            [jnp.where(example == e, rounded, 0.0) for e in range(EX)], axis=1
        ).astype(bf16)

    total[...] = before[...] + lax.dot_general(
        jnp.concatenate([down_part, input_part], axis=0),
        jnp.concatenate([by_example(out_acc[...]), by_example(in_acc[...])], axis=0),
        (((0,), (0,)), ((), ())),
        preferred_element_type=jnp.float32,
    )


def chunk(pieces, gate_rows, up_rows, down_rows, feature_table, tables, before):
    units, model = gate_rows.shape
    count = len(pieces)
    rows = pieces[0][0].shape[0] * count
    ins, in_at, outs, out_at = zip(*pieces)
    f32 = jnp.float32

    def kernel(*refs):
        named = (refs[:count], refs[count : 2 * count], *refs[2 * count : 2 * count + 7])
        chunk_kernel((in_at, out_at), named, refs[2 * count + 7 :])

    return pl.pallas_call(
        kernel,
        in_specs=[pl.BlockSpec(memory_space=pltpu.VMEM)] * (2 * count + 6),
        out_specs=pl.BlockSpec(memory_space=pltpu.VMEM),
        out_shape=jax.ShapeDtypeStruct(before.shape, f32),
        scratch_shapes=[pltpu.VMEM((rows, units), f32)] * 3 + [pltpu.VMEM((rows, K2), f32)] * 2,
        compiler_params=pltpu.CompilerParams(vmem_limit_bytes=VMEM_LIMIT),
        cost_estimate=pl.CostEstimate(
            flops=2 * rows * model * (3 * units + 2 * K2),
            bytes_accessed=2 * model * (3 * units + K2 + 2 * rows),
            transcendentals=rows * units,
        ),
        name="chunk",
    )(*ins, *outs, gate_rows, up_rows, down_rows, feature_table, tables, before)


def on_device(
    layout,
    inputs,
    out_grad,
    example_ids,
    gate_weight,
    up_weight,
    down_weight,
    unit_buckets,
    unit_signs,
    feature_buckets,
    feature_signs,
):
    def move(value, pairs):
        return lax.ppermute(value, "fsdp", pairs)

    me = lax.axis_index("fsdp")
    core = me % CORES
    inner = (me // CORES) % layout.inner
    outer = me // (CORES * layout.inner)
    rows = inputs.shape[0]

    unit_tables = sign_tables(unit_buckets, unit_signs, K1)
    feature_table = sign_tables(feature_buckets, feature_signs, K2)

    example = jnp.broadcast_to(example_ids[:, None], (rows, LANES)).astype(jnp.bfloat16)
    own = jnp.concatenate([inputs, out_grad, example], axis=1)

    total = jnp.zeros((K1, EX * K2), jnp.float32)
    add = lambda pieces, total: chunk(
        pieces, gate_weight.T, up_weight.T, down_weight, feature_table, unit_tables, total
    )
    width = inputs.shape[1]
    both = lambda piece: (piece, 0, piece, width)
    swap = lambda piece: move(piece, layout.core_swap())
    if layout.inner == 2:
        here, across = own, None
        for step in range(layout.outer):
            if step < layout.outer - 1:
                coming = [
                    move(here, layout.outer_ring()),
                    move(here, layout.inner_ring()),
                ]
            else:
                coming = [
                    move(here[:, :width], layout.inner_ring()),
                    move(across[:, width:], layout.outer_ring()),
                ]
            pieces = [both(here), both(swap(here))]
            if across is not None:
                pieces += [both(across), both(swap(across))]
            total = add(pieces, total)
            here, across, total = lax.optimization_barrier((*coming, total))
        pieces = [(here, 0, across, 0), (swap(here), 0, swap(across), 0)]
        total = add(pieces, total)
    else:
        total = add([both(lax.all_gather(own, "fsdp", axis=0, tiled=True))], total)

    part = total.reshape(layout.outer, layout.inner, CORES, -1, EX * K2)
    take = lambda v, at, axis: lax.dynamic_index_in_dim(v, at, axis, keepdims=False)
    part = take(part, core, 2) + move(take(part, 1 - core, 2), layout.core_swap())
    part = take(part, inner, 1) + sum(
        move(take(part, (inner + by) % layout.inner, 1), layout.inner_shift(by))
        for by in range(1, layout.inner)
    )
    part = take(part, outer, 0) + sum(
        move(take(part, (outer + by) % layout.outer, 0), layout.outer_shift(by))
        for by in range(1, layout.outer)
    )
    factor = (3.0 * SEQ * FF * D / (K1 * K2)) ** (-0.5)
    return (factor * part).reshape(-1, EX, K2).transpose(1, 0, 2)


def solution(mesh):
    layout = Layout(mesh.shape["fsdp"])
    in_specs = (
        P(("groups", "fsdp"), None),
        P(("groups", "fsdp"), None),
        P(("groups", "fsdp")),
        P(None, "fsdp"),
        P(None, "fsdp"),
        P("fsdp", None),
        P(None, "fsdp"),
        P(None, "fsdp"),
        P(),
        P(),
    )
    out_specs = P("groups", "fsdp", None)
    return jax.shard_map(
        lambda *args: on_device(layout, *args),
        mesh=mesh,
        in_specs=in_specs,
        out_specs=out_specs,
        check_vma=False,
    )
```

```python
import jax
import jax.numpy as jnp
from jax import lax
from jax.experimental import pallas as pl
from jax.experimental.pallas import tpu as pltpu
from jax.sharding import PartitionSpec as P

D = 5120
FF = 13824
EX = 2
SEQ = 512
K1 = 256
K2 = 256
CORES = 2
OUTER = 4
DEPTH = 1024
LANES = 128
VMEM_LIMIT = 12 << 20


def sign_tables(buckets, sign_bits, buckets_count):
    matches = buckets[..., None, :] == jnp.arange(buckets_count, dtype=jnp.int32)[:, None]
    signed = (2 * sign_bits - 1).astype(jnp.bfloat16)[..., None, :]
    return jnp.where(matches, signed, jnp.zeros_like(signed))


class Layout:
    def __init__(self, count):
        self.outer = OUTER if count % (OUTER * CORES) == 0 else 1
        self.inner = count // (self.outer * CORES)
        self.count = count

    def index(self, outer, inner, core):
        return ((outer % self.outer) * self.inner + inner % self.inner) * CORES + core

    def pairs(self, step):
        places = [
            (o, i, c)
            for o in range(self.outer)
            for i in range(self.inner)
            for c in range(CORES)
        ]
        return [(self.index(o, i, c), self.index(*step(o, i, c))) for o, i, c in places]

    def outer_ring(self):
        return self.pairs(lambda o, i, c: (o + 1 - 2 * c, i, c))

    def inner_ring(self):
        return self.pairs(lambda o, i, c: (o, i + 1 - 2 * c, c))

    def core_swap(self):
        return self.pairs(lambda o, i, c: (o, i, 1 - c))


def dot(left, right):
    return jnp.dot(left, right, preferred_element_type=jnp.float32)


def dot_rows(left, right):
    return lax.dot_general(
        left, right, (((1,), (1,)), ((), ())), preferred_element_type=jnp.float32
    )


def chunk_kernel(offsets, refs, scratch):
    ins, outs, gate_w, up_w, down_w, feature_w, tables, before, total = refs
    gate_acc, up_acc, hidden_acc, in_acc, out_acc = scratch
    model = gate_w.shape[1]
    depth = min(DEPTH, model)
    for acc in scratch:
        acc[...] = jnp.zeros_like(acc)

    def rows_of(xs, side, first, count):
        parts = [
            x[:, pl.ds(pl.multiple_of(offset + first, LANES), count)]
            for x, offset in zip(xs, offsets[side])
        ]
        return jnp.concatenate(parts, axis=0) if len(parts) > 1 else parts[0]

    def body(step, _):
        first = pl.multiple_of(step * depth, depth)
        here = pl.ds(first, depth)
        rows_in, rows_out = (rows_of(xs, side, first, depth) for side, xs in enumerate((ins, outs)))
        gate_acc[...] += dot_rows(rows_in, gate_w[:, here])
        up_acc[...] += dot_rows(rows_in, up_w[:, here])
        in_acc[...] += dot_rows(rows_in, feature_w[:, here])
        hidden_acc[...] += dot_rows(rows_out, down_w[:, here])
        out_acc[...] += dot_rows(rows_out, feature_w[:, here])
        return 0

    lax.fori_loop(0, model // depth, body, 0)

    bf16 = jnp.bfloat16
    gate, up, hidden_grad = gate_acc[...], up_acc[...], hidden_acc[...]
    sigmoid = jax.nn.sigmoid(gate)
    activated = gate * sigmoid
    hidden = activated * up
    gate_grad = hidden_grad * up * sigmoid * (1.0 + gate * (1.0 - sigmoid))
    up_grad = hidden_grad * activated
    down_part = dot_rows(hidden.astype(bf16), tables[2]).astype(bf16)
    input_part = (
        dot_rows(gate_grad.astype(bf16), tables[0]) + dot_rows(up_grad.astype(bf16), tables[1])
    ).astype(bf16)
    example = rows_of(outs, 1, model, LANES).astype(jnp.float32)
    example = jnp.concatenate([example] * (K2 // LANES), axis=1)

    def by_example(features):
        rounded = features.astype(bf16).astype(jnp.float32)
        return jnp.concatenate(
            [jnp.where(example == e, rounded, 0.0) for e in range(EX)], axis=1
        ).astype(bf16)

    total[...] = before[...] + lax.dot_general(
        jnp.concatenate([down_part, input_part], axis=0),
        jnp.concatenate([by_example(out_acc[...]), by_example(in_acc[...])], axis=0),
        (((0,), (0,)), ((), ())),
        preferred_element_type=jnp.float32,
    )


def chunk(pieces, gate_rows, up_rows, down_rows, feature_table, tables, before):
    units, model = gate_rows.shape
    count = len(pieces)
    rows = pieces[0][0].shape[0] * count
    ins, in_at, outs, out_at = zip(*pieces)
    f32 = jnp.float32

    def kernel(*refs):
        named = (refs[:count], refs[count : 2 * count], *refs[2 * count : 2 * count + 7])
        chunk_kernel((in_at, out_at), named, refs[2 * count + 7 :])

    return pl.pallas_call(
        kernel,
        in_specs=[pl.BlockSpec(memory_space=pltpu.VMEM)] * (2 * count + 6),
        out_specs=pl.BlockSpec(memory_space=pltpu.VMEM),
        out_shape=jax.ShapeDtypeStruct(before.shape, f32),
        scratch_shapes=[pltpu.VMEM((rows, units), f32)] * 3 + [pltpu.VMEM((rows, K2), f32)] * 2,
        compiler_params=pltpu.CompilerParams(vmem_limit_bytes=VMEM_LIMIT),
        cost_estimate=pl.CostEstimate(
            flops=2 * rows * model * (3 * units + 2 * K2),
            bytes_accessed=2 * model * (3 * units + K2 + 2 * rows),
            transcendentals=rows * units,
        ),
        name="chunk",
    )(*ins, *outs, gate_rows, up_rows, down_rows, feature_table, tables, before)


def on_device(
    layout,
    inputs,
    out_grad,
    example_ids,
    gate_weight,
    up_weight,
    down_weight,
    unit_buckets,
    unit_signs,
    feature_buckets,
    feature_signs,
):
    def move(value, pairs):
        return lax.ppermute(value, "fsdp", pairs)

    rows = inputs.shape[0]

    unit_tables = sign_tables(unit_buckets, unit_signs, K1)
    feature_table = sign_tables(feature_buckets, feature_signs, K2)

    example = jnp.broadcast_to(example_ids[:, None], (rows, LANES)).astype(jnp.bfloat16)
    own = jnp.concatenate([inputs, out_grad, example], axis=1)

    total = jnp.zeros((K1, EX * K2), jnp.float32)
    add = lambda pieces, total: chunk(
        pieces, gate_weight.T, up_weight.T, down_weight, feature_table, unit_tables, total
    )
    width = inputs.shape[1]
    both = lambda piece: (piece, 0, piece, width)
    swap = lambda piece: move(piece, layout.core_swap())
    if layout.inner == 2:
        last = layout.outer - 1
        here, across, swapped = own, None, swap(own)
        for step in range(last):
            coming = [move(here, layout.outer_ring()), move(here, layout.inner_ring())]
            if step:
                total = add([both(piece) for piece in done], total)
            ahead, across, total = lax.optimization_barrier((*coming, total))
            done = [here, swapped, across, swap(across)]
            here, swapped = ahead, swap(ahead)
        coming = [
            move(here[:, :width], layout.inner_ring()),
            move(across[:, width:], layout.outer_ring()),
        ]
        total = add([both(piece) for piece in done], total)
        *sides, total = lax.optimization_barrier((*coming, total))
        split = lambda pair: (pair[0], 0, pair[1], 0)
        pieces = [both(here), both(swapped), split(sides), split([swap(side) for side in sides])]
        total = add(pieces, total)
    else:
        total = add([both(lax.all_gather(own, "fsdp", axis=0, tiled=True))], total)

    parts = total.astype(jnp.bfloat16).reshape(layout.count, -1, EX * K2)
    parts = lax.all_to_all(parts, "fsdp", 0, 0)
    part = jnp.sum(parts.astype(jnp.float32), axis=0)
    factor = (3.0 * SEQ * FF * D / (K1 * K2)) ** (-0.5)
    return (factor * part).reshape(-1, EX, K2).transpose(1, 0, 2)


def solution(mesh):
    layout = Layout(mesh.shape["fsdp"])
    in_specs = (
        P(("groups", "fsdp"), None),
        P(("groups", "fsdp"), None),
        P(("groups", "fsdp")),
        P(None, "fsdp"),
        P(None, "fsdp"),
        P("fsdp", None),
        P(None, "fsdp"),
        P(None, "fsdp"),
        P(),
        P(),
    )
    out_specs = P("groups", "fsdp", None)
    return jax.shard_map(
        lambda *args: on_device(layout, *args),
        mesh=mesh,
        in_specs=in_specs,
        out_specs=out_specs,
        check_vma=False,
    )
```

```python
import jax
import jax.numpy as jnp
from jax import lax
from jax.experimental import pallas as pl
from jax.experimental.pallas import tpu as pltpu
from jax.sharding import PartitionSpec as P

D = 5120
FF = 13824
EX = 2
SEQ = 512
K1 = 256
K2 = 256
CORES = 2
OUTER = 4
DEPTH = 1024
LANES = 128
VMEM_LIMIT = 12 << 20


def sign_tables(buckets, sign_bits, buckets_count):
    matches = buckets[..., None, :] == jnp.arange(buckets_count, dtype=jnp.int32)[:, None]
    signed = (2 * sign_bits - 1).astype(jnp.bfloat16)[..., None, :]
    return jnp.where(matches, signed, jnp.zeros_like(signed))


class Layout:
    def __init__(self, count):
        self.outer = OUTER if count % (OUTER * CORES) == 0 else 1
        self.inner = count // (self.outer * CORES)
        self.count = count

    def index(self, outer, inner, core):
        return ((outer % self.outer) * self.inner + inner % self.inner) * CORES + core

    def pairs(self, step, cores=range(CORES)):
        places = [
            (o, i, c) for o in range(self.outer) for i in range(self.inner) for c in cores
        ]
        return [(self.index(o, i, c), self.index(*step(o, i, c))) for o, i, c in places]

    def outer_ring(self, *cores):
        return self.pairs(lambda o, i, c: (o + 1 - 2 * c, i, c), *cores)

    def inner_ring(self, *cores):
        return self.pairs(lambda o, i, c: (o, i + 1 - 2 * c, c), *cores)

    def core_swap(self):
        return self.pairs(lambda o, i, c: (o, i, 1 - c))


def dot(left, right):
    return jnp.dot(left, right, preferred_element_type=jnp.float32)


def dot_rows(left, right):
    return lax.dot_general(
        left, right, (((1,), (1,)), ((), ())), preferred_element_type=jnp.float32
    )


def chunk_kernel(offsets, refs, scratch):
    ins, outs, gate_w, up_w, down_w, feature_w, tables, before, total = refs
    gate_acc, up_acc, hidden_acc, in_acc, out_acc = scratch
    model = gate_w.shape[1]
    depth = min(DEPTH, model)
    for acc in scratch:
        acc[...] = jnp.zeros_like(acc)

    def rows_of(xs, side, first, count):
        parts = [
            x[:, pl.ds(pl.multiple_of(offset + first, LANES), count)]
            for x, offset in zip(xs, offsets[side])
        ]
        return jnp.concatenate(parts, axis=0) if len(parts) > 1 else parts[0]

    def body(step, _):
        first = pl.multiple_of(step * depth, depth)
        here = pl.ds(first, depth)
        rows_in, rows_out = (rows_of(xs, side, first, depth) for side, xs in enumerate((ins, outs)))
        gate_acc[...] += dot_rows(rows_in, gate_w[:, here])
        up_acc[...] += dot_rows(rows_in, up_w[:, here])
        in_acc[...] += dot_rows(rows_in, feature_w[:, here])
        hidden_acc[...] += dot_rows(rows_out, down_w[:, here])
        out_acc[...] += dot_rows(rows_out, feature_w[:, here])
        return 0

    lax.fori_loop(0, model // depth, body, 0)

    bf16 = jnp.bfloat16
    gate, up, hidden_grad = gate_acc[...], up_acc[...], hidden_acc[...]
    sigmoid = jax.nn.sigmoid(gate)
    activated = gate * sigmoid
    hidden = activated * up
    gate_grad = hidden_grad * up * sigmoid * (1.0 + gate * (1.0 - sigmoid))
    up_grad = hidden_grad * activated
    down_part = dot_rows(hidden.astype(bf16), tables[2]).astype(bf16)
    input_part = (
        dot_rows(gate_grad.astype(bf16), tables[0]) + dot_rows(up_grad.astype(bf16), tables[1])
    ).astype(bf16)
    example = rows_of(outs, 1, model, LANES).astype(jnp.float32)
    example = jnp.concatenate([example] * (K2 // LANES), axis=1)

    def by_example(features):
        rounded = features.astype(bf16).astype(jnp.float32)
        return jnp.concatenate(
            [jnp.where(example == e, rounded, 0.0) for e in range(EX)], axis=1
        ).astype(bf16)

    total[...] = before[...] + lax.dot_general(
        jnp.concatenate([down_part, input_part], axis=0),
        jnp.concatenate([by_example(out_acc[...]), by_example(in_acc[...])], axis=0),
        (((0,), (0,)), ((), ())),
        preferred_element_type=jnp.float32,
    )


def chunk(pieces, gate_rows, up_rows, down_rows, feature_table, tables, before):
    units, model = gate_rows.shape
    count = len(pieces)
    rows = pieces[0][0].shape[0] * count
    ins, in_at, outs, out_at = zip(*pieces)
    f32 = jnp.float32

    def kernel(*refs):
        named = (refs[:count], refs[count : 2 * count], *refs[2 * count : 2 * count + 7])
        chunk_kernel((in_at, out_at), named, refs[2 * count + 7 :])

    return pl.pallas_call(
        kernel,
        in_specs=[pl.BlockSpec(memory_space=pltpu.VMEM)] * (2 * count + 6),
        out_specs=pl.BlockSpec(memory_space=pltpu.VMEM),
        out_shape=jax.ShapeDtypeStruct(before.shape, f32),
        scratch_shapes=[pltpu.VMEM((rows, units), f32)] * 3 + [pltpu.VMEM((rows, K2), f32)] * 2,
        compiler_params=pltpu.CompilerParams(vmem_limit_bytes=VMEM_LIMIT),
        cost_estimate=pl.CostEstimate(
            flops=2 * rows * model * (3 * units + 2 * K2),
            bytes_accessed=2 * model * (3 * units + K2 + 2 * rows),
            transcendentals=rows * units,
        ),
        name="chunk",
    )(*ins, *outs, gate_rows, up_rows, down_rows, feature_table, tables, before)


def on_device(
    layout,
    inputs,
    out_grad,
    example_ids,
    gate_weight,
    up_weight,
    down_weight,
    unit_buckets,
    unit_signs,
    feature_buckets,
    feature_signs,
):
    def move(value, pairs):
        return lax.ppermute(value, "fsdp", pairs)

    rows = inputs.shape[0]

    unit_tables = sign_tables(unit_buckets, unit_signs, K1)
    feature_table = sign_tables(feature_buckets, feature_signs, K2)

    example = jnp.broadcast_to(example_ids[:, None], (rows, LANES)).astype(jnp.bfloat16)
    own = jnp.concatenate([inputs, out_grad, example], axis=1)

    total = jnp.zeros((K1, EX * K2), jnp.float32)
    add = lambda pieces, total: chunk(
        pieces, gate_weight.T, up_weight.T, down_weight, feature_table, unit_tables, total
    )
    width = inputs.shape[1]
    both = lambda piece: (piece, 0, piece, width)
    swap = lambda piece: move(piece, layout.core_swap())
    if layout.inner == 2:
        last = layout.outer - 1
        here, across, swapped = own, None, swap(own)
        first = [move(own, ring([0])) for ring in (layout.outer_ring, layout.inner_ring)]
        later, swapped, feature_table, unit_tables = lax.optimization_barrier(
            (own, swapped, feature_table, unit_tables)
        )
        second = [move(later, ring([1])) for ring in (layout.outer_ring, layout.inner_ring)]
        is_first = lax.axis_index("fsdp") % CORES == 0
        for step in range(last):
            if step == 0:
                four = lax.optimization_barrier((*first, *second))
                first, second = four[:2], four[2:]
                coming = [jnp.where(is_first, *pair) for pair in zip(first, second)]
            else:
                coming = [move(here, layout.outer_ring()), move(here, layout.inner_ring())]
                total = add([both(piece) for piece in done], total)
            ahead, across, total = lax.optimization_barrier((*coming, total))
            done = [here, swapped, across, swap(across)]
            here, swapped = ahead, swap(ahead)
        coming = [
            move(here[:, :width], layout.inner_ring()),
            move(across[:, width:], layout.outer_ring()),
        ]
        total = add([both(piece) for piece in done], total)
        *sides, total = lax.optimization_barrier((*coming, total))
        split = lambda pair: (pair[0], 0, pair[1], 0)
        pieces = [both(here), both(swapped), split(sides), split([swap(side) for side in sides])]
        total = add(pieces, total)
    else:
        total = add([both(lax.all_gather(own, "fsdp", axis=0, tiled=True))], total)

    parts = total.astype(jnp.bfloat16).reshape(layout.count, -1, EX * K2)
    parts = lax.all_to_all(parts, "fsdp", 0, 0)
    part = jnp.sum(parts.astype(jnp.float32), axis=0)
    factor = (3.0 * SEQ * FF * D / (K1 * K2)) ** (-0.5)
    return (factor * part).reshape(-1, EX, K2).transpose(1, 0, 2)


def solution(mesh):
    layout = Layout(mesh.shape["fsdp"])
    in_specs = (
        P(("groups", "fsdp"), None),
        P(("groups", "fsdp"), None),
        P(("groups", "fsdp")),
        P(None, "fsdp"),
        P(None, "fsdp"),
        P("fsdp", None),
        P(None, "fsdp"),
        P(None, "fsdp"),
        P(),
        P(),
    )
    out_specs = P("groups", "fsdp", None)
    return jax.shard_map(
        lambda *args: on_device(layout, *args),
        mesh=mesh,
        in_specs=in_specs,
        out_specs=out_specs,
        check_vma=False,
    )
```

```python
import jax
import jax.numpy as jnp
from jax import lax
from jax.experimental import pallas as pl
from jax.experimental.pallas import tpu as pltpu
from jax.sharding import PartitionSpec as P

D = 5120
FF = 13824
EX = 2
SEQ = 512
K1 = 256
K2 = 256
CORES = 2
OUTER = 4
DEPTH = 1024
LANES = 128
VMEM_LIMIT = 12 << 20


def sign_tables(buckets, sign_bits, buckets_count):
    matches = buckets[..., None, :] == jnp.arange(buckets_count, dtype=jnp.int32)[:, None]
    signed = (2 * sign_bits - 1).astype(jnp.bfloat16)[..., None, :]
    return jnp.where(matches, signed, jnp.zeros_like(signed))


class Layout:
    def __init__(self, count):
        self.outer = OUTER if count % (OUTER * CORES) == 0 else 1
        self.inner = count // (self.outer * CORES)
        self.count = count

    def index(self, outer, inner, core):
        return ((outer % self.outer) * self.inner + inner % self.inner) * CORES + core

    def pairs(self, step):
        places = [
            (o, i, c)
            for o in range(self.outer)
            for i in range(self.inner)
            for c in range(CORES)
        ]
        return [(self.index(o, i, c), self.index(*step(o, i, c))) for o, i, c in places]

    def outer_ring(self):
        return self.pairs(lambda o, i, c: (o + 1 - 2 * c, i, c))

    def inner_ring(self):
        return self.pairs(lambda o, i, c: (o, i + 1 - 2 * c, c))

    def core_swap(self):
        return self.pairs(lambda o, i, c: (o, i, 1 - c))


def dot(left, right):
    return jnp.dot(left, right, preferred_element_type=jnp.float32)


def dot_rows(left, right):
    return lax.dot_general(
        left, right, (((1,), (1,)), ((), ())), preferred_element_type=jnp.float32
    )


def joined(refs, lanes):
    parts = [ref[:, lanes] for ref in refs]
    return jnp.concatenate(parts, axis=0) if len(parts) > 1 else parts[0]


def add_products(refs, model, sums):
    depth = min(DEPTH, model)
    for acc, _ in sums:
        acc[...] = jnp.zeros_like(acc)

    def body(step, _):
        here = pl.ds(pl.multiple_of(step * depth, depth), depth)
        rows = joined(refs, here)
        for acc, weight in sums:
            acc[...] += dot_rows(rows, weight[:, here])
        return 0

    lax.fori_loop(0, model // depth, body, 0)


def forward_kernel(pieces, *refs):
    gate_w, up_w, feature_w, tables = refs[pieces : pieces + 4]
    to_gate, to_up, down_part, feature_in = refs[pieces + 4 : pieces + 8]
    gate_acc, up_acc, feature_acc = refs[pieces + 8 :]
    sums = ((gate_acc, gate_w), (up_acc, up_w), (feature_acc, feature_w))
    add_products(refs[:pieces], gate_w.shape[1], sums)
    gate, up = gate_acc[...], up_acc[...]
    sigmoid = jax.nn.sigmoid(gate)
    activated = gate * sigmoid
    to_gate[...] = up * sigmoid * (1.0 + gate * (1.0 - sigmoid))
    to_up[...] = activated
    hidden = (activated * up).astype(jnp.bfloat16)
    down_part[...] = dot_rows(hidden, tables[2]).astype(jnp.bfloat16)
    feature_in[...] = feature_acc[...].astype(jnp.bfloat16)


def backward_kernel(pieces, *refs):
    down_w, feature_w, tables, to_gate, to_up, down_part, feature_in, before = refs[
        pieces : pieces + 8
    ]
    total, hidden_acc, feature_acc = refs[pieces + 8 :]
    model = down_w.shape[1]
    add_products(refs[:pieces], model, ((hidden_acc, down_w), (feature_acc, feature_w)))
    bf16 = jnp.bfloat16
    hidden_grad = hidden_acc[...]
    gate_grad = (hidden_grad * to_gate[...]).astype(bf16)
    up_grad = (hidden_grad * to_up[...]).astype(bf16)
    input_part = (dot_rows(gate_grad, tables[0]) + dot_rows(up_grad, tables[1])).astype(bf16)
    example = joined(refs[:pieces], pl.ds(model, LANES)).astype(jnp.float32)
    example = jnp.concatenate([example] * (K2 // LANES), axis=1)

    def by_example(features):
        features = features.astype(jnp.float32)
        return jnp.concatenate(
            [jnp.where(example == e, features, 0.0) for e in range(EX)], axis=1
        ).astype(bf16)

    feature_out = feature_acc[...].astype(bf16)
    total[...] = before[...] + lax.dot_general(
        jnp.concatenate([down_part[...], input_part], axis=0),
        jnp.concatenate([by_example(feature_out), by_example(feature_in[...])], axis=0),
        (((0,), (0,)), ((), ())),
        preferred_element_type=jnp.float32,
    )


def on_chip(kernel, name, pieces, operands, outs, sums):
    rows = sum(piece.shape[0] for piece in pieces)
    vmem = pl.BlockSpec(memory_space=pltpu.VMEM)
    return pl.pallas_call(
        lambda *refs: kernel(len(pieces), *refs),
        in_specs=[vmem] * (len(pieces) + len(operands)),
        out_specs=[vmem] * len(outs),
        out_shape=outs,
        scratch_shapes=[pltpu.VMEM((rows, columns), jnp.float32) for columns in sums],
        compiler_params=pltpu.CompilerParams(vmem_limit_bytes=VMEM_LIMIT),
        cost_estimate=pl.CostEstimate(flops=0, bytes_accessed=0, transcendentals=0),
        name=name,
    )(*pieces, *operands)


def forward(pieces, gate_rows, up_rows, feature_table, tables):
    units, model = gate_rows.shape
    rows = sum(piece.shape[0] for piece in pieces)
    outs = [
        jax.ShapeDtypeStruct((rows, units), jnp.float32),
        jax.ShapeDtypeStruct((rows, units), jnp.float32),
        jax.ShapeDtypeStruct((rows, K1), jnp.bfloat16),
        jax.ShapeDtypeStruct((rows, K2), jnp.bfloat16),
    ]
    operands = (gate_rows, up_rows, feature_table, tables)
    return on_chip(forward_kernel, "forward", pieces, operands, outs, (units, units, K2))


def backward(pieces, down_rows, feature_table, tables, saved, before):
    units, model = down_rows.shape
    outs = [jax.ShapeDtypeStruct(before.shape, jnp.float32)]
    operands = (down_rows, feature_table, tables, *saved, before)
    return on_chip(backward_kernel, "backward", pieces, operands, outs, (units, K2))[0]


def on_device(
    layout,
    inputs,
    out_grad,
    example_ids,
    gate_weight,
    up_weight,
    down_weight,
    unit_buckets,
    unit_signs,
    feature_buckets,
    feature_signs,
):
    def move(value, pairs):
        return lax.ppermute(value, "fsdp", pairs)

    rows = inputs.shape[0]

    unit_tables = sign_tables(unit_buckets, unit_signs, K1)
    feature_table = sign_tables(feature_buckets, feature_signs, K2)

    example = jnp.broadcast_to(example_ids[:, None], (rows, LANES)).astype(jnp.bfloat16)
    tagged = jnp.concatenate([out_grad, example], axis=1)
    gate_rows, up_rows = gate_weight.T, up_weight.T
    total = jnp.zeros((K1, EX * K2), jnp.float32)

    if layout.inner == 2:
        ahead = lambda piece: move(piece, layout.outer_ring())
        aside = lambda piece: move(piece, layout.inner_ring())
        swap = lambda piece: [
            move(part, layout.core_swap()) for part in jnp.split(piece, 2, axis=0)
        ]
        after = lax.optimization_barrier
        last = layout.outer - 1
        here_in, here_out = inputs, tagged
        coming_in = ahead(here_in), aside(here_in)
        here_out, feature_table, unit_tables = after((here_out, feature_table, unit_tables))
        coming_out = ahead(here_out), aside(here_out)
        swapped_in = swap(here_in)
        for step in range(layout.outer + 1)[1:]:
            if step <= last:
                next_in, across_in, total = after((*coming_in, total))
                coming_in = (ahead(next_in) if step < last else None), aside(next_in)
            else:
                across_in, total = after((coming_in[1], total))
            swapped_across = swap(across_in)
            here_out, swapped_across = after((here_out, swapped_across))
            swapped_out = swap(here_out)
            pieces = [here_in, *swapped_in, across_in, *swapped_across]
            saved = forward(pieces, gate_rows, up_rows, feature_table, unit_tables)
            if step <= last:
                next_out, across_out, saved = after((*coming_out, saved))
            else:
                across_out, saved = after((coming_out[1], saved))
            if step < last:
                coming_out = ahead(next_out), aside(next_out)
            elif step == last:
                coming_out = None, ahead(across_out)
            pieces = [here_out, *swapped_out, across_out, *swap(across_out)]
            total = backward(pieces, down_weight, feature_table, unit_tables, saved, total)
            if step <= last:
                here_in, here_out = next_in, next_out
                here_in, total = after((here_in, total))
                swapped_in = swap(here_in)
    else:
        gather = lambda piece: lax.all_gather(piece, "fsdp", axis=0, tiled=True)
        saved = forward([gather(inputs)], gate_rows, up_rows, feature_table, unit_tables)
        total = backward([gather(tagged)], down_weight, feature_table, unit_tables, saved, total)

    parts = total.astype(jnp.bfloat16).reshape(layout.count, -1, EX * K2)
    parts = lax.all_to_all(parts, "fsdp", 0, 0)
    part = jnp.sum(parts.astype(jnp.float32), axis=0)
    factor = (3.0 * SEQ * FF * D / (K1 * K2)) ** (-0.5)
    return (factor * part).reshape(-1, EX, K2).transpose(1, 0, 2)


def solution(mesh):
    layout = Layout(mesh.shape["fsdp"])
    in_specs = (
        P(("groups", "fsdp"), None),
        P(("groups", "fsdp"), None),
        P(("groups", "fsdp")),
        P(None, "fsdp"),
        P(None, "fsdp"),
        P("fsdp", None),
        P(None, "fsdp"),
        P(None, "fsdp"),
        P(),
        P(),
    )
    out_specs = P("groups", "fsdp", None)
    return jax.shard_map(
        lambda *args: on_device(layout, *args),
        mesh=mesh,
        in_specs=in_specs,
        out_specs=out_specs,
        check_vma=False,
    )
```

```python
import jax
import jax.numpy as jnp
from jax import lax
from jax.experimental import pallas as pl
from jax.experimental.pallas import tpu as pltpu
from jax.sharding import PartitionSpec as P

D = 5120
FF = 13824
EX = 2
SEQ = 512
K1 = 256
K2 = 256
CORES = 2
OUTER = 4
DEPTH = 2560
LANES = 128
VMEM_LIMIT = 12 << 20


def sign_tables(buckets, sign_bits, buckets_count):
    matches = buckets[..., None, :] == jnp.arange(buckets_count, dtype=jnp.int32)[:, None]
    signed = (2 * sign_bits - 1).astype(jnp.bfloat16)[..., None, :]
    return jnp.where(matches, signed, jnp.zeros_like(signed))


class Layout:
    def __init__(self, count):
        self.outer = OUTER if count % (OUTER * CORES) == 0 else 1
        self.inner = count // (self.outer * CORES)
        self.count = count

    def index(self, outer, inner, core):
        return ((outer % self.outer) * self.inner + inner % self.inner) * CORES + core

    def pairs(self, step):
        places = [
            (o, i, c)
            for o in range(self.outer)
            for i in range(self.inner)
            for c in range(CORES)
        ]
        return [(self.index(o, i, c), self.index(*step(o, i, c))) for o, i, c in places]

    def outer_ring(self):
        return self.pairs(lambda o, i, c: (o + 1 - 2 * c, i, c))

    def inner_ring(self):
        return self.pairs(lambda o, i, c: (o, i + 1 - 2 * c, c))

    def core_swap(self):
        return self.pairs(lambda o, i, c: (o, i, 1 - c))


def dot(left, right):
    return jnp.dot(left, right, preferred_element_type=jnp.float32)


def dot_rows(left, right):
    return lax.dot_general(
        left, right, (((1,), (1,)), ((), ())), preferred_element_type=jnp.float32
    )


def joined(refs, lanes):
    parts = [ref[:, lanes] for ref in refs]
    return jnp.concatenate(parts, axis=0) if len(parts) > 1 else parts[0]


def add_products(refs, model, sums):
    depth = min(DEPTH, model)
    for acc, _ in sums:
        acc[...] = jnp.zeros_like(acc)

    def body(step, _):
        here = pl.ds(pl.multiple_of(step * depth, depth), depth)
        rows = joined(refs, here)
        for acc, weight in sums:
            acc[...] += dot_rows(rows, weight[:, here])
        return 0

    lax.fori_loop(0, model // depth, body, 0)


def forward_kernel(pieces, *refs):
    gate_w, up_w, feature_w, tables = refs[pieces : pieces + 4]
    to_gate, to_up, down_part, feature_in = refs[pieces + 4 : pieces + 8]
    gate_acc, up_acc, feature_acc = refs[pieces + 8 :]
    sums = ((gate_acc, gate_w), (up_acc, up_w), (feature_acc, feature_w))
    add_products(refs[:pieces], gate_w.shape[1], sums)
    gate, up = gate_acc[...], up_acc[...]
    sigmoid = jax.nn.sigmoid(gate)
    activated = gate * sigmoid
    to_gate[...] = up * sigmoid * (1.0 + gate * (1.0 - sigmoid))
    to_up[...] = activated
    hidden = (activated * up).astype(jnp.bfloat16)
    down_part[...] = dot_rows(hidden, tables[2]).astype(jnp.bfloat16)
    feature_in[...] = feature_acc[...].astype(jnp.bfloat16)


def backward_kernel(pieces, *refs):
    down_w, feature_w, tables, to_gate, to_up, down_part, feature_in, before = refs[
        pieces : pieces + 8
    ]
    total, hidden_acc, feature_acc = refs[pieces + 8 :]
    model = down_w.shape[1]
    add_products(refs[:pieces], model, ((hidden_acc, down_w), (feature_acc, feature_w)))
    bf16 = jnp.bfloat16
    hidden_grad = hidden_acc[...]
    gate_grad = (hidden_grad * to_gate[...]).astype(bf16)
    up_grad = (hidden_grad * to_up[...]).astype(bf16)
    input_part = (dot_rows(gate_grad, tables[0]) + dot_rows(up_grad, tables[1])).astype(bf16)
    example = joined(refs[:pieces], pl.ds(model, LANES)).astype(jnp.float32)
    example = jnp.concatenate([example] * (K2 // LANES), axis=1)

    def by_example(features):
        features = features.astype(jnp.float32)
        return jnp.concatenate(
            [jnp.where(example == e, features, 0.0) for e in range(EX)], axis=1
        ).astype(bf16)

    feature_out = feature_acc[...].astype(bf16)
    total[...] = before[...] + lax.dot_general(
        jnp.concatenate([down_part[...], input_part], axis=0),
        jnp.concatenate([by_example(feature_out), by_example(feature_in[...])], axis=0),
        (((0,), (0,)), ((), ())),
        preferred_element_type=jnp.float32,
    )


def on_chip(kernel, name, pieces, operands, outs, sums):
    rows = sum(piece.shape[0] for piece in pieces)
    vmem = pl.BlockSpec(memory_space=pltpu.VMEM)
    return pl.pallas_call(
        lambda *refs: kernel(len(pieces), *refs),
        in_specs=[vmem] * (len(pieces) + len(operands)),
        out_specs=[vmem] * len(outs),
        out_shape=outs,
        scratch_shapes=[pltpu.VMEM((rows, columns), jnp.float32) for columns in sums],
        compiler_params=pltpu.CompilerParams(vmem_limit_bytes=VMEM_LIMIT),
        cost_estimate=pl.CostEstimate(flops=0, bytes_accessed=0, transcendentals=0),
        name=name,
    )(*pieces, *operands)


def forward(pieces, gate_rows, up_rows, feature_table, tables):
    units, model = gate_rows.shape
    rows = sum(piece.shape[0] for piece in pieces)
    outs = [
        jax.ShapeDtypeStruct((rows, units), jnp.float32),
        jax.ShapeDtypeStruct((rows, units), jnp.float32),
        jax.ShapeDtypeStruct((rows, K1), jnp.bfloat16),
        jax.ShapeDtypeStruct((rows, K2), jnp.bfloat16),
    ]
    operands = (gate_rows, up_rows, feature_table, tables)
    return on_chip(forward_kernel, "forward", pieces, operands, outs, (units, units, K2))


def backward(pieces, down_rows, feature_table, tables, saved, before):
    units, model = down_rows.shape
    outs = [jax.ShapeDtypeStruct(before.shape, jnp.float32)]
    operands = (down_rows, feature_table, tables, *saved, before)
    return on_chip(backward_kernel, "backward", pieces, operands, outs, (units, K2))[0]


def on_device(
    layout,
    inputs,
    out_grad,
    example_ids,
    gate_weight,
    up_weight,
    down_weight,
    unit_buckets,
    unit_signs,
    feature_buckets,
    feature_signs,
):
    def move(value, pairs):
        return lax.ppermute(value, "fsdp", pairs)

    rows = inputs.shape[0]

    unit_tables = sign_tables(unit_buckets, unit_signs, K1)
    feature_table = sign_tables(feature_buckets, feature_signs, K2)

    example = jnp.broadcast_to(example_ids[:, None], (rows, LANES)).astype(jnp.bfloat16)
    tagged = jnp.concatenate([out_grad, example], axis=1)
    gate_rows, up_rows = gate_weight.T, up_weight.T
    total = jnp.zeros((K1, EX * K2), jnp.float32)

    if layout.inner == 2:
        ahead = lambda piece: move(piece, layout.outer_ring())
        aside = lambda piece: move(piece, layout.inner_ring())
        swap = lambda piece: [
            move(part, layout.core_swap()) for part in jnp.split(piece, 2, axis=0)
        ]
        after = lax.optimization_barrier
        first_side = lambda rows_in: forward(
            rows_in, gate_rows, up_rows, feature_table, unit_tables
        )
        other_side = lambda rows_out, saved, total: backward(
            rows_out, down_weight, feature_table, unit_tables, saved, total
        )
        last = layout.outer - 1
        here_in, here_out = inputs, tagged
        coming_in = ahead(here_in), aside(here_in)
        here_out, feature_table, unit_tables = after((here_out, feature_table, unit_tables))
        coming_out = ahead(here_out), aside(here_out)
        swapped_in = swap(here_in)
        for step in range(1, last):
            next_in, across_in, total = after((*coming_in, total))
            coming_in = ahead(next_in), aside(next_in)
            swapped_across = swap(across_in)
            here_out, swapped_across = after((here_out, swapped_across))
            swapped_out = swap(here_out)
            saved = first_side([here_in, *swapped_in, across_in, *swapped_across])
            next_out, across_out, saved = after((*coming_out, saved))
            by_inner = aside(next_out) if step < last - 1 else ahead(across_out)
            coming_out = ahead(next_out), by_inner
            rows_out = [here_out, *swapped_out, across_out, *swap(across_out)]
            total = other_side(rows_out, saved, total)
            here_in, total = after((next_in, total))
            here_out, swapped_in = next_out, swap(here_in)

        last_in, across_in, total = after((*coming_in, total))
        coming_in = aside(last_in)
        swapped_last, swapped_across = after((swap(last_in), swap(across_in)))
        saved = first_side([here_in, *swapped_in, last_in, *swapped_last])
        last_out, saved = after((coming_out[0], saved))
        coming_last = aside(last_out)
        here_out, saved = after((here_out, saved))
        rows_out = [here_out, *swap(here_out), last_out, *swap(last_out)]
        corner_in, saved = after((coming_in, saved))
        swapped_corner = swap(corner_in)
        total = other_side(rows_out, saved, total)
        corner_in, total = after((corner_in, total))
        saved = first_side([across_in, *swapped_across, corner_in, *swapped_corner])
        across_out, saved = after((coming_out[1], saved))
        swapped_out = swap(across_out)
        corner_out, saved = after((coming_last, saved))
        rows_out = [across_out, *swapped_out, corner_out, *swap(corner_out)]
        total = other_side(rows_out, saved, total)
    else:
        gather = lambda piece: lax.all_gather(piece, "fsdp", axis=0, tiled=True)
        saved = forward([gather(inputs)], gate_rows, up_rows, feature_table, unit_tables)
        total = backward([gather(tagged)], down_weight, feature_table, unit_tables, saved, total)

    parts = total.astype(jnp.bfloat16).reshape(layout.count, -1, EX * K2)
    parts = lax.all_to_all(parts, "fsdp", 0, 0)
    part = jnp.sum(parts.astype(jnp.float32), axis=0)
    factor = (3.0 * SEQ * FF * D / (K1 * K2)) ** (-0.5)
    return (factor * part).reshape(-1, EX, K2).transpose(1, 0, 2)


def solution(mesh):
    layout = Layout(mesh.shape["fsdp"])
    in_specs = (
        P(("groups", "fsdp"), None),
        P(("groups", "fsdp"), None),
        P(("groups", "fsdp")),
        P(None, "fsdp"),
        P(None, "fsdp"),
        P("fsdp", None),
        P(None, "fsdp"),
        P(None, "fsdp"),
        P(),
        P(),
    )
    out_specs = P("groups", "fsdp", None)
    return jax.shard_map(
        lambda *args: on_device(layout, *args),
        mesh=mesh,
        in_specs=in_specs,
        out_specs=out_specs,
        check_vma=False,
    )
```

```python
import jax
import jax.numpy as jnp
from jax import lax
from jax.experimental import pallas as pl
from jax.experimental.pallas import tpu as pltpu
from jax.sharding import PartitionSpec as P

D = 5120
FF = 13824
EX = 2
SEQ = 512
K1 = 256
K2 = 256
CORES = 2
OUTER = 4
DEPTH = 2560
LANES = 128
VMEM_LIMIT = 12 << 20


def sign_tables(buckets, sign_bits, buckets_count):
    matches = buckets[..., None, :] == jnp.arange(buckets_count, dtype=jnp.int32)[:, None]
    signed = (2 * sign_bits - 1).astype(jnp.bfloat16)[..., None, :]
    return jnp.where(matches, signed, jnp.zeros_like(signed))


class Layout:
    def __init__(self, count):
        self.outer = OUTER if count % (OUTER * CORES) == 0 else 1
        self.inner = count // (self.outer * CORES)
        self.count = count

    def index(self, outer, inner, core):
        return ((outer % self.outer) * self.inner + inner % self.inner) * CORES + core

    def pairs(self, step):
        places = [
            (o, i, c)
            for o in range(self.outer)
            for i in range(self.inner)
            for c in range(CORES)
        ]
        return [(self.index(o, i, c), self.index(*step(o, i, c))) for o, i, c in places]

    def outer_ring(self):
        return self.pairs(lambda o, i, c: (o + 1 - 2 * c, i, c))

    def inner_ring(self):
        return self.pairs(lambda o, i, c: (o, i + 1 - 2 * c, c))

    def core_swap(self):
        return self.pairs(lambda o, i, c: (o, i, 1 - c))


def dot(left, right):
    return jnp.dot(left, right, preferred_element_type=jnp.float32)


def dot_rows(left, right):
    return lax.dot_general(
        left, right, (((1,), (1,)), ((), ())), preferred_element_type=jnp.float32
    )


def joined(refs, lanes):
    parts = [ref[:, lanes] for ref in refs]
    return jnp.concatenate(parts, axis=0) if len(parts) > 1 else parts[0]


def add_products(refs, model, sums):
    depth = min(DEPTH, model)
    for acc, _ in sums:
        acc[...] = jnp.zeros_like(acc)

    def body(step, _):
        here = pl.ds(pl.multiple_of(step * depth, depth), depth)
        rows = joined(refs, here)
        for acc, weight in sums:
            acc[...] += dot_rows(rows, weight[:, here])
        return 0

    lax.fori_loop(0, model // depth, body, 0)


def forward_kernel(pieces, *refs):
    gate_w, up_w, feature_w, tables = refs[pieces : pieces + 4]
    to_gate, to_up, down_part, feature_in = refs[pieces + 4 : pieces + 8]
    gate_acc, up_acc, feature_acc = refs[pieces + 8 :]
    sums = ((gate_acc, gate_w), (up_acc, up_w), (feature_acc, feature_w))
    add_products(refs[:pieces], gate_w.shape[1], sums)
    gate, up = gate_acc[...], up_acc[...]
    sigmoid = jax.nn.sigmoid(gate)
    activated = gate * sigmoid
    to_gate[...] = up * sigmoid * (1.0 + gate * (1.0 - sigmoid))
    to_up[...] = activated
    hidden = (activated * up).astype(jnp.bfloat16)
    down_part[...] = dot_rows(hidden, tables[2]).astype(jnp.bfloat16)
    feature_in[...] = feature_acc[...].astype(jnp.bfloat16)


def backward_kernel(pieces, *refs):
    down_w, feature_w, tables, to_gate, to_up, down_part, feature_in, before = refs[
        pieces : pieces + 8
    ]
    total, hidden_acc, feature_acc = refs[pieces + 8 :]
    model = down_w.shape[1]
    add_products(refs[:pieces], model, ((hidden_acc, down_w), (feature_acc, feature_w)))
    bf16 = jnp.bfloat16
    hidden_grad = hidden_acc[...]
    gate_grad = (hidden_grad * to_gate[...]).astype(bf16)
    up_grad = (hidden_grad * to_up[...]).astype(bf16)
    input_part = (dot_rows(gate_grad, tables[0]) + dot_rows(up_grad, tables[1])).astype(bf16)
    example = joined(refs[:pieces], pl.ds(model, LANES)).astype(jnp.float32)
    example = jnp.concatenate([example] * (K2 // LANES), axis=1)

    def by_example(features):
        features = features.astype(jnp.float32)
        return jnp.concatenate(
            [jnp.where(example == e, features, 0.0) for e in range(EX)], axis=1
        ).astype(bf16)

    feature_out = feature_acc[...].astype(bf16)
    total[...] = before[...] + lax.dot_general(
        jnp.concatenate([down_part[...], input_part], axis=0),
        jnp.concatenate([by_example(feature_out), by_example(feature_in[...])], axis=0),
        (((0,), (0,)), ((), ())),
        preferred_element_type=jnp.float32,
    )


def on_chip(kernel, name, pieces, operands, outs, sums):
    rows = sum(piece.shape[0] for piece in pieces)
    vmem = pl.BlockSpec(memory_space=pltpu.VMEM)
    return pl.pallas_call(
        lambda *refs: kernel(len(pieces), *refs),
        in_specs=[vmem] * (len(pieces) + len(operands)),
        out_specs=[vmem] * len(outs),
        out_shape=outs,
        scratch_shapes=[pltpu.VMEM((rows, columns), jnp.float32) for columns in sums],
        compiler_params=pltpu.CompilerParams(vmem_limit_bytes=VMEM_LIMIT),
        cost_estimate=pl.CostEstimate(flops=0, bytes_accessed=0, transcendentals=0),
        name=name,
    )(*pieces, *operands)


def forward(pieces, gate_rows, up_rows, feature_table, tables):
    units, model = gate_rows.shape
    rows = sum(piece.shape[0] for piece in pieces)
    outs = [
        jax.ShapeDtypeStruct((rows, units), jnp.float32),
        jax.ShapeDtypeStruct((rows, units), jnp.float32),
        jax.ShapeDtypeStruct((rows, K1), jnp.bfloat16),
        jax.ShapeDtypeStruct((rows, K2), jnp.bfloat16),
    ]
    operands = (gate_rows, up_rows, feature_table, tables)
    return on_chip(forward_kernel, "forward", pieces, operands, outs, (units, units, K2))


def backward(pieces, down_rows, feature_table, tables, saved, before):
    units, model = down_rows.shape
    outs = [jax.ShapeDtypeStruct(before.shape, jnp.float32)]
    operands = (down_rows, feature_table, tables, *saved, before)
    return on_chip(backward_kernel, "backward", pieces, operands, outs, (units, K2))[0]


def on_device(
    layout,
    inputs,
    out_grad,
    example_ids,
    gate_weight,
    up_weight,
    down_weight,
    unit_buckets,
    unit_signs,
    feature_buckets,
    feature_signs,
):
    def move(value, pairs):
        return lax.ppermute(value, "fsdp", pairs)

    rows = inputs.shape[0]

    unit_tables = sign_tables(unit_buckets, unit_signs, K1)
    feature_table = sign_tables(feature_buckets, feature_signs, K2)

    example = jnp.broadcast_to(example_ids[:, None], (rows, LANES)).astype(jnp.bfloat16)
    tagged = jnp.concatenate([out_grad, example], axis=1)
    gate_rows, up_rows = gate_weight.T, up_weight.T
    total = jnp.zeros((K1, EX * K2), jnp.float32)

    if layout.inner == 2 and layout.outer > 2:
        ahead = lambda piece: move(piece, layout.outer_ring())
        aside = lambda piece: move(piece, layout.inner_ring())
        swap = lambda piece, parts=2: [
            move(part, layout.core_swap()) for part in jnp.split(piece, parts, axis=0)
        ]
        after = lax.optimization_barrier
        first_side = lambda rows_in: forward(
            rows_in, gate_rows, up_rows, feature_table, unit_tables
        )
        other_side = lambda rows_out, saved, total: backward(
            rows_out, down_weight, feature_table, unit_tables, saved, total
        )
        last = layout.outer - 1
        here_in, here_out = inputs, tagged
        coming_in = ahead(here_in), aside(here_in)
        here_out, feature_table, unit_tables = after((here_out, feature_table, unit_tables))
        coming_out = ahead(here_out), aside(here_out)
        swapped_in = swap(here_in)
        for step in range(1, last):
            next_in, across_in, total = after((*coming_in, total))
            coming_in = ahead(next_in), aside(next_in)
            swapped_across = swap(across_in)
            here_out, swapped_across = after((here_out, swapped_across))
            swapped_out = swap(here_out)
            saved = first_side([here_in, *swapped_in, across_in, *swapped_across])
            next_out, across_out, saved = after((*coming_out, saved))
            by_inner = aside(next_out) if step < last - 1 else ahead(across_out)
            coming_out = ahead(next_out), by_inner
            rows_out = [here_out, *swapped_out, across_out, *swap(across_out)]
            if step == last - 1:
                next_out, saved = after((next_out, saved))
                swapped_here, saved = after((swap(next_out), saved))
            total = other_side(rows_out, saved, total)
            here_in, total = after((next_in, total))
            here_out, swapped_in = next_out, swap(here_in)

        last_in, across_in, total = after((*coming_in, total))
        coming_in = aside(last_in)
        swapped_last, swapped_across = after((swap(last_in), swap(across_in)))
        saved = first_side([here_in, *swapped_in, last_in, *swapped_last])
        last_out, saved = after((coming_out[0], saved))
        coming_last = aside(last_out)
        rows_out = [here_out, *swapped_here, last_out, *swap(last_out)]
        total = other_side(rows_out, saved, total)
        corner_in = coming_in
        swapped_corner = swap(corner_in, 1)
        saved = first_side([across_in, *swapped_across, corner_in, *swapped_corner])
        across_out, corner_out, total, saved = after((coming_out[1], coming_last, total, saved))
        swapped_out = swap(across_out)
        rows_out = [across_out, *swapped_out, corner_out, *swap(corner_out)]
        total = other_side(rows_out, saved, total)
    else:
        gather = lambda piece: lax.all_gather(piece, "fsdp", axis=0, tiled=True)
        saved = forward([gather(inputs)], gate_rows, up_rows, feature_table, unit_tables)
        total = backward([gather(tagged)], down_weight, feature_table, unit_tables, saved, total)

    parts = total.astype(jnp.bfloat16).reshape(layout.count, -1, EX * K2)
    parts = lax.all_to_all(parts, "fsdp", 0, 0)
    part = jnp.sum(parts.astype(jnp.float32), axis=0)
    factor = (3.0 * SEQ * FF * D / (K1 * K2)) ** (-0.5)
    return (factor * part).reshape(-1, EX, K2).transpose(1, 0, 2)


def solution(mesh):
    layout = Layout(mesh.shape["fsdp"])
    in_specs = (
        P(("groups", "fsdp"), None),
        P(("groups", "fsdp"), None),
        P(("groups", "fsdp")),
        P(None, "fsdp"),
        P(None, "fsdp"),
        P("fsdp", None),
        P(None, "fsdp"),
        P(None, "fsdp"),
        P(),
        P(),
    )
    out_specs = P("groups", "fsdp", None)
    return jax.shard_map(
        lambda *args: on_device(layout, *args),
        mesh=mesh,
        in_specs=in_specs,
        out_specs=out_specs,
        check_vma=False,
    )
```

```python
import jax
import jax.numpy as jnp
from jax import lax
from jax.experimental import pallas as pl
from jax.experimental.pallas import tpu as pltpu
from jax.sharding import PartitionSpec as P

D = 5120
FF = 13824
EX = 2
SEQ = 512
K1 = 256
K2 = 256
CORES = 2
OUTER = 4
PRODUCT_ELEMENTS = 256 * 5120
LANES = 128
VMEM_LIMIT = 12 << 20


def sign_tables(buckets, sign_bits, order):
    matches = buckets[..., None, :] == order[:, None]
    signed = (2 * sign_bits - 1).astype(jnp.bfloat16)[..., None, :]
    return jnp.where(matches, signed, jnp.zeros_like(signed))


class Layout:
    def __init__(self, count):
        self.outer = OUTER if count % (OUTER * CORES) == 0 else 1
        self.inner = count // (self.outer * CORES)
        self.count = count

    def index(self, outer, inner, core):
        return ((outer % self.outer) * self.inner + inner % self.inner) * CORES + core

    def pairs(self, step):
        places = [
            (o, i, c)
            for o in range(self.outer)
            for i in range(self.inner)
            for c in range(CORES)
        ]
        return [(self.index(o, i, c), self.index(*step(o, i, c))) for o, i, c in places]

    def outer_ring(self):
        return self.pairs(lambda o, i, c: (o + 1 - 2 * c, i, c))

    def inner_ring(self):
        return self.pairs(lambda o, i, c: (o, i + 1 - 2 * c, c))

    def core_swap(self):
        return self.pairs(lambda o, i, c: (o, i, 1 - c))


def dot(left, right):
    return jnp.dot(left, right, preferred_element_type=jnp.float32)


def dot_rows(left, right):
    return lax.dot_general(
        left, right, (((1,), (1,)), ((), ())), preferred_element_type=jnp.float32
    )


def joined(refs, lanes):
    parts = [ref[:, lanes] for ref in refs]
    return jnp.concatenate(parts, axis=0) if len(parts) > 1 else parts[0]


def add_products(refs, model, sums):
    depth = model
    while sums[0][0].shape[0] * depth > PRODUCT_ELEMENTS and depth % (2 * LANES) == 0:
        depth //= 2
    for acc, _ in sums:
        acc[...] = jnp.zeros_like(acc)

    def body(step, _):
        here = pl.ds(pl.multiple_of(step * depth, depth), depth)
        rows = joined(refs, here)
        for acc, weight in sums:
            acc[...] += dot_rows(rows, weight[:, here])
        return 0

    lax.fori_loop(0, model // depth, body, 0)


def forward_kernel(pieces, *refs):
    gate_w, up_w, feature_w, tables = refs[pieces : pieces + 4]
    to_gate, to_up, down_part, feature_in = refs[pieces + 4 : pieces + 8]
    gate_acc, up_acc, feature_acc = refs[pieces + 8 :]
    sums = ((gate_acc, gate_w), (up_acc, up_w), (feature_acc, feature_w))
    add_products(refs[:pieces], gate_w.shape[1], sums)
    gate, up = gate_acc[...], up_acc[...]
    sigmoid = jax.nn.sigmoid(gate)
    activated = gate * sigmoid
    to_gate[...] = up * sigmoid * (1.0 + gate * (1.0 - sigmoid))
    to_up[...] = activated
    hidden = (activated * up).astype(jnp.bfloat16)
    down_part[...] = dot_rows(hidden, tables[2]).astype(jnp.bfloat16)
    feature_in[...] = feature_acc[...].astype(jnp.bfloat16)


def backward_kernel(pieces, *refs):
    down_w, feature_w, tables, to_gate, to_up, down_part, feature_in, before = refs[
        pieces : pieces + 8
    ]
    total, hidden_acc, feature_acc = refs[pieces + 8 :]
    model = down_w.shape[1]
    add_products(refs[:pieces], model, ((hidden_acc, down_w), (feature_acc, feature_w)))
    bf16 = jnp.bfloat16
    hidden_grad = hidden_acc[...]
    gate_grad = (hidden_grad * to_gate[...]).astype(bf16)
    up_grad = (hidden_grad * to_up[...]).astype(bf16)
    input_part = (dot_rows(gate_grad, tables[0]) + dot_rows(up_grad, tables[1])).astype(bf16)
    example = joined(refs[:pieces], pl.ds(model, LANES)).astype(jnp.float32)
    example = jnp.concatenate([example] * (K2 // LANES), axis=1)

    def by_example(features):
        features = features.astype(jnp.float32)
        return jnp.concatenate(
            [jnp.where(example == e, features, 0.0) for e in range(EX)], axis=1
        ).astype(bf16)

    feature_out = feature_acc[...].astype(bf16)
    total[...] = before[...] + lax.dot_general(
        jnp.concatenate([down_part[...], input_part], axis=0),
        jnp.concatenate([by_example(feature_out), by_example(feature_in[...])], axis=0),
        (((0,), (0,)), ((), ())),
        preferred_element_type=jnp.float32,
    )


def on_chip(kernel, name, pieces, operands, outs, sums):
    rows = sum(piece.shape[0] for piece in pieces)
    vmem = pl.BlockSpec(memory_space=pltpu.VMEM)
    return pl.pallas_call(
        lambda *refs: kernel(len(pieces), *refs),
        in_specs=[vmem] * (len(pieces) + len(operands)),
        out_specs=[vmem] * len(outs),
        out_shape=outs,
        scratch_shapes=[pltpu.VMEM((rows, columns), jnp.float32) for columns in sums],
        compiler_params=pltpu.CompilerParams(vmem_limit_bytes=VMEM_LIMIT),
        cost_estimate=pl.CostEstimate(flops=0, bytes_accessed=0, transcendentals=0),
        name=name,
    )(*pieces, *operands)


def forward(pieces, gate_rows, up_rows, feature_table, tables):
    units, model = gate_rows.shape
    rows = sum(piece.shape[0] for piece in pieces)
    outs = [
        jax.ShapeDtypeStruct((rows, units), jnp.float32),
        jax.ShapeDtypeStruct((rows, units), jnp.float32),
        jax.ShapeDtypeStruct((rows, K1), jnp.bfloat16),
        jax.ShapeDtypeStruct((rows, K2), jnp.bfloat16),
    ]
    operands = (gate_rows, up_rows, feature_table, tables)
    return on_chip(forward_kernel, "forward", pieces, operands, outs, (units, units, K2))


def backward(pieces, down_rows, feature_table, tables, saved, before):
    units, model = down_rows.shape
    outs = [jax.ShapeDtypeStruct(before.shape, jnp.float32)]
    operands = (down_rows, feature_table, tables, *saved, before)
    return on_chip(backward_kernel, "backward", pieces, operands, outs, (units, K2))[0]


def scatter_sum(parts, groups):
    sent = lax.all_to_all(parts.astype(jnp.bfloat16), "fsdp", 0, 0, axis_index_groups=groups)
    return jnp.sum(sent.astype(jnp.float32), axis=0)


def on_device(
    layout,
    inputs,
    out_grad,
    example_ids,
    gate_weight,
    up_weight,
    down_weight,
    unit_buckets,
    unit_signs,
    feature_buckets,
    feature_signs,
):
    def move(value, pairs):
        return lax.ppermute(value, "fsdp", pairs)

    rows = inputs.shape[0]

    around = layout.inner * CORES
    order = jnp.arange(K1, dtype=jnp.int32).reshape(layout.outer, around, -1)
    unit_tables = sign_tables(unit_buckets, unit_signs, order.swapaxes(0, 1).reshape(-1))
    feature_table = sign_tables(feature_buckets, feature_signs, jnp.arange(K2, dtype=jnp.int32))

    example = jnp.broadcast_to(example_ids[:, None], (rows, LANES)).astype(jnp.bfloat16)
    tagged = jnp.concatenate([out_grad, example], axis=1)
    gate_rows, up_rows = gate_weight.T, up_weight.T
    total = jnp.zeros((K1, EX * K2), jnp.float32)

    if layout.inner == 2 and layout.outer > 2:
        ahead = lambda piece: move(piece, layout.outer_ring())
        aside = lambda piece: move(piece, layout.inner_ring())
        swap = lambda piece, parts=2: [
            move(part, layout.core_swap()) for part in jnp.split(piece, parts, axis=0)
        ]
        after = lax.optimization_barrier
        first_side = lambda rows_in: forward(
            rows_in, gate_rows, up_rows, feature_table, unit_tables
        )
        other_side = lambda rows_out, saved, total: backward(
            rows_out, down_weight, feature_table, unit_tables, saved, total
        )
        last = layout.outer - 1
        here_in, here_out = inputs, tagged
        coming_in = ahead(here_in), aside(here_in)
        here_out, feature_table, unit_tables = after((here_out, feature_table, unit_tables))
        coming_out = ahead(here_out), aside(here_out)
        swapped_in = swap(here_in)
        for step in range(1, last):
            next_in, across_in, total = after((*coming_in, total))
            coming_in = ahead(next_in), aside(next_in)
            swapped_across = swap(across_in)
            here_out, swapped_across = after((here_out, swapped_across))
            swapped_out = swap(here_out)
            saved = first_side([here_in, *swapped_in, across_in, *swapped_across])
            next_out, across_out, saved = after((*coming_out, saved))
            by_inner = aside(next_out) if step < last - 1 else ahead(across_out)
            coming_out = ahead(next_out), by_inner
            rows_out = [here_out, *swapped_out, across_out, *swap(across_out)]
            if step == last - 1:
                next_out, saved = after((next_out, saved))
                swapped_here, saved = after((swap(next_out), saved))
            total = other_side(rows_out, saved, total)
            here_in, total = after((next_in, total))
            here_out, swapped_in = next_out, swap(here_in)

        last_in, across_in, total = after((*coming_in, total))
        coming_in = aside(last_in)
        swapped_last, swapped_across = after((swap(last_in), swap(across_in)))
        saved = first_side([here_in, *swapped_in, last_in, *swapped_last])
        last_out, saved = after((coming_out[0], saved))
        coming_last = aside(last_out)
        rows_out = [here_out, *swapped_here, last_out, *swap(last_out)]
        total = other_side(rows_out, saved, total)
        corner_in = coming_in
        swapped_corner = swap(corner_in, 1)
        saved = first_side([across_in, *swapped_across, corner_in, *swapped_corner])
        across_out, corner_out, total, saved = after((coming_out[1], coming_last, total, saved))
        swapped_out = swap(across_out, 1)
        rows_out = [across_out, *swapped_out, corner_out, *swap(corner_out, 1)]
        total = other_side(rows_out, saved, total)
    else:
        gather = lambda piece: lax.all_gather(piece, "fsdp", axis=0, tiled=True)
        saved = forward([gather(inputs)], gate_rows, up_rows, feature_table, unit_tables)
        total = backward([gather(tagged)], down_weight, feature_table, unit_tables, saved, total)

    places = [[o * around + a for a in range(around)] for o in range(layout.outer)]
    parts = total.reshape(around, layout.outer, -1, EX * K2)
    part = scatter_sum(parts, places)
    part = scatter_sum(part, [list(group) for group in zip(*places)])
    factor = (3.0 * SEQ * FF * D / (K1 * K2)) ** (-0.5)
    return (factor * part).reshape(-1, EX, K2).transpose(1, 0, 2)


def solution(mesh):
    layout = Layout(mesh.shape["fsdp"])
    in_specs = (
        P(("groups", "fsdp"), None),
        P(("groups", "fsdp"), None),
        P(("groups", "fsdp")),
        P(None, "fsdp"),
        P(None, "fsdp"),
        P("fsdp", None),
        P(None, "fsdp"),
        P(None, "fsdp"),
        P(),
        P(),
    )
    out_specs = P("groups", "fsdp", None)
    return jax.shard_map(
        lambda *args: on_device(layout, *args),
        mesh=mesh,
        in_specs=in_specs,
        out_specs=out_specs,
        check_vma=False,
    )
```

```python
import jax
import jax.numpy as jnp
from jax import lax
from jax.experimental import pallas as pl
from jax.experimental.pallas import tpu as pltpu
from jax.sharding import PartitionSpec as P

D = 5120
FF = 13824
EX = 2
SEQ = 512
K1 = 256
K2 = 256
CORES = 2
OUTER = 4
PRODUCT_ELEMENTS = 256 * 5120
LANES = 128
VMEM_LIMIT = 12 << 20


def sign_tables(buckets, sign_bits, buckets_count):
    matches = buckets[..., None, :] == jnp.arange(buckets_count, dtype=jnp.int32)[:, None]
    signed = (2 * sign_bits - 1).astype(jnp.bfloat16)[..., None, :]
    return jnp.where(matches, signed, jnp.zeros_like(signed))


class Layout:
    def __init__(self, count):
        self.outer = OUTER if count % (OUTER * CORES) == 0 else 1
        self.inner = count // (self.outer * CORES)
        self.count = count

    def index(self, outer, inner, core):
        return ((outer % self.outer) * self.inner + inner % self.inner) * CORES + core

    def pairs(self, step):
        places = [
            (o, i, c)
            for o in range(self.outer)
            for i in range(self.inner)
            for c in range(CORES)
        ]
        return [(self.index(o, i, c), self.index(*step(o, i, c))) for o, i, c in places]

    def outer_ring(self):
        return self.pairs(lambda o, i, c: (o + 1 - 2 * c, i, c))

    def inner_ring(self):
        return self.pairs(lambda o, i, c: (o, i + 1 - 2 * c, c))

    def core_swap(self):
        return self.pairs(lambda o, i, c: (o, i, 1 - c))


def dot(left, right):
    return jnp.dot(left, right, preferred_element_type=jnp.float32)


def dot_rows(left, right):
    return lax.dot_general(
        left, right, (((1,), (1,)), ((), ())), preferred_element_type=jnp.float32
    )


def joined(refs, lanes):
    parts = [ref[:, lanes] for ref in refs]
    return jnp.concatenate(parts, axis=0) if len(parts) > 1 else parts[0]


def add_products(refs, model, sums):
    depth = model
    while sums[0][0].shape[0] * depth > PRODUCT_ELEMENTS and depth % (2 * LANES) == 0:
        depth //= 2
    for acc, _ in sums:
        acc[...] = jnp.zeros_like(acc)

    def body(step, _):
        here = pl.ds(pl.multiple_of(step * depth, depth), depth)
        rows = joined(refs, here)
        for acc, weight in sums:
            acc[...] += dot_rows(rows, weight[:, here])
        return 0

    lax.fori_loop(0, model // depth, body, 0)


def forward_kernel(pieces, *refs):
    gate_w, up_w, feature_w, tables = refs[pieces : pieces + 4]
    to_gate, to_up, down_part, feature_in = refs[pieces + 4 : pieces + 8]
    gate_acc, up_acc, feature_acc = refs[pieces + 8 :]
    sums = ((gate_acc, gate_w), (up_acc, up_w), (feature_acc, feature_w))
    add_products(refs[:pieces], gate_w.shape[1], sums)
    gate, up = gate_acc[...], up_acc[...]
    sigmoid = jax.nn.sigmoid(gate)
    activated = gate * sigmoid
    to_gate[...] = up * sigmoid * (1.0 + gate * (1.0 - sigmoid))
    to_up[...] = activated
    hidden = (activated * up).astype(jnp.bfloat16)
    down_part[...] = dot_rows(hidden, tables[2]).astype(jnp.bfloat16)
    feature_in[...] = feature_acc[...].astype(jnp.bfloat16)


def backward_kernel(pieces, *refs):
    down_w, feature_w, tables, to_gate, to_up, down_part, feature_in, before = refs[
        pieces : pieces + 8
    ]
    total, hidden_acc, feature_acc = refs[pieces + 8 :]
    model = down_w.shape[1]
    add_products(refs[:pieces], model, ((hidden_acc, down_w), (feature_acc, feature_w)))
    bf16 = jnp.bfloat16
    hidden_grad = hidden_acc[...]
    gate_grad = (hidden_grad * to_gate[...]).astype(bf16)
    up_grad = (hidden_grad * to_up[...]).astype(bf16)
    input_part = (dot_rows(gate_grad, tables[0]) + dot_rows(up_grad, tables[1])).astype(bf16)
    example = joined(refs[:pieces], pl.ds(model, LANES)).astype(jnp.float32)
    example = jnp.concatenate([example] * (K2 // LANES), axis=1)

    def by_example(features):
        features = features.astype(jnp.float32)
        return jnp.concatenate(
            [jnp.where(example == e, features, 0.0) for e in range(EX)], axis=1
        ).astype(bf16)

    feature_out = feature_acc[...].astype(bf16)
    total[...] = before[...] + lax.dot_general(
        jnp.concatenate([down_part[...], input_part], axis=0),
        jnp.concatenate([by_example(feature_out), by_example(feature_in[...])], axis=0),
        (((0,), (0,)), ((), ())),
        preferred_element_type=jnp.float32,
    )


def on_chip(kernel, name, pieces, operands, outs, sums):
    rows = sum(piece.shape[0] for piece in pieces)
    vmem = pl.BlockSpec(memory_space=pltpu.VMEM)
    return pl.pallas_call(
        lambda *refs: kernel(len(pieces), *refs),
        in_specs=[vmem] * (len(pieces) + len(operands)),
        out_specs=[vmem] * len(outs),
        out_shape=outs,
        scratch_shapes=[pltpu.VMEM((rows, columns), jnp.float32) for columns in sums],
        compiler_params=pltpu.CompilerParams(vmem_limit_bytes=VMEM_LIMIT),
        cost_estimate=pl.CostEstimate(flops=0, bytes_accessed=0, transcendentals=0),
        name=name,
    )(*pieces, *operands)


def forward(pieces, gate_rows, up_rows, feature_table, tables):
    units, model = gate_rows.shape
    rows = sum(piece.shape[0] for piece in pieces)
    outs = [
        jax.ShapeDtypeStruct((rows, units), jnp.float32),
        jax.ShapeDtypeStruct((rows, units), jnp.float32),
        jax.ShapeDtypeStruct((rows, K1), jnp.bfloat16),
        jax.ShapeDtypeStruct((rows, K2), jnp.bfloat16),
    ]
    operands = (gate_rows, up_rows, feature_table, tables)
    return on_chip(forward_kernel, "forward", pieces, operands, outs, (units, units, K2))


def backward(pieces, down_rows, feature_table, tables, saved, before):
    units, model = down_rows.shape
    outs = [jax.ShapeDtypeStruct(before.shape, jnp.float32)]
    operands = (down_rows, feature_table, tables, *saved, before)
    return on_chip(backward_kernel, "backward", pieces, operands, outs, (units, K2))[0]


def on_device(
    layout,
    inputs,
    out_grad,
    example_ids,
    gate_weight,
    up_weight,
    down_weight,
    unit_buckets,
    unit_signs,
    feature_buckets,
    feature_signs,
):
    def move(value, pairs):
        return lax.ppermute(value, "fsdp", pairs)

    rows = inputs.shape[0]

    unit_tables = sign_tables(unit_buckets, unit_signs, K1)
    feature_table = sign_tables(feature_buckets, feature_signs, K2)

    example = jnp.broadcast_to(example_ids[:, None], (rows, LANES)).astype(jnp.bfloat16)
    tagged = jnp.concatenate([out_grad, example], axis=1)
    gate_rows, up_rows = gate_weight.T, up_weight.T
    total = jnp.zeros((K1, EX * K2), jnp.float32)

    if layout.inner == 2 and layout.outer > 2:
        ahead = lambda piece: move(piece, layout.outer_ring())
        aside = lambda piece: move(piece, layout.inner_ring())
        swap = lambda piece, parts=2: [
            move(part, layout.core_swap()) for part in jnp.split(piece, parts, axis=0)
        ]
        after = lax.optimization_barrier
        first_side = lambda rows_in: forward(
            rows_in, gate_rows, up_rows, feature_table, unit_tables
        )
        other_side = lambda rows_out, saved, total: backward(
            rows_out, down_weight, feature_table, unit_tables, saved, total
        )
        last = layout.outer - 1
        here_in, here_out = inputs, tagged
        coming_in = ahead(here_in), aside(here_in)
        here_out, feature_table, unit_tables = after((here_out, feature_table, unit_tables))
        coming_out = ahead(here_out), aside(here_out)
        swapped_in = swap(here_in)
        for step in range(1, last):
            next_in, across_in, total = after((*coming_in, total))
            coming_in = ahead(next_in), aside(next_in)
            swapped_across = swap(across_in)
            here_out, swapped_across = after((here_out, swapped_across))
            swapped_out = swap(here_out)
            saved = first_side([here_in, *swapped_in, across_in, *swapped_across])
            next_out, across_out, saved = after((*coming_out, saved))
            by_inner = aside(next_out) if step < last - 1 else ahead(across_out)
            coming_out = ahead(next_out), by_inner
            rows_out = [here_out, *swapped_out, across_out, *swap(across_out)]
            if step == last - 1:
                next_out, saved = after((next_out, saved))
                swapped_here, saved = after((swap(next_out), saved))
            total = other_side(rows_out, saved, total)
            here_in, total = after((next_in, total))
            here_out, swapped_in = next_out, swap(here_in)

        last_in, across_in, total = after((*coming_in, total))
        coming_in = aside(last_in)
        swapped_last, swapped_across = after((swap(last_in), swap(across_in)))
        saved = first_side([here_in, *swapped_in, last_in, *swapped_last])
        last_out, saved = after((coming_out[0], saved))
        coming_last = aside(last_out)
        rows_out = [here_out, *swapped_here, last_out, *swap(last_out)]
        total = other_side(rows_out, saved, total)
        corner_in = coming_in
        swapped_corner = swap(corner_in, 1)
        saved = first_side([across_in, *swapped_across, corner_in, *swapped_corner])
        across_out, corner_out, total, saved = after((coming_out[1], coming_last, total, saved))
        swapped_out = swap(across_out, 1)
        rows_out = [across_out, *swapped_out, corner_out, *swap(corner_out, 1)]
        total = other_side(rows_out, saved, total)
    else:
        gather = lambda piece: lax.all_gather(piece, "fsdp", axis=0, tiled=True)
        saved = forward([gather(inputs)], gate_rows, up_rows, feature_table, unit_tables)
        total = backward([gather(tagged)], down_weight, feature_table, unit_tables, saved, total)

    parts = total.astype(jnp.bfloat16).reshape(layout.count, -1, EX * K2)
    parts = lax.all_to_all(parts, "fsdp", 0, 0)
    part = jnp.sum(parts.astype(jnp.float32), axis=0)
    factor = (3.0 * SEQ * FF * D / (K1 * K2)) ** (-0.5)
    return (factor * part).reshape(-1, EX, K2).transpose(1, 0, 2)


def solution(mesh):
    layout = Layout(mesh.shape["fsdp"])
    in_specs = (
        P(("groups", "fsdp"), None),
        P(("groups", "fsdp"), None),
        P(("groups", "fsdp")),
        P(None, "fsdp"),
        P(None, "fsdp"),
        P("fsdp", None),
        P(None, "fsdp"),
        P(None, "fsdp"),
        P(),
        P(),
    )
    out_specs = P("groups", "fsdp", None)
    return jax.shard_map(
        lambda *args: on_device(layout, *args),
        mesh=mesh,
        in_specs=in_specs,
        out_specs=out_specs,
        check_vma=False,
    )
```

```python
import jax
import jax.numpy as jnp
from jax import lax
from jax.experimental import pallas as pl
from jax.experimental.pallas import tpu as pltpu
from jax.sharding import PartitionSpec as P

D = 5120
FF = 13824
EX = 2
SEQ = 512
K1 = 256
K2 = 256
CORES = 2
OUTER = 4
PRODUCT_ELEMENTS = 256 * 5120
LANES = 128
VMEM_LIMIT = 12 << 20


def sign_tables(buckets, sign_bits, buckets_count):
    matches = buckets[..., None, :] == jnp.arange(buckets_count, dtype=jnp.int32)[:, None]
    signed = (2 * sign_bits - 1).astype(jnp.bfloat16)[..., None, :]
    return jnp.where(matches, signed, jnp.zeros_like(signed))


class Layout:
    def __init__(self, count):
        self.outer = OUTER if count % (OUTER * CORES) == 0 else 1
        self.inner = count // (self.outer * CORES)
        self.count = count

    def index(self, outer, inner, core):
        return ((outer % self.outer) * self.inner + inner % self.inner) * CORES + core

    def pairs(self, step):
        places = [
            (o, i, c)
            for o in range(self.outer)
            for i in range(self.inner)
            for c in range(CORES)
        ]
        return [(self.index(o, i, c), self.index(*step(o, i, c))) for o, i, c in places]

    def outer_ring(self):
        return self.pairs(lambda o, i, c: (o + 1 - 2 * c, i, c))

    def inner_ring(self):
        return self.pairs(lambda o, i, c: (o, i + 1 - 2 * c, c))

    def core_swap(self):
        return self.pairs(lambda o, i, c: (o, i, 1 - c))


def dot(left, right):
    return jnp.dot(left, right, preferred_element_type=jnp.float32)


def dot_rows(left, right):
    return lax.dot_general(
        left, right, (((1,), (1,)), ((), ())), preferred_element_type=jnp.float32
    )


def joined(refs, lanes):
    parts = [ref[:, lanes] for ref in refs]
    return jnp.concatenate(parts, axis=0) if len(parts) > 1 else parts[0]


def add_products(refs, model, sums):
    depth = model
    while sums[0][0].shape[0] * depth > PRODUCT_ELEMENTS and depth % (2 * LANES) == 0:
        depth //= 2
    for acc, _ in sums:
        acc[...] = jnp.zeros_like(acc)

    def body(step, _):
        here = pl.ds(pl.multiple_of(step * depth, depth), depth)
        rows = joined(refs, here)
        for acc, weight in sums:
            acc[...] += dot_rows(rows, weight[:, here])
        return 0

    lax.fori_loop(0, model // depth, body, 0)


def forward_kernel(pieces, *refs):
    gate_w, up_w, feature_w, tables = refs[pieces : pieces + 4]
    to_gate, to_up, down_part, feature_in = refs[pieces + 4 : pieces + 8]
    gate_acc, up_acc, feature_acc = refs[pieces + 8 :]
    sums = ((gate_acc, gate_w), (up_acc, up_w), (feature_acc, feature_w))
    add_products(refs[:pieces], gate_w.shape[1], sums)
    gate, up = gate_acc[...], up_acc[...]
    sigmoid = jax.nn.sigmoid(gate)
    activated = gate * sigmoid
    to_gate[...] = up * sigmoid * (1.0 + gate * (1.0 - sigmoid))
    to_up[...] = activated
    hidden = (activated * up).astype(jnp.bfloat16)
    down_part[...] = dot_rows(hidden, tables[2]).astype(jnp.bfloat16)
    feature_in[...] = feature_acc[...].astype(jnp.bfloat16)


def backward_kernel(pieces, *refs):
    down_w, feature_w, tables, to_gate, to_up, down_part, feature_in, before = refs[
        pieces : pieces + 8
    ]
    total, hidden_acc, feature_acc = refs[pieces + 8 :]
    model = down_w.shape[1]
    add_products(refs[:pieces], model, ((hidden_acc, down_w), (feature_acc, feature_w)))
    bf16 = jnp.bfloat16
    hidden_grad = hidden_acc[...]
    gate_grad = (hidden_grad * to_gate[...]).astype(bf16)
    up_grad = (hidden_grad * to_up[...]).astype(bf16)
    input_part = (dot_rows(gate_grad, tables[0]) + dot_rows(up_grad, tables[1])).astype(bf16)
    example = joined(refs[:pieces], pl.ds(model, LANES)).astype(jnp.float32)
    example = jnp.concatenate([example] * (K2 // LANES), axis=1)

    def by_example(features):
        features = features.astype(jnp.float32)
        return jnp.concatenate(
            [jnp.where(example == e, features, 0.0) for e in range(EX)], axis=1
        ).astype(bf16)

    feature_out = feature_acc[...].astype(bf16)
    total[...] = before[...] + lax.dot_general(
        jnp.concatenate([down_part[...], input_part], axis=0),
        jnp.concatenate([by_example(feature_out), by_example(feature_in[...])], axis=0),
        (((0,), (0,)), ((), ())),
        preferred_element_type=jnp.float32,
    )


def on_chip(kernel, name, pieces, operands, outs, sums):
    rows = sum(piece.shape[0] for piece in pieces)
    vmem = pl.BlockSpec(memory_space=pltpu.VMEM)
    return pl.pallas_call(
        lambda *refs: kernel(len(pieces), *refs),
        in_specs=[vmem] * (len(pieces) + len(operands)),
        out_specs=[vmem] * len(outs),
        out_shape=outs,
        scratch_shapes=[pltpu.VMEM((rows, columns), jnp.float32) for columns in sums],
        compiler_params=pltpu.CompilerParams(vmem_limit_bytes=VMEM_LIMIT),
        cost_estimate=pl.CostEstimate(flops=0, bytes_accessed=0, transcendentals=0),
        name=name,
    )(*pieces, *operands)


def forward(pieces, gate_rows, up_rows, feature_table, tables):
    units, model = gate_rows.shape
    rows = sum(piece.shape[0] for piece in pieces)
    outs = [
        jax.ShapeDtypeStruct((rows, units), jnp.float32),
        jax.ShapeDtypeStruct((rows, units), jnp.float32),
        jax.ShapeDtypeStruct((rows, K1), jnp.bfloat16),
        jax.ShapeDtypeStruct((rows, K2), jnp.bfloat16),
    ]
    operands = (gate_rows, up_rows, feature_table, tables)
    return on_chip(forward_kernel, "forward", pieces, operands, outs, (units, units, K2))


def backward(pieces, down_rows, feature_table, tables, saved, before):
    units, model = down_rows.shape
    outs = [jax.ShapeDtypeStruct(before.shape, jnp.float32)]
    operands = (down_rows, feature_table, tables, *saved, before)
    return on_chip(backward_kernel, "backward", pieces, operands, outs, (units, K2))[0]


def on_device(
    layout,
    inputs,
    out_grad,
    example_ids,
    gate_weight,
    up_weight,
    down_weight,
    unit_buckets,
    unit_signs,
    feature_buckets,
    feature_signs,
):
    def move(value, pairs):
        return lax.ppermute(value, "fsdp", pairs)

    rows = inputs.shape[0]

    unit_tables = sign_tables(unit_buckets, unit_signs, K1)
    feature_table = sign_tables(feature_buckets, feature_signs, K2)

    example = jnp.broadcast_to(example_ids[:, None], (rows, LANES)).astype(jnp.bfloat16)
    tagged = jnp.concatenate([out_grad, example], axis=1)
    gate_rows, up_rows = gate_weight.T, up_weight.T
    total = jnp.zeros((K1, EX * K2), jnp.float32)

    if layout.inner == 2 and layout.outer > 2:
        ahead = lambda piece: move(piece, layout.outer_ring())
        aside = lambda piece: move(piece, layout.inner_ring())
        swap = lambda piece, parts=2: [
            move(part, layout.core_swap()) for part in jnp.split(piece, parts, axis=0)
        ]
        after = lax.optimization_barrier
        first_side = lambda rows_in: forward(
            rows_in, gate_rows, up_rows, feature_table, unit_tables
        )
        other_side = lambda rows_out, saved, total: backward(
            rows_out, down_weight, feature_table, unit_tables, saved, total
        )
        last = layout.outer - 1
        here_in, here_out = inputs, tagged
        coming_in = ahead(here_in), aside(here_in)
        here_out, feature_table, unit_tables = after((here_out, feature_table, unit_tables))
        coming_out = ahead(here_out), aside(here_out)
        swapped_in = swap(here_in)
        for step in range(1, last):
            next_in, across_in, total = after((*coming_in, total))
            coming_in = ahead(next_in), aside(next_in)
            swapped_across = swap(across_in)
            here_out, swapped_across = after((here_out, swapped_across))
            swapped_out = swap(here_out)
            saved = first_side([here_in, *swapped_in, across_in, *swapped_across])
            next_out, across_out, saved = after((*coming_out, saved))
            coming_out = ahead(next_out), (aside(next_out) if step < last - 1 else across_out)
            rows_out = [here_out, *swapped_out, across_out, *swap(across_out)]
            if step == last - 1:
                next_out, saved = after((next_out, saved))
                swapped_here, saved = after((swap(next_out), saved))
            total = other_side(rows_out, saved, total)
            here_in, total = after((next_in, total))
            here_out, swapped_in = next_out, swap(here_in)

        last_in, across_in, total = after((*coming_in, total))
        coming_in = aside(last_in)
        over_inner, swapped_in, swapped_last, swapped_across = after(
            (coming_out[1], swapped_in, swap(last_in), swap(across_in))
        )
        coming_across = ahead(over_inner)
        saved = first_side([here_in, *swapped_in, last_in, *swapped_last])
        last_out, saved = after((coming_out[0], saved))
        coming_last = aside(last_out)
        rows_out = [here_out, *swapped_here, last_out, *swap(last_out)]
        total = other_side(rows_out, saved, total)
        corner_in = coming_in
        swapped_corner = swap(corner_in, 1)
        saved = first_side([across_in, *swapped_across, corner_in, *swapped_corner])
        across_out, corner_out, total, saved = after((coming_across, coming_last, total, saved))
        swapped_out = swap(across_out, 1)
        rows_out = [across_out, *swapped_out, corner_out, *swap(corner_out, 1)]
        total = other_side(rows_out, saved, total)
    else:
        gather = lambda piece: lax.all_gather(piece, "fsdp", axis=0, tiled=True)
        saved = forward([gather(inputs)], gate_rows, up_rows, feature_table, unit_tables)
        total = backward([gather(tagged)], down_weight, feature_table, unit_tables, saved, total)

    parts = total.astype(jnp.bfloat16).reshape(layout.count, -1, EX * K2)
    parts = lax.all_to_all(parts, "fsdp", 0, 0)
    part = jnp.sum(parts.astype(jnp.float32), axis=0)
    factor = (3.0 * SEQ * FF * D / (K1 * K2)) ** (-0.5)
    return (factor * part).reshape(-1, EX, K2).transpose(1, 0, 2)


def solution(mesh):
    layout = Layout(mesh.shape["fsdp"])
    in_specs = (
        P(("groups", "fsdp"), None),
        P(("groups", "fsdp"), None),
        P(("groups", "fsdp")),
        P(None, "fsdp"),
        P(None, "fsdp"),
        P("fsdp", None),
        P(None, "fsdp"),
        P(None, "fsdp"),
        P(),
        P(),
    )
    out_specs = P("groups", "fsdp", None)
    return jax.shard_map(
        lambda *args: on_device(layout, *args),
        mesh=mesh,
        in_specs=in_specs,
        out_specs=out_specs,
        check_vma=False,
    )
```

```python
import jax
import jax.numpy as jnp
from jax import lax
from jax.experimental import pallas as pl
from jax.experimental.pallas import tpu as pltpu
from jax.sharding import PartitionSpec as P

D = 5120
FF = 13824
EX = 2
SEQ = 512
K1 = 256
K2 = 256
CORES = 2
OUTER = 4
TILE = 256
LANES = 128
VMEM_LIMIT = 12 << 20


def sign_tables(buckets, sign_bits, buckets_count):
    matches = buckets[..., None, :] == jnp.arange(buckets_count, dtype=jnp.int32)[:, None]
    signed = (2 * sign_bits - 1).astype(jnp.bfloat16)[..., None, :]
    return jnp.where(matches, signed, jnp.zeros_like(signed))


class Layout:
    def __init__(self, count):
        self.outer = OUTER if count % (OUTER * CORES) == 0 else 1
        self.inner = count // (self.outer * CORES)
        self.count = count

    def index(self, outer, inner, core):
        return ((outer % self.outer) * self.inner + inner % self.inner) * CORES + core

    def pairs(self, step):
        places = [
            (o, i, c)
            for o in range(self.outer)
            for i in range(self.inner)
            for c in range(CORES)
        ]
        return [(self.index(o, i, c), self.index(*step(o, i, c))) for o, i, c in places]

    def outer_ring(self):
        return self.pairs(lambda o, i, c: (o + 1 - 2 * c, i, c))

    def inner_ring(self):
        return self.pairs(lambda o, i, c: (o, i + 1 - 2 * c, c))

    def core_swap(self):
        return self.pairs(lambda o, i, c: (o, i, 1 - c))


def dot(left, right):
    return jnp.dot(left, right, preferred_element_type=jnp.float32)


def dot_rows(left, right):
    return lax.dot_general(
        left, right, (((1,), (1,)), ((), ())), preferred_element_type=jnp.float32
    )


def products(refs, rows, model, outs):
    if rows is None:
        rows = refs[0]
    else:
        own = 0
        for ref in refs:
            rows[pl.ds(own, ref.shape[0]), :] = ref[:, :model]
            own += ref.shape[0]
    for out, weight in outs:
        units = weight.shape[0]
        tiles = units // TILE

        def body(tile, _, out=out, weight=weight):
            here = pl.ds(pl.multiple_of(tile * TILE, TILE), TILE)
            out[:, here] = dot_rows(rows[:, :model], weight[here, :])
            return 0

        lax.fori_loop(0, tiles, body, 0)
        if units % TILE:
            here = slice(tiles * TILE, units)
            out[:, here] = dot_rows(rows[:, :model], weight[here, :])


def forward_kernel(pieces, *refs):
    gate_w, up_w, feature_w, tables = refs[pieces : pieces + 4]
    to_gate, to_up, down_part, feature_in = refs[pieces + 4 : pieces + 8]
    gate_acc, up_acc, feature_acc, *rows = refs[pieces + 8 :]
    outs = ((gate_acc, gate_w), (up_acc, up_w), (feature_acc, feature_w))
    products(refs[:pieces], *(rows or [None]), gate_w.shape[1], outs)
    gate, up = gate_acc[...], up_acc[...]
    sigmoid = jax.nn.sigmoid(gate)
    activated = gate * sigmoid
    to_gate[...] = up * sigmoid * (1.0 + gate * (1.0 - sigmoid))
    to_up[...] = activated
    hidden = (activated * up).astype(jnp.bfloat16)
    down_part[...] = dot_rows(hidden, tables[2]).astype(jnp.bfloat16)
    feature_in[...] = feature_acc[...].astype(jnp.bfloat16)


def backward_kernel(pieces, *refs):
    down_w, feature_w, tables, to_gate, to_up, down_part, feature_in, before = refs[
        pieces : pieces + 8
    ]
    total, hidden_acc, feature_acc, *rows = refs[pieces + 8 :]
    model = down_w.shape[1]
    outs = ((hidden_acc, down_w), (feature_acc, feature_w))
    products(refs[:pieces], *(rows or [None]), model, outs)
    bf16 = jnp.bfloat16
    hidden_grad = hidden_acc[...]
    gate_grad = (hidden_grad * to_gate[...]).astype(bf16)
    up_grad = (hidden_grad * to_up[...]).astype(bf16)
    input_part = (dot_rows(gate_grad, tables[0]) + dot_rows(up_grad, tables[1])).astype(bf16)
    example = [ref[:, model:].astype(jnp.float32) for ref in refs[:pieces]]
    example = jnp.concatenate(example, axis=0) if pieces > 1 else example[0]
    example = jnp.concatenate([example] * (K2 // LANES), axis=1)

    def by_example(features):
        features = features.astype(jnp.float32)
        return jnp.concatenate(
            [jnp.where(example == e, features, 0.0) for e in range(EX)], axis=1
        ).astype(bf16)

    feature_out = feature_acc[...].astype(bf16)
    total[...] = before[...] + lax.dot_general(
        jnp.concatenate([down_part[...], input_part], axis=0),
        jnp.concatenate([by_example(feature_out), by_example(feature_in[...])], axis=0),
        (((0,), (0,)), ((), ())),
        preferred_element_type=jnp.float32,
    )


def on_chip(kernel, name, pieces, operands, outs, sums, model):
    rows = sum(piece.shape[0] for piece in pieces)
    vmem = pl.BlockSpec(memory_space=pltpu.VMEM)
    return pl.pallas_call(
        lambda *refs: kernel(len(pieces), *refs),
        in_specs=[vmem] * (len(pieces) + len(operands)),
        out_specs=[vmem] * len(outs),
        out_shape=outs,
        scratch_shapes=[pltpu.VMEM((rows, columns), jnp.float32) for columns in sums]
        + [pltpu.VMEM((rows, model), jnp.bfloat16)] * (len(pieces) > 1),
        compiler_params=pltpu.CompilerParams(vmem_limit_bytes=VMEM_LIMIT),
        cost_estimate=pl.CostEstimate(flops=0, bytes_accessed=0, transcendentals=0),
        name=name,
    )(*pieces, *operands)


def forward(pieces, gate_rows, up_rows, feature_table, tables):
    units, model = gate_rows.shape
    rows = sum(piece.shape[0] for piece in pieces)
    outs = [
        jax.ShapeDtypeStruct((rows, units), jnp.float32),
        jax.ShapeDtypeStruct((rows, units), jnp.float32),
        jax.ShapeDtypeStruct((rows, K1), jnp.bfloat16),
        jax.ShapeDtypeStruct((rows, K2), jnp.bfloat16),
    ]
    operands = (gate_rows, up_rows, feature_table, tables)
    return on_chip(forward_kernel, "forward", pieces, operands, outs, (units, units, K2), model)


def backward(pieces, down_rows, feature_table, tables, saved, before):
    units, model = down_rows.shape
    outs = [jax.ShapeDtypeStruct(before.shape, jnp.float32)]
    operands = (down_rows, feature_table, tables, *saved, before)
    return on_chip(backward_kernel, "backward", pieces, operands, outs, (units, K2), model)[0]


def on_device(
    layout,
    inputs,
    out_grad,
    example_ids,
    gate_weight,
    up_weight,
    down_weight,
    unit_buckets,
    unit_signs,
    feature_buckets,
    feature_signs,
):
    def move(value, pairs):
        return lax.ppermute(value, "fsdp", pairs)

    rows = inputs.shape[0]

    unit_tables = sign_tables(unit_buckets, unit_signs, K1)
    feature_table = sign_tables(feature_buckets, feature_signs, K2)

    example = jnp.broadcast_to(example_ids[:, None], (rows, LANES)).astype(jnp.bfloat16)
    tagged = jnp.concatenate([out_grad, example], axis=1)
    gate_rows, up_rows = gate_weight.T, up_weight.T
    total = jnp.zeros((K1, EX * K2), jnp.float32)

    if layout.inner == 2 and layout.outer > 2:
        ahead = lambda piece: move(piece, layout.outer_ring())
        aside = lambda piece: move(piece, layout.inner_ring())
        swap = lambda piece, parts=2: [
            move(part, layout.core_swap()) for part in jnp.split(piece, parts, axis=0)
        ]
        after = lax.optimization_barrier
        first_side = lambda rows_in: forward(
            rows_in, gate_rows, up_rows, feature_table, unit_tables
        )
        other_side = lambda rows_out, saved, total: backward(
            rows_out, down_weight, feature_table, unit_tables, saved, total
        )
        last = layout.outer - 1
        here_in, here_out = inputs, tagged
        coming_in = ahead(here_in), aside(here_in)
        here_out, feature_table, unit_tables = after((here_out, feature_table, unit_tables))
        coming_out = ahead(here_out), aside(here_out)
        swapped_in = swap(here_in)
        for step in range(1, last):
            next_in, across_in, total = after((*coming_in, total))
            coming_in = ahead(next_in), aside(next_in)
            swapped_across = swap(across_in)
            here_out, swapped_across = after((here_out, swapped_across))
            swapped_out = swap(here_out)
            saved = first_side([here_in, *swapped_in, across_in, *swapped_across])
            next_out, across_out, saved = after((*coming_out, saved))
            by_inner = aside(next_out) if step < last - 1 else ahead(across_out)
            coming_out = ahead(next_out), by_inner
            rows_out = [here_out, *swapped_out, across_out, *swap(across_out)]
            if step == last - 1:
                next_out, saved = after((next_out, saved))
                swapped_here, saved = after((swap(next_out), saved))
            total = other_side(rows_out, saved, total)
            here_in, total = after((next_in, total))
            here_out, swapped_in = next_out, swap(here_in)

        last_in, across_in, total = after((*coming_in, total))
        coming_in = aside(last_in)
        swapped_last, swapped_across = after((swap(last_in), swap(across_in)))
        saved = first_side([here_in, *swapped_in, last_in, *swapped_last])
        last_out, saved = after((coming_out[0], saved))
        coming_last = aside(last_out)
        rows_out = [here_out, *swapped_here, last_out, *swap(last_out)]
        total = other_side(rows_out, saved, total)
        corner_in = coming_in
        swapped_corner = swap(corner_in, 1)
        saved = first_side([across_in, *swapped_across, corner_in, *swapped_corner])
        across_out, corner_out, total, saved = after((coming_out[1], coming_last, total, saved))
        swapped_out = swap(across_out)
        rows_out = [across_out, *swapped_out, corner_out, *swap(corner_out)]
        total = other_side(rows_out, saved, total)
    else:
        gather = lambda piece: lax.all_gather(piece, "fsdp", axis=0, tiled=True)
        saved = forward([gather(inputs)], gate_rows, up_rows, feature_table, unit_tables)
        total = backward([gather(tagged)], down_weight, feature_table, unit_tables, saved, total)

    parts = total.astype(jnp.bfloat16).reshape(layout.count, -1, EX * K2)
    parts = lax.all_to_all(parts, "fsdp", 0, 0)
    part = jnp.sum(parts.astype(jnp.float32), axis=0)
    factor = (3.0 * SEQ * FF * D / (K1 * K2)) ** (-0.5)
    return (factor * part).reshape(-1, EX, K2).transpose(1, 0, 2)


def solution(mesh):
    layout = Layout(mesh.shape["fsdp"])
    in_specs = (
        P(("groups", "fsdp"), None),
        P(("groups", "fsdp"), None),
        P(("groups", "fsdp")),
        P(None, "fsdp"),
        P(None, "fsdp"),
        P("fsdp", None),
        P(None, "fsdp"),
        P(None, "fsdp"),
        P(),
        P(),
    )
    out_specs = P("groups", "fsdp", None)
    return jax.shard_map(
        lambda *args: on_device(layout, *args),
        mesh=mesh,
        in_specs=in_specs,
        out_specs=out_specs,
        check_vma=False,
    )
```

```python
import jax
import jax.numpy as jnp
from jax import lax
from jax.experimental import pallas as pl
from jax.experimental.pallas import tpu as pltpu
from jax.sharding import PartitionSpec as P

D = 5120
FF = 13824
EX = 2
SEQ = 512
K1 = 256
K2 = 256
CORES = 2
OUTER = 4
DEPTH = 2560
WIDE_ELEMENTS = 256 * 5120
LANES = 128
VMEM_LIMIT = 12 << 20


def sign_tables(buckets, sign_bits, order):
    matches = buckets[..., None, :] == order[:, None]
    signed = (2 * sign_bits - 1).astype(jnp.bfloat16)[..., None, :]
    return jnp.where(matches, signed, jnp.zeros_like(signed))


class Layout:
    def __init__(self, count):
        self.outer = OUTER if count % (OUTER * CORES) == 0 else 1
        self.inner = count // (self.outer * CORES)
        self.count = count

    def index(self, outer, inner, core):
        return ((outer % self.outer) * self.inner + inner % self.inner) * CORES + core

    def pairs(self, step):
        places = [
            (o, i, c)
            for o in range(self.outer)
            for i in range(self.inner)
            for c in range(CORES)
        ]
        return [(self.index(o, i, c), self.index(*step(o, i, c))) for o, i, c in places]

    def outer_ring(self):
        return self.pairs(lambda o, i, c: (o + 1 - 2 * c, i, c))

    def inner_ring(self):
        return self.pairs(lambda o, i, c: (o, i + 1 - 2 * c, c))

    def core_swap(self):
        return self.pairs(lambda o, i, c: (o, i, 1 - c))


def dot(left, right):
    return jnp.dot(left, right, preferred_element_type=jnp.float32)


def dot_rows(left, right):
    return lax.dot_general(
        left, right, (((1,), (1,)), ((), ())), preferred_element_type=jnp.float32
    )


def joined(refs, lanes):
    parts = [ref[:, lanes] for ref in refs]
    return jnp.concatenate(parts, axis=0) if len(parts) > 1 else parts[0]


def add_products(refs, model, sums, depth):
    for acc, _ in sums:
        acc[...] = jnp.zeros_like(acc)

    def body(step, _):
        here = pl.ds(pl.multiple_of(step * depth, depth), depth)
        rows = joined(refs, here)
        for acc, weight in sums:
            acc[...] += dot_rows(rows, weight[:, here])
        return 0

    lax.fori_loop(0, model // depth, body, 0)


def forward_kernel(pieces, *refs):
    gate_w, up_w, feature_w, tables = refs[pieces : pieces + 4]
    to_gate, to_up, down_part, feature_in = refs[pieces + 4 : pieces + 8]
    gate_acc, up_acc, feature_acc = refs[pieces + 8 :]
    sums = ((gate_acc, gate_w), (up_acc, up_w), (feature_acc, feature_w))
    add_products(refs[:pieces], gate_w.shape[1], sums, min(DEPTH, gate_w.shape[1]))
    gate, up = gate_acc[...], up_acc[...]
    sigmoid = jax.nn.sigmoid(gate)
    activated = gate * sigmoid
    to_gate[...] = up * sigmoid * (1.0 + gate * (1.0 - sigmoid))
    to_up[...] = activated
    hidden = (activated * up).astype(jnp.bfloat16)
    down_part[...] = dot_rows(hidden, tables[2]).astype(jnp.bfloat16)
    feature_in[...] = feature_acc[...].astype(jnp.bfloat16)


def backward_kernel(pieces, *refs):
    down_w, feature_w, tables, to_gate, to_up, down_part, feature_in, before = refs[
        pieces : pieces + 8
    ]
    total, hidden_acc, feature_acc = refs[pieces + 8 :]
    model = down_w.shape[1]
    wide = hidden_acc.shape[0] * model <= WIDE_ELEMENTS
    sums = ((hidden_acc, down_w), (feature_acc, feature_w))
    add_products(refs[:pieces], model, sums, model if wide else min(DEPTH, model))
    bf16 = jnp.bfloat16
    hidden_grad = hidden_acc[...]
    gate_grad = (hidden_grad * to_gate[...]).astype(bf16)
    up_grad = (hidden_grad * to_up[...]).astype(bf16)
    input_part = (dot_rows(gate_grad, tables[0]) + dot_rows(up_grad, tables[1])).astype(bf16)
    example = joined(refs[:pieces], pl.ds(model, LANES)).astype(jnp.float32)
    example = jnp.concatenate([example] * (K2 // LANES), axis=1)

    def by_example(features):
        features = features.astype(jnp.float32)
        return jnp.concatenate(
            [jnp.where(example == e, features, 0.0) for e in range(EX)], axis=1
        ).astype(bf16)

    feature_out = feature_acc[...].astype(bf16)
    total[...] = before[...] + lax.dot_general(
        jnp.concatenate([down_part[...], input_part], axis=0),
        jnp.concatenate([by_example(feature_out), by_example(feature_in[...])], axis=0),
        (((0,), (0,)), ((), ())),
        preferred_element_type=jnp.float32,
    )


def on_chip(kernel, name, pieces, operands, outs, sums):
    rows = sum(piece.shape[0] for piece in pieces)
    vmem = pl.BlockSpec(memory_space=pltpu.VMEM)
    return pl.pallas_call(
        lambda *refs: kernel(len(pieces), *refs),
        in_specs=[vmem] * (len(pieces) + len(operands)),
        out_specs=[vmem] * len(outs),
        out_shape=outs,
        scratch_shapes=[pltpu.VMEM((rows, columns), jnp.float32) for columns in sums],
        compiler_params=pltpu.CompilerParams(vmem_limit_bytes=VMEM_LIMIT),
        cost_estimate=pl.CostEstimate(flops=0, bytes_accessed=0, transcendentals=0),
        name=name,
    )(*pieces, *operands)


def forward(pieces, gate_rows, up_rows, feature_table, tables):
    units, model = gate_rows.shape
    rows = sum(piece.shape[0] for piece in pieces)
    outs = [
        jax.ShapeDtypeStruct((rows, units), jnp.float32),
        jax.ShapeDtypeStruct((rows, units), jnp.float32),
        jax.ShapeDtypeStruct((rows, K1), jnp.bfloat16),
        jax.ShapeDtypeStruct((rows, K2), jnp.bfloat16),
    ]
    operands = (gate_rows, up_rows, feature_table, tables)
    return on_chip(forward_kernel, "forward", pieces, operands, outs, (units, units, K2))


def backward(pieces, down_rows, feature_table, tables, saved, before):
    units, model = down_rows.shape
    outs = [jax.ShapeDtypeStruct(before.shape, jnp.float32)]
    operands = (down_rows, feature_table, tables, *saved, before)
    return on_chip(backward_kernel, "backward", pieces, operands, outs, (units, K2))[0]


def on_device(
    layout,
    inputs,
    out_grad,
    example_ids,
    gate_weight,
    up_weight,
    down_weight,
    unit_buckets,
    unit_signs,
    feature_buckets,
    feature_signs,
):
    def move(value, pairs):
        return lax.ppermute(value, "fsdp", pairs)

    rows = inputs.shape[0]

    own_rows = K1 // layout.count
    order = jnp.arange(K1, dtype=jnp.int32).reshape(-1, CORES, own_rows).swapaxes(0, 1)
    order = jnp.where(lax.axis_index("fsdp") % CORES == 0, order, order[::-1]).reshape(-1)
    unit_tables = sign_tables(unit_buckets, unit_signs, order)
    feature_table = sign_tables(feature_buckets, feature_signs, jnp.arange(K2, dtype=jnp.int32))

    example = jnp.broadcast_to(example_ids[:, None], (rows, LANES)).astype(jnp.bfloat16)
    tagged = jnp.concatenate([out_grad, example], axis=1)
    gate_rows, up_rows = gate_weight.T, up_weight.T
    total = jnp.zeros((K1, EX * K2), jnp.float32)

    if layout.inner == 2 and layout.outer > 2:
        ahead = lambda piece: move(piece, layout.outer_ring())
        aside = lambda piece: move(piece, layout.inner_ring())
        swap = lambda piece, parts=2: [
            move(part, layout.core_swap()) for part in jnp.split(piece, parts, axis=0)
        ]
        after = lax.optimization_barrier
        first_side = lambda rows_in: forward(
            rows_in, gate_rows, up_rows, feature_table, unit_tables
        )
        other_side = lambda rows_out, saved, total: backward(
            rows_out, down_weight, feature_table, unit_tables, saved, total
        )
        last = layout.outer - 1
        here_in, here_out = inputs, tagged
        coming_in = ahead(here_in), aside(here_in)
        here_out, feature_table, unit_tables = after((here_out, feature_table, unit_tables))
        coming_out = ahead(here_out), aside(here_out)
        swapped_in = swap(here_in)
        for step in range(1, last):
            next_in, across_in, total = after((*coming_in, total))
            coming_in = ahead(next_in), aside(next_in)
            swapped_across = swap(across_in)
            here_out, swapped_across = after((here_out, swapped_across))
            swapped_out = swap(here_out)
            saved = first_side([here_in, *swapped_in, across_in, *swapped_across])
            next_out, across_out, saved = after((*coming_out, saved))
            by_inner = aside(next_out) if step < last - 1 else ahead(across_out)
            coming_out = ahead(next_out), by_inner
            rows_out = [here_out, *swapped_out, across_out, *swap(across_out)]
            if step == last - 1:
                next_out, saved = after((next_out, saved))
                swapped_here, saved = after((swap(next_out), saved))
            total = other_side(rows_out, saved, total)
            here_in, total = after((next_in, total))
            here_out, swapped_in = next_out, swap(here_in)

        last_in, across_in, total = after((*coming_in, total))
        coming_in = aside(last_in)
        swapped_last, swapped_across = after((swap(last_in), swap(across_in)))
        saved = first_side([here_in, *swapped_in, last_in, *swapped_last])
        last_out, saved = after((coming_out[0], saved))
        coming_last = aside(last_out)
        rows_out = [here_out, *swapped_here, last_out, *swap(last_out)]
        total = other_side(rows_out, saved, total)
        corner_in = coming_in
        swapped_corner = swap(corner_in, 1)
        saved = first_side([across_in, *swapped_across, corner_in, *swapped_corner])
        across_out, corner_out, total, saved = after((coming_out[1], coming_last, total, saved))
        swapped_out = swap(across_out)
        rows_out = [across_out, *swapped_out, corner_out, *swap(corner_out)]
        total = other_side(rows_out, saved, total)
    else:
        gather = lambda piece: lax.all_gather(piece, "fsdp", axis=0, tiled=True)
        saved = forward([gather(inputs)], gate_rows, up_rows, feature_table, unit_tables)
        total = backward([gather(tagged)], down_weight, feature_table, unit_tables, saved, total)

    half = K1 // CORES
    part = total[:half] + move(total[half:].astype(jnp.bfloat16), layout.core_swap())
    parts = part.astype(jnp.bfloat16).reshape(-1, own_rows, EX * K2)
    chips = [list(range(core, layout.count, CORES)) for core in range(CORES)]
    parts = lax.all_to_all(parts, "fsdp", 0, 0, axis_index_groups=chips)
    part = jnp.sum(parts.astype(jnp.float32), axis=0)
    factor = (3.0 * SEQ * FF * D / (K1 * K2)) ** (-0.5)
    return (factor * part).reshape(-1, EX, K2).transpose(1, 0, 2)


def solution(mesh):
    layout = Layout(mesh.shape["fsdp"])
    in_specs = (
        P(("groups", "fsdp"), None),
        P(("groups", "fsdp"), None),
        P(("groups", "fsdp")),
        P(None, "fsdp"),
        P(None, "fsdp"),
        P("fsdp", None),
        P(None, "fsdp"),
        P(None, "fsdp"),
        P(),
        P(),
    )
    out_specs = P("groups", "fsdp", None)
    return jax.shard_map(
        lambda *args: on_device(layout, *args),
        mesh=mesh,
        in_specs=in_specs,
        out_specs=out_specs,
        check_vma=False,
    )
```

```python
import functools

import jax
import jax.numpy as jnp
from jax import lax
from jax.experimental import pallas as pl
from jax.experimental.pallas import tpu as pltpu
from jax.sharding import PartitionSpec as P

D = 5120
FF = 13824
EX = 2
SEQ = 512
K1 = 256
K2 = 256
CORES = 2
OUTER = 4
DEPTH = 2560
WIDE_ELEMENTS = 256 * 5120
LANES = 128
VMEM_LIMIT = 12 << 20


def sign_tables(buckets, sign_bits, order):
    matches = buckets[..., None, :] == order[:, None]
    signed = (2 * sign_bits - 1).astype(jnp.bfloat16)[..., None, :]
    return jnp.where(matches, signed, jnp.zeros_like(signed))


class Layout:
    def __init__(self, count):
        self.outer = OUTER if count % (OUTER * CORES) == 0 else 1
        self.inner = count // (self.outer * CORES)
        self.count = count

    def index(self, outer, inner, core):
        return ((outer % self.outer) * self.inner + inner % self.inner) * CORES + core

    def pairs(self, step):
        places = [
            (o, i, c)
            for o in range(self.outer)
            for i in range(self.inner)
            for c in range(CORES)
        ]
        return [(self.index(o, i, c), self.index(*step(o, i, c))) for o, i, c in places]

    def outer_ring(self):
        return self.pairs(lambda o, i, c: (o + 1 - 2 * c, i, c))

    def inner_ring(self):
        return self.pairs(lambda o, i, c: (o, i + 1 - 2 * c, c))

    def core_swap(self):
        return self.pairs(lambda o, i, c: (o, i, 1 - c))


def dot(left, right):
    return jnp.dot(left, right, preferred_element_type=jnp.float32)


def dot_rows(left, right):
    return lax.dot_general(
        left, right, (((1,), (1,)), ((), ())), preferred_element_type=jnp.float32
    )


def joined(refs, lanes):
    parts = [ref[:, lanes] for ref in refs]
    return jnp.concatenate(parts, axis=0) if len(parts) > 1 else parts[0]


def add_products(refs, model, sums, depth):
    for acc, _ in sums:
        acc[...] = jnp.zeros_like(acc)

    def body(step, _):
        here = pl.ds(pl.multiple_of(step * depth, depth), depth)
        rows = joined(refs, here)
        for acc, weight in sums:
            acc[...] += dot_rows(rows, weight[:, here])
        return 0

    lax.fori_loop(0, model // depth, body, 0)


def forward_kernel(depth, pieces, *refs):
    gate_w, up_w, feature_w, tables = refs[pieces : pieces + 4]
    to_gate, to_up, down_part, feature_in = refs[pieces + 4 : pieces + 8]
    gate_acc, up_acc, feature_acc = refs[pieces + 8 :]
    sums = ((gate_acc, gate_w), (up_acc, up_w), (feature_acc, feature_w))
    add_products(refs[:pieces], gate_w.shape[1], sums, depth)
    gate, up = gate_acc[...], up_acc[...]
    sigmoid = jax.nn.sigmoid(gate)
    activated = gate * sigmoid
    to_gate[...] = up * sigmoid * (1.0 + gate * (1.0 - sigmoid))
    to_up[...] = activated
    hidden = (activated * up).astype(jnp.bfloat16)
    down_part[...] = dot_rows(hidden, tables[2]).astype(jnp.bfloat16)
    feature_in[...] = feature_acc[...].astype(jnp.bfloat16)


def backward_kernel(pieces, *refs):
    down_w, feature_w, tables, to_gate, to_up, down_part, feature_in, before = refs[
        pieces : pieces + 8
    ]
    total, hidden_acc, feature_acc = refs[pieces + 8 :]
    model = down_w.shape[1]
    wide = hidden_acc.shape[0] * model <= WIDE_ELEMENTS
    sums = ((hidden_acc, down_w), (feature_acc, feature_w))
    add_products(refs[:pieces], model, sums, model if wide else min(DEPTH, model))
    bf16 = jnp.bfloat16
    hidden_grad = hidden_acc[...]
    gate_grad = (hidden_grad * to_gate[...]).astype(bf16)
    up_grad = (hidden_grad * to_up[...]).astype(bf16)
    input_part = (dot_rows(gate_grad, tables[0]) + dot_rows(up_grad, tables[1])).astype(bf16)
    example = joined(refs[:pieces], pl.ds(model, LANES)).astype(jnp.float32)
    example = jnp.concatenate([example] * (K2 // LANES), axis=1)

    def by_example(features):
        features = features.astype(jnp.float32)
        return jnp.concatenate(
            [jnp.where(example == e, features, 0.0) for e in range(EX)], axis=1
        ).astype(bf16)

    feature_out = feature_acc[...].astype(bf16)
    total[...] = before[...] + lax.dot_general(
        jnp.concatenate([down_part[...], input_part], axis=0),
        jnp.concatenate([by_example(feature_out), by_example(feature_in[...])], axis=0),
        (((0,), (0,)), ((), ())),
        preferred_element_type=jnp.float32,
    )


def on_chip(kernel, name, pieces, operands, outs, sums):
    rows = sum(piece.shape[0] for piece in pieces)
    vmem = pl.BlockSpec(memory_space=pltpu.VMEM)
    return pl.pallas_call(
        lambda *refs: kernel(len(pieces), *refs),
        in_specs=[vmem] * (len(pieces) + len(operands)),
        out_specs=[vmem] * len(outs),
        out_shape=outs,
        scratch_shapes=[pltpu.VMEM((rows, columns), jnp.float32) for columns in sums],
        compiler_params=pltpu.CompilerParams(vmem_limit_bytes=VMEM_LIMIT),
        cost_estimate=pl.CostEstimate(flops=0, bytes_accessed=0, transcendentals=0),
        name=name,
    )(*pieces, *operands)


def forward(pieces, gate_rows, up_rows, feature_table, tables, depth=DEPTH):
    units, model = gate_rows.shape
    kernel = functools.partial(forward_kernel, min(depth, model))
    rows = sum(piece.shape[0] for piece in pieces)
    outs = [
        jax.ShapeDtypeStruct((rows, units), jnp.float32),
        jax.ShapeDtypeStruct((rows, units), jnp.float32),
        jax.ShapeDtypeStruct((rows, K1), jnp.bfloat16),
        jax.ShapeDtypeStruct((rows, K2), jnp.bfloat16),
    ]
    operands = (gate_rows, up_rows, feature_table, tables)
    return on_chip(kernel, "forward", pieces, operands, outs, (units, units, K2))


def backward(pieces, down_rows, feature_table, tables, saved, before):
    units, model = down_rows.shape
    outs = [jax.ShapeDtypeStruct(before.shape, jnp.float32)]
    operands = (down_rows, feature_table, tables, *saved, before)
    return on_chip(backward_kernel, "backward", pieces, operands, outs, (units, K2))[0]


def on_device(
    layout,
    inputs,
    out_grad,
    example_ids,
    gate_weight,
    up_weight,
    down_weight,
    unit_buckets,
    unit_signs,
    feature_buckets,
    feature_signs,
):
    def move(value, pairs):
        return lax.ppermute(value, "fsdp", pairs)

    rows = inputs.shape[0]

    own_rows = K1 // layout.count
    order = jnp.arange(K1, dtype=jnp.int32).reshape(-1, CORES, own_rows).swapaxes(0, 1)
    order = jnp.where(lax.axis_index("fsdp") % CORES == 0, order, order[::-1]).reshape(-1)
    unit_tables = sign_tables(unit_buckets, unit_signs, order)
    feature_table = sign_tables(feature_buckets, feature_signs, jnp.arange(K2, dtype=jnp.int32))

    example = jnp.broadcast_to(example_ids[:, None], (rows, LANES)).astype(jnp.bfloat16)
    tagged = jnp.concatenate([out_grad, example], axis=1)
    gate_rows, up_rows = gate_weight.T, up_weight.T
    total = jnp.zeros((K1, EX * K2), jnp.float32)

    if layout.inner == 2 and layout.outer > 2:
        ahead = lambda piece: move(piece, layout.outer_ring())
        aside = lambda piece: move(piece, layout.inner_ring())
        swap = lambda piece, parts=2: [
            move(part, layout.core_swap()) for part in jnp.split(piece, parts, axis=0)
        ]
        after = lax.optimization_barrier
        first_side = lambda rows_in, *depth: forward(
            rows_in, gate_rows, up_rows, feature_table, unit_tables, *depth
        )
        other_side = lambda rows_out, saved, total: backward(
            rows_out, down_weight, feature_table, unit_tables, saved, total
        )
        last = layout.outer - 1
        here_in, here_out = inputs, tagged
        coming_in = ahead(here_in), aside(here_in)
        here_out, feature_table, unit_tables = after((here_out, feature_table, unit_tables))
        coming_out = ahead(here_out), aside(here_out)
        swapped_in = swap(here_in)
        for step in range(1, last):
            next_in, across_in, total = after((*coming_in, total))
            coming_in = ahead(next_in), aside(next_in)
            swapped_across = swap(across_in)
            here_out, swapped_across = after((here_out, swapped_across))
            swapped_out = swap(here_out)
            saved = first_side([here_in, *swapped_in, across_in, *swapped_across])
            next_out, across_out, saved = after((*coming_out, saved))
            by_inner = aside(next_out) if step < last - 1 else ahead(across_out)
            coming_out = ahead(next_out), by_inner
            rows_out = [here_out, *swapped_out, across_out, *swap(across_out)]
            if step == last - 1:
                next_out, saved = after((next_out, saved))
                swapped_here, saved = after((swap(next_out), saved))
            total = other_side(rows_out, saved, total)
            here_in, total = after((next_in, total))
            here_out, swapped_in = next_out, swap(here_in)

        last_in, across_in, total = after((*coming_in, total))
        coming_in = aside(last_in)
        swapped_last, swapped_across = after((swap(last_in), swap(across_in)))
        saved = first_side([here_in, *swapped_in, last_in, *swapped_last])
        last_out, saved = after((coming_out[0], saved))
        coming_last = aside(last_out)
        rows_out = [here_out, *swapped_here, last_out, *swap(last_out)]
        total = other_side(rows_out, saved, total)
        corner_in = coming_in
        swapped_corner = swap(corner_in, 1)
        rows_in = [across_in, *swapped_across, corner_in, *swapped_corner]
        saved = first_side(rows_in, inputs.shape[1])
        across_out, corner_out, total, saved = after((coming_out[1], coming_last, total, saved))
        swapped_out = swap(across_out)
        rows_out = [across_out, *swapped_out, corner_out, *swap(corner_out)]
        total = other_side(rows_out, saved, total)
    else:
        gather = lambda piece: lax.all_gather(piece, "fsdp", axis=0, tiled=True)
        saved = forward([gather(inputs)], gate_rows, up_rows, feature_table, unit_tables)
        total = backward([gather(tagged)], down_weight, feature_table, unit_tables, saved, total)

    half = K1 // CORES
    part = total[:half] + move(total[half:].astype(jnp.bfloat16), layout.core_swap())
    parts = part.astype(jnp.bfloat16).reshape(-1, own_rows, EX * K2)
    chips = [list(range(core, layout.count, CORES)) for core in range(CORES)]
    parts = lax.all_to_all(parts, "fsdp", 0, 0, axis_index_groups=chips)
    part = jnp.sum(parts.astype(jnp.float32), axis=0)
    factor = (3.0 * SEQ * FF * D / (K1 * K2)) ** (-0.5)
    return (factor * part).reshape(-1, EX, K2).transpose(1, 0, 2)


def solution(mesh):
    layout = Layout(mesh.shape["fsdp"])
    in_specs = (
        P(("groups", "fsdp"), None),
        P(("groups", "fsdp"), None),
        P(("groups", "fsdp")),
        P(None, "fsdp"),
        P(None, "fsdp"),
        P("fsdp", None),
        P(None, "fsdp"),
        P(None, "fsdp"),
        P(),
        P(),
    )
    out_specs = P("groups", "fsdp", None)
    return jax.shard_map(
        lambda *args: on_device(layout, *args),
        mesh=mesh,
        in_specs=in_specs,
        out_specs=out_specs,
        check_vma=False,
    )
```

```python
import functools

import jax
import jax.numpy as jnp
from jax import lax
from jax.experimental import pallas as pl
from jax.experimental.pallas import tpu as pltpu
from jax.sharding import PartitionSpec as P

D = 5120
FF = 13824
EX = 2
SEQ = 512
K1 = 256
K2 = 256
CORES = 2
OUTER = 4
DEPTH = 2560
LANES = 128
VMEM_LIMIT = 12 << 20


def sign_tables(buckets, sign_bits, order):
    matches = buckets[..., None, :] == order[:, None]
    signed = (2 * sign_bits - 1).astype(jnp.bfloat16)[..., None, :]
    return jnp.where(matches, signed, jnp.zeros_like(signed))


class Layout:
    def __init__(self, count):
        self.outer = OUTER if count % (OUTER * CORES) == 0 else 1
        self.inner = count // (self.outer * CORES)
        self.count = count

    def index(self, outer, inner, core):
        return ((outer % self.outer) * self.inner + inner % self.inner) * CORES + core

    def pairs(self, step):
        places = [
            (o, i, c)
            for o in range(self.outer)
            for i in range(self.inner)
            for c in range(CORES)
        ]
        return [(self.index(o, i, c), self.index(*step(o, i, c))) for o, i, c in places]

    def outer_ring(self):
        return self.pairs(lambda o, i, c: (o + 1 - 2 * c, i, c))

    def inner_ring(self):
        return self.pairs(lambda o, i, c: (o, i + 1 - 2 * c, c))

    def core_swap(self):
        return self.pairs(lambda o, i, c: (o, i, 1 - c))


def dot(left, right):
    return jnp.dot(left, right, preferred_element_type=jnp.float32)


def dot_rows(left, right):
    return lax.dot_general(
        left, right, (((1,), (1,)), ((), ())), preferred_element_type=jnp.float32
    )


def joined(refs, lanes):
    parts = [ref[:, lanes] for ref in refs]
    return jnp.concatenate(parts, axis=0) if len(parts) > 1 else parts[0]


def add_products(refs, model, sums, depth):
    for acc, _ in sums:
        acc[...] = jnp.zeros_like(acc)

    def body(step, _):
        here = pl.ds(pl.multiple_of(step * depth, depth), depth)
        rows = joined(refs, here)
        for acc, weight in sums:
            acc[...] += dot_rows(rows, weight[:, here])
        return 0

    lax.fori_loop(0, model // depth, body, 0)


def forward_kernel(depth, pieces, *refs):
    gate_w, up_w, feature_w, tables = refs[pieces : pieces + 4]
    to_gate, to_up, down_part, feature_in = refs[pieces + 4 : pieces + 8]
    gate_acc, up_acc, feature_acc = refs[pieces + 8 :]
    sums = ((gate_acc, gate_w), (up_acc, up_w), (feature_acc, feature_w))
    add_products(refs[:pieces], gate_w.shape[1], sums, depth)
    gate, up = gate_acc[...], up_acc[...]
    sigmoid = jax.nn.sigmoid(gate)
    activated = gate * sigmoid
    to_gate[...] = up * sigmoid * (1.0 + gate * (1.0 - sigmoid))
    to_up[...] = activated
    hidden = (activated * up).astype(jnp.bfloat16)
    down_part[...] = dot_rows(hidden, tables[2]).astype(jnp.bfloat16)
    feature_in[...] = feature_acc[...].astype(jnp.bfloat16)


def backward_kernel(depth, pieces, *refs):
    down_w, feature_w, tables, to_gate, to_up, down_part, feature_in, before = refs[
        pieces : pieces + 8
    ]
    total, hidden_acc, feature_acc = refs[pieces + 8 :]
    model = down_w.shape[1]
    add_products(refs[:pieces], model, ((hidden_acc, down_w), (feature_acc, feature_w)), depth)
    bf16 = jnp.bfloat16
    hidden_grad = hidden_acc[...]
    gate_grad = (hidden_grad * to_gate[...]).astype(bf16)
    up_grad = (hidden_grad * to_up[...]).astype(bf16)
    input_part = (dot_rows(gate_grad, tables[0]) + dot_rows(up_grad, tables[1])).astype(bf16)
    example = joined(refs[:pieces], pl.ds(model, LANES)).astype(jnp.float32)
    example = jnp.concatenate([example] * (K2 // LANES), axis=1)

    def by_example(features):
        features = features.astype(jnp.float32)
        return jnp.concatenate(
            [jnp.where(example == e, features, 0.0) for e in range(EX)], axis=1
        ).astype(bf16)

    feature_out = feature_acc[...].astype(bf16)
    total[...] = before[...] + lax.dot_general(
        jnp.concatenate([down_part[...], input_part], axis=0),
        jnp.concatenate([by_example(feature_out), by_example(feature_in[...])], axis=0),
        (((0,), (0,)), ((), ())),
        preferred_element_type=jnp.float32,
    )


def on_chip(kernel, name, pieces, operands, outs, sums):
    rows = sum(piece.shape[0] for piece in pieces)
    vmem = pl.BlockSpec(memory_space=pltpu.VMEM)
    return pl.pallas_call(
        lambda *refs: kernel(len(pieces), *refs),
        in_specs=[vmem] * (len(pieces) + len(operands)),
        out_specs=[vmem] * len(outs),
        out_shape=outs,
        scratch_shapes=[pltpu.VMEM((rows, columns), jnp.float32) for columns in sums],
        compiler_params=pltpu.CompilerParams(vmem_limit_bytes=VMEM_LIMIT),
        cost_estimate=pl.CostEstimate(flops=0, bytes_accessed=0, transcendentals=0),
        name=name,
    )(*pieces, *operands)


def forward(pieces, gate_rows, up_rows, feature_table, tables, depth=DEPTH):
    units, model = gate_rows.shape
    kernel = functools.partial(forward_kernel, min(depth, model))
    rows = sum(piece.shape[0] for piece in pieces)
    outs = [
        jax.ShapeDtypeStruct((rows, units), jnp.float32),
        jax.ShapeDtypeStruct((rows, units), jnp.float32),
        jax.ShapeDtypeStruct((rows, K1), jnp.bfloat16),
        jax.ShapeDtypeStruct((rows, K2), jnp.bfloat16),
    ]
    operands = (gate_rows, up_rows, feature_table, tables)
    return on_chip(kernel, "forward", pieces, operands, outs, (units, units, K2))


def backward(pieces, down_rows, feature_table, tables, saved, before, depth=DEPTH):
    units, model = down_rows.shape
    kernel = functools.partial(backward_kernel, min(depth, model))
    outs = [jax.ShapeDtypeStruct(before.shape, jnp.float32)]
    operands = (down_rows, feature_table, tables, *saved, before)
    return on_chip(kernel, "backward", pieces, operands, outs, (units, K2))[0]


def on_device(
    layout,
    inputs,
    out_grad,
    example_ids,
    gate_weight,
    up_weight,
    down_weight,
    unit_buckets,
    unit_signs,
    feature_buckets,
    feature_signs,
):
    def move(value, pairs):
        return lax.ppermute(value, "fsdp", pairs)

    rows = inputs.shape[0]

    own_rows = K1 // layout.count
    order = jnp.arange(K1, dtype=jnp.int32).reshape(-1, CORES, own_rows).swapaxes(0, 1)
    order = jnp.where(lax.axis_index("fsdp") % CORES == 0, order, order[::-1]).reshape(-1)
    unit_tables = sign_tables(unit_buckets, unit_signs, order)
    feature_table = sign_tables(feature_buckets, feature_signs, jnp.arange(K2, dtype=jnp.int32))

    example = jnp.broadcast_to(example_ids[:, None], (rows, LANES)).astype(jnp.bfloat16)
    tagged = jnp.concatenate([out_grad, example], axis=1)
    gate_rows, up_rows = gate_weight.T, up_weight.T
    total = jnp.zeros((K1, EX * K2), jnp.float32)

    if layout.inner == 2 and layout.outer > 2:
        ahead = lambda piece: move(piece, layout.outer_ring())
        aside = lambda piece: move(piece, layout.inner_ring())
        swap = lambda piece, parts=2: [
            move(part, layout.core_swap()) for part in jnp.split(piece, parts, axis=0)
        ]
        after = lax.optimization_barrier
        first_side = lambda rows_in, *depth: forward(
            rows_in, gate_rows, up_rows, feature_table, unit_tables, *depth
        )
        other_side = lambda rows_out, saved, total, *depth: backward(
            rows_out, down_weight, feature_table, unit_tables, saved, total, *depth
        )
        width = inputs.shape[1]
        last = layout.outer - 1
        here_in, here_out = inputs, tagged
        coming_in = ahead(here_in), aside(here_in)
        here_out, feature_table, unit_tables = after((here_out, feature_table, unit_tables))
        coming_out = ahead(here_out), aside(here_out)
        swapped_in = swap(here_in)
        for step in range(1, last):
            next_in, across_in, total = after((*coming_in, total))
            coming_in = ahead(next_in), aside(next_in)
            swapped_across = swap(across_in)
            here_out, swapped_across = after((here_out, swapped_across))
            swapped_out = swap(here_out)
            saved = first_side([here_in, *swapped_in, across_in, *swapped_across])
            next_out, across_out, saved = after((*coming_out, saved))
            by_inner = aside(next_out) if step < last - 1 else ahead(across_out)
            coming_out = ahead(next_out), by_inner
            rows_out = [here_out, *swapped_out, across_out, *swap(across_out)]
            if step == last - 1:
                next_out, saved = after((next_out, saved))
                swapped_here, saved = after((swap(next_out), saved))
            total = other_side(rows_out, saved, total)
            here_in, total = after((next_in, total))
            here_out, swapped_in = next_out, swap(here_in)

        last_in, across_in, total = after((*coming_in, total))
        coming_in = aside(last_in)
        swapped_last, swapped_across = after((swap(last_in), swap(across_in)))
        saved = first_side([here_in, *swapped_in, last_in, *swapped_last])
        last_out, saved = after((coming_out[0], saved))
        coming_last = aside(last_out)
        rows_out = [here_out, *swapped_here, last_out, *swap(last_out)]
        total = other_side(rows_out, saved, total, width)
        corner_in = coming_in
        swapped_corner = swap(corner_in, 1)
        rows_in = [across_in, *swapped_across, corner_in, *swapped_corner]
        saved = first_side(rows_in, width)
        across_out, corner_out, total, saved = after((coming_out[1], coming_last, total, saved))
        swapped_out = swap(across_out)
        rows_out = [across_out, *swapped_out, corner_out, *swap(corner_out)]
        total = other_side(rows_out, saved, total, width)
    else:
        gather = lambda piece: lax.all_gather(piece, "fsdp", axis=0, tiled=True)
        saved = forward([gather(inputs)], gate_rows, up_rows, feature_table, unit_tables)
        total = backward([gather(tagged)], down_weight, feature_table, unit_tables, saved, total)

    half = K1 // CORES
    part = total[:half] + move(total[half:].astype(jnp.bfloat16), layout.core_swap())
    parts = part.astype(jnp.bfloat16).reshape(-1, own_rows, EX * K2)
    chips = [list(range(core, layout.count, CORES)) for core in range(CORES)]
    parts = lax.all_to_all(parts, "fsdp", 0, 0, axis_index_groups=chips)
    part = jnp.sum(parts.astype(jnp.float32), axis=0)
    factor = (3.0 * SEQ * FF * D / (K1 * K2)) ** (-0.5)
    return (factor * part).reshape(-1, EX, K2).transpose(1, 0, 2)


def solution(mesh):
    layout = Layout(mesh.shape["fsdp"])
    in_specs = (
        P(("groups", "fsdp"), None),
        P(("groups", "fsdp"), None),
        P(("groups", "fsdp")),
        P(None, "fsdp"),
        P(None, "fsdp"),
        P("fsdp", None),
        P(None, "fsdp"),
        P(None, "fsdp"),
        P(),
        P(),
    )
    out_specs = P("groups", "fsdp", None)
    return jax.shard_map(
        lambda *args: on_device(layout, *args),
        mesh=mesh,
        in_specs=in_specs,
        out_specs=out_specs,
        check_vma=False,
    )
```

```python
import functools

import jax
import jax.numpy as jnp
from jax import lax
from jax.experimental import pallas as pl
from jax.experimental.pallas import tpu as pltpu
from jax.sharding import PartitionSpec as P

D = 5120
FF = 13824
EX = 2
SEQ = 512
K1 = 256
K2 = 256
CORES = 2
OUTER = 4
DEPTH = 2560
LANES = 128
VMEM_LIMIT = 12 << 20


def sign_tables(buckets, sign_bits, order):
    matches = buckets[..., None, :] == order[:, None]
    signed = (2 * sign_bits - 1).astype(jnp.bfloat16)[..., None, :]
    return jnp.where(matches, signed, jnp.zeros_like(signed))


class Layout:
    def __init__(self, count):
        self.outer = OUTER if count % (OUTER * CORES) == 0 else 1
        self.inner = count // (self.outer * CORES)
        self.count = count

    def index(self, outer, inner, core):
        return ((outer % self.outer) * self.inner + inner % self.inner) * CORES + core

    def pairs(self, step):
        places = [
            (o, i, c)
            for o in range(self.outer)
            for i in range(self.inner)
            for c in range(CORES)
        ]
        return [(self.index(o, i, c), self.index(*step(o, i, c))) for o, i, c in places]

    def outer_ring(self):
        return self.pairs(lambda o, i, c: (o + 1 - 2 * c, i, c))

    def inner_ring(self):
        return self.pairs(lambda o, i, c: (o, i + 1 - 2 * c, c))

    def core_swap(self):
        return self.pairs(lambda o, i, c: (o, i, 1 - c))


def dot(left, right):
    return jnp.dot(left, right, preferred_element_type=jnp.float32)


def dot_rows(left, right):
    return lax.dot_general(
        left, right, (((1,), (1,)), ((), ())), preferred_element_type=jnp.float32
    )


def joined(refs, lanes):
    parts = [ref[:, lanes] for ref in refs]
    return jnp.concatenate(parts, axis=0) if len(parts) > 1 else parts[0]


def add_products(refs, model, sums, depth):
    for acc, _ in sums:
        acc[...] = jnp.zeros_like(acc)

    def body(step, _):
        here = pl.ds(pl.multiple_of(step * depth, depth), depth)
        rows = joined(refs, here)
        for acc, weight in sums:
            acc[...] += dot_rows(rows, weight[:, here])
        return 0

    lax.fori_loop(0, model // depth, body, 0)


def forward_kernel(depth, pieces, *refs):
    gate_w, up_w, feature_w, tables = refs[pieces : pieces + 4]
    to_gate, to_up, down_part, feature_in = refs[pieces + 4 : pieces + 8]
    gate_acc, up_acc, feature_acc = refs[pieces + 8 :]
    sums = ((gate_acc, gate_w), (up_acc, up_w), (feature_acc, feature_w))
    add_products(refs[:pieces], gate_w.shape[1], sums, depth)
    gate, up = gate_acc[...], up_acc[...]
    sigmoid = jax.nn.sigmoid(gate)
    activated = gate * sigmoid
    to_gate[...] = up * sigmoid * (1.0 + gate * (1.0 - sigmoid))
    to_up[...] = activated
    hidden = (activated * up).astype(jnp.bfloat16)
    down_part[...] = dot_rows(hidden, tables[2]).astype(jnp.bfloat16)
    feature_in[...] = feature_acc[...].astype(jnp.bfloat16)


def backward_kernel(depth, pieces, *refs):
    down_w, feature_w, tables, to_gate, to_up, down_part, feature_in, before = refs[
        pieces : pieces + 8
    ]
    total, hidden_acc, feature_acc = refs[pieces + 8 :]
    model = down_w.shape[1]
    add_products(refs[:pieces], model, ((hidden_acc, down_w), (feature_acc, feature_w)), depth)
    bf16 = jnp.bfloat16
    hidden_grad = hidden_acc[...]
    gate_grad = (hidden_grad * to_gate[...]).astype(bf16)
    up_grad = (hidden_grad * to_up[...]).astype(bf16)
    input_part = (dot_rows(gate_grad, tables[0]) + dot_rows(up_grad, tables[1])).astype(bf16)
    example = joined(refs[:pieces], pl.ds(model, LANES)).astype(jnp.float32)
    example = jnp.concatenate([example] * (K2 // LANES), axis=1)

    def by_example(features):
        features = features.astype(jnp.float32)
        return jnp.concatenate(
            [jnp.where(example == e, features, 0.0) for e in range(EX)], axis=1
        ).astype(bf16)

    feature_out = feature_acc[...].astype(bf16)
    total[...] = before[...] + lax.dot_general(
        jnp.concatenate([down_part[...], input_part], axis=0),
        jnp.concatenate([by_example(feature_out), by_example(feature_in[...])], axis=0),
        (((0,), (0,)), ((), ())),
        preferred_element_type=jnp.float32,
    )


def on_chip(kernel, name, pieces, operands, outs, sums):
    rows = sum(piece.shape[0] for piece in pieces)
    vmem = pl.BlockSpec(memory_space=pltpu.VMEM)
    return pl.pallas_call(
        lambda *refs: kernel(len(pieces), *refs),
        in_specs=[vmem] * (len(pieces) + len(operands)),
        out_specs=[vmem] * len(outs),
        out_shape=outs,
        scratch_shapes=[pltpu.VMEM((rows, columns), jnp.float32) for columns in sums],
        compiler_params=pltpu.CompilerParams(vmem_limit_bytes=VMEM_LIMIT),
        cost_estimate=pl.CostEstimate(flops=0, bytes_accessed=0, transcendentals=0),
        name=name,
    )(*pieces, *operands)


def forward(pieces, gate_rows, up_rows, feature_table, tables, depth=DEPTH):
    units, model = gate_rows.shape
    kernel = functools.partial(forward_kernel, min(depth, model))
    rows = sum(piece.shape[0] for piece in pieces)
    outs = [
        jax.ShapeDtypeStruct((rows, units), jnp.float32),
        jax.ShapeDtypeStruct((rows, units), jnp.float32),
        jax.ShapeDtypeStruct((rows, K1), jnp.bfloat16),
        jax.ShapeDtypeStruct((rows, K2), jnp.bfloat16),
    ]
    operands = (gate_rows, up_rows, feature_table, tables)
    return on_chip(kernel, "forward", pieces, operands, outs, (units, units, K2))


def backward(pieces, down_rows, feature_table, tables, saved, before, depth=DEPTH):
    units, model = down_rows.shape
    kernel = functools.partial(backward_kernel, min(depth, model))
    outs = [jax.ShapeDtypeStruct(before.shape, jnp.float32)]
    operands = (down_rows, feature_table, tables, *saved, before)
    return on_chip(kernel, "backward", pieces, operands, outs, (units, K2))[0]


def on_device(
    layout,
    inputs,
    out_grad,
    example_ids,
    gate_weight,
    up_weight,
    down_weight,
    unit_buckets,
    unit_signs,
    feature_buckets,
    feature_signs,
):
    def move(value, pairs):
        return lax.ppermute(value, "fsdp", pairs)

    rows = inputs.shape[0]

    own_rows = K1 // layout.count
    order = jnp.arange(K1, dtype=jnp.int32).reshape(-1, CORES, own_rows).swapaxes(0, 1)
    order = jnp.where(lax.axis_index("fsdp") % CORES == 0, order, order[::-1]).reshape(-1)
    unit_tables = sign_tables(unit_buckets, unit_signs, order)
    feature_table = sign_tables(feature_buckets, feature_signs, jnp.arange(K2, dtype=jnp.int32))

    example = jnp.broadcast_to(example_ids[:, None], (rows, LANES)).astype(jnp.bfloat16)
    tagged = jnp.concatenate([out_grad, example], axis=1)
    gate_rows, up_rows = gate_weight.T, up_weight.T
    total = jnp.zeros((K1, EX * K2), jnp.float32)

    if layout.inner == 2 and layout.outer > 2:
        ahead = lambda piece: move(piece, layout.outer_ring())
        aside = lambda piece: move(piece, layout.inner_ring())
        swap = lambda piece, parts=2: [
            move(part, layout.core_swap()) for part in jnp.split(piece, parts, axis=0)
        ]
        after = lax.optimization_barrier
        first_side = lambda rows_in, *depth: forward(
            rows_in, gate_rows, up_rows, feature_table, unit_tables, *depth
        )
        other_side = lambda rows_out, saved, total, *depth: backward(
            rows_out, down_weight, feature_table, unit_tables, saved, total, *depth
        )
        width = inputs.shape[1]
        last = layout.outer - 1
        here_in, here_out = inputs, tagged
        coming_in = ahead(here_in), aside(here_in)
        here_out, feature_table, unit_tables = after((here_out, feature_table, unit_tables))
        coming_out = ahead(here_out), aside(here_out)
        swapped_in = swap(here_in)
        for step in range(1, last):
            next_in, across_in, total = after((*coming_in, total))
            coming_in = ahead(next_in), aside(next_in)
            swapped_across = swap(across_in)
            here_out, swapped_across = after((here_out, swapped_across))
            swapped_out = swap(here_out)
            saved = first_side([here_in, *swapped_in, across_in, *swapped_across])
            next_out, across_out, saved = after((*coming_out, saved))
            by_inner = aside(next_out) if step < last - 1 else ahead(across_out)
            coming_out = ahead(next_out), by_inner
            rows_out = [here_out, *swapped_out, across_out, *swap(across_out)]
            if step == last - 1:
                next_out, saved = after((next_out, saved))
                swapped_here, saved = after((swap(next_out), saved))
            total = other_side(rows_out, saved, total)
            here_in, total = after((next_in, total))
            here_out, swapped_in = next_out, swap(here_in)

        last_in, across_in, total = after((*coming_in, total))
        coming_in = aside(last_in)
        swapped_last, swapped_across = after((swap(last_in), swap(across_in)))
        saved = first_side([here_in, *swapped_in, last_in, *swapped_last])
        last_out, saved = after((coming_out[0], saved))
        coming_last = aside(last_out)
        rows_out = [here_out, *swapped_here, last_out, *swap(last_out)]
        total = other_side(rows_out, saved, total, width)
        corner_in = coming_in
        swapped_corner = swap(corner_in, 1)
        rows_in = [across_in, *swapped_across, corner_in, *swapped_corner]
        saved = first_side(rows_in, width)
        across_out, corner_out, total, saved = after((coming_out[1], coming_last, total, saved))
        swapped_out = swap(across_out, 1)
        rows_out = [across_out, *swapped_out, corner_out, *swap(corner_out, 1)]
        total = other_side(rows_out, saved, total, width)
    else:
        gather = lambda piece: lax.all_gather(piece, "fsdp", axis=0, tiled=True)
        saved = forward([gather(inputs)], gate_rows, up_rows, feature_table, unit_tables)
        total = backward([gather(tagged)], down_weight, feature_table, unit_tables, saved, total)

    half = K1 // CORES
    part = total[:half] + move(total[half:].astype(jnp.bfloat16), layout.core_swap())
    parts = part.astype(jnp.bfloat16).reshape(-1, own_rows, EX * K2)
    chips = [list(range(core, layout.count, CORES)) for core in range(CORES)]
    parts = lax.all_to_all(parts, "fsdp", 0, 0, axis_index_groups=chips)
    part = jnp.sum(parts.astype(jnp.float32), axis=0)
    factor = (3.0 * SEQ * FF * D / (K1 * K2)) ** (-0.5)
    return (factor * part).reshape(-1, EX, K2).transpose(1, 0, 2)


def solution(mesh):
    layout = Layout(mesh.shape["fsdp"])
    in_specs = (
        P(("groups", "fsdp"), None),
        P(("groups", "fsdp"), None),
        P(("groups", "fsdp")),
        P(None, "fsdp"),
        P(None, "fsdp"),
        P("fsdp", None),
        P(None, "fsdp"),
        P(None, "fsdp"),
        P(),
        P(),
    )
    out_specs = P("groups", "fsdp", None)
    return jax.shard_map(
        lambda *args: on_device(layout, *args),
        mesh=mesh,
        in_specs=in_specs,
        out_specs=out_specs,
        check_vma=False,
    )
```
